32 devices in a mesh: img: 8 (over y, x, core), tok: 4 (over z).
Axes of the slice: x: 2, y: 2, z: 4, core: 2. Of those that a mesh axis runs over, the one named last changes fastest.
Arguments:
- tokens: bfloat16 [8, 4096, 1280], P('img', 'tok'), may hold values from -8 to 8
- ln_gain: float32 [1280], replicated, may hold values from 0.25 to 1.75
- w_qkv: bfloat16 [1280, 1920], replicated, may hold values from -2 to 2
- w_proj: bfloat16 [640, 1280], replicated, may hold values from -0.25 to 0.25
- w_neck1: bfloat16 [1280, 256], replicated, may hold values from -0.15625 to 0.15625
- neck_gain1: float32 [256], replicated, may hold values from 0.25 to 1.75
- w_neck2: bfloat16 [2304, 256], replicated, may hold values from -0.125 to 0.125
- neck_gain2: float32 [256], replicated, may hold values from 0.25 to 1.75
- pe_matrix: float32 [2, 128], replicated, may hold values from -6 to 6
- query_bias: float32 [256], replicated, may hold values from -6 to 6
- dec_qkv: float32 [3, 256, 128], replicated, may hold values from -2 to 2
- dec_out: float32 [128, 256], replicated, may hold values from -0.5 to 0.5
- dec_gains: float32 [2, 256], replicated, may hold values from 0.25 to 1.75
- w_mlp1: float32 [256, 2048], replicated, may hold values from -0.375 to 0.375
- w_mlp2: float32 [2048, 256], replicated, may hold values from -0.1875 to 0.1875
- w_hyper: float32 [2, 256, 256], replicated, may hold values from -0.5 to 0.5
- w_hyper_out: float32 [256, 32], replicated, may hold values from -0.5 to 0.5
- w_up1: float32 [256, 256], replicated, may hold values from -0.375 to 0.375
- up_gain: float32 [64], replicated, may hold values from 0.25 to 1.75
- w_up2: float32 [64, 128], replicated, may hold values from -0.75 to 0.75
- req_image: int32 [128, 1], P('img'), may hold values from 0 to 7; in each aligned block of 16 rows (0 to 15, 16 to 31, ...) at most 4 rows name the same one
- points: int32 [128, 2], P('img'), may hold values from 0 to 1023
Outputs:
- masks: float32 [128, 65536], P('img', 'tok')
The draws below stay inside these ranges and needn't reach their ends.
Inputs may be any that keep to these rules, and one draw needn't show every extreme that they name: `req_image`: among the 16 rows of one owner no image is named more than 4 times; in some owner's rows an image is named exactly 4 times.
All inputs are finite; a program needn't handle non-finite values.
Results may differ from the reference program's by a relative error of at most 0.035.
Values may be sent and summed in bfloat16 or wider, within the bound.
No kernel may reach another device: no remote copies, remote signals or barrier semaphores. Data moves between devices by JAX's collectives and lax.ppermute only.
A program may use at most 320 MiB of HBM per device.

```python
import math
import jax
import jax.numpy as jnp
import numpy as np
from jax import lax

WIDTH = 1280
HEADS = 8
HDIM = 80
GRID = 64
NECK = 256
ATTN_DIM = 128
DEC_HEADS = 8
MLP_DIM = 2048
UP1 = 64
UP2 = 32
IMG_SIDE = 1024
TOKENS = 4096
N_IMAGES = 8
SLOTS = 16
CAP = 4
N_IMG = 8


def draw_tokens(key, part):
    drawn_draw = jax.random.normal(jax.random.fold_in(key, 17), (N_IMAGES, TOKENS, WIDTH), jnp.float32)
    return jnp.clip(drawn_draw, -6.0, 6.0).astype(jnp.bfloat16)


def draw_w_qkv(key, part):
    spread = (WIDTH // 4) ** (-0.5)
    drawn_draw = jnp.clip(jax.random.normal(jax.random.fold_in(key, 21), (WIDTH, 3 * HEADS * HDIM), jnp.float32), -5.0, 5.0) * spread
    return jnp.clip(drawn_draw, -2.0, 2.0).astype(jnp.bfloat16)


def draw_query_bias(key, part):
    drawn_draw = jnp.clip(jax.random.normal(jax.random.fold_in(key, 31), (NECK,), jnp.float32), -6.0, 6.0)
    return jnp.clip(drawn_draw, -6.0, 6.0)


def draw_dec_qkv(key, part):
    spread = (NECK // 4) ** (-0.5)
    drawn_draw = jnp.clip(jax.random.normal(jax.random.fold_in(key, 41), (3, NECK, ATTN_DIM), jnp.float32), -5.0, 5.0) * spread
    return jnp.clip(drawn_draw, -2.0, 2.0)


def set_ends(entries, own_key, low, largest):
    longest = entries.shape.index(max(entries.shape))
    spots = []
    for shift in (0, 1):
        where = [jax.random.randint(jax.random.fold_in(own_key, axis), (), 0, length) for axis, length in enumerate(entries.shape)]
        where[longest] = (where[longest] + shift) % entries.shape[longest]
        spots.append(tuple(where))
    return entries.at[spots[0]].set(low).at[spots[1]].set(largest)


def deal_out(key, own, number, rows, number_of, top, bound, slope):
    sequence = jax.random.permutation(key, number_of)
    crowded, usual = shares(number_of, rows * top, bound, slope, True), shares(number_of, rows * top, bound, slope, False)
    places = jnp.arange(number_of)

    def named(tallies, rotation):
        used = int((tallies > 0).sum())
        fixed = max(1, used // 4)
        shifted = fixed + (places - fixed + rotation * (used - fixed)) % max(1, number_of - fixed)
        return jnp.zeros((number_of,), jnp.int32).at[sequence[jnp.where(places < fixed, places, shifted)]].set(jnp.asarray(tallies, jnp.int32))

    tallies = jnp.where(number % 4 == 0, named(crowded, number // 4), named(usual, number - number // 4 - 1))
    mixed = jax.random.permutation(jax.random.fold_in(own, 3), number_of)
    source_of, taker = mixed[0:number_of // 2 * 2:2], mixed[1:number_of // 2 * 2:2]
    slack = jnp.minimum(tallies[source_of] - 1, bound - tallies[taker]) // 2
    slack = jnp.where((source_of == sequence[0]) | (taker == sequence[0]) | (tallies[taker] == 0), 0, jnp.maximum(slack, 0))
    shifted = jax.random.randint(jax.random.fold_in(own, 4), (number_of // 2,), 0, 1 << 20) % (slack + 1)
    tallies = tallies.at[source_of].add(-shifted).at[taker].add(shifted)
    members = jnp.searchsorted(jnp.cumsum(tallies), jnp.arange(rows * top), side="right").astype(jnp.int32)
    listing = members.reshape(top, rows).T
    listing = listing[jax.random.permutation(jax.random.fold_in(own, 1), rows)]
    rotation = jax.random.randint(jax.random.fold_in(own, 2), (rows, 1), 0, top)
    return jnp.take_along_axis(listing, (jnp.arange(top)[None, :] + rotation) % top, axis=1)


def shares(number_of, total, most, slope, full):
    loads = [(1 << 20) // math.isqrt(grade ** slope) + 1 for grade in range(1, number_of + 1)]
    largest = most if full else min(most, max(-(-total // number_of), total * loads[0] // sum(loads)))
    least = 1 if total - largest >= number_of - 1 else 0
    counts, surplus = [largest] + [least] * (number_of - 1), total - largest - least * (number_of - 1)
    while surplus > 0:
        movable = [i for i in range(1, number_of) if counts[i] < largest] or [i for i in range(1, number_of) if counts[i] < most]
        pool, left = sum([loads[i] for i in movable]), surplus
        for i in movable:
            extra = min(most - counts[i], max(1, left * loads[i] // pool), surplus)
            counts[i] = counts[i] + extra
            surplus = surplus - extra
    return np.array(counts)


def scatter_about(rng, dims, scale, reach, held_as=jnp.bfloat16):
    drawn = jax.random.normal(rng, dims, jnp.float32) * scale
    return jnp.minimum(jnp.maximum(drawn, -reach), reach).astype(held_as)


def setup_inputs(seed: int = 0) -> dict:
    arg_keys = jax.random.split(jax.random.key(seed), 23)
    tokens = draw_tokens(jax.random.fold_in(arg_keys[22], 71), 0)
    ln_gain = jnp.clip(1.0 + 0.15 * jax.random.normal(arg_keys[1], (WIDTH,), jnp.float32), 0.25, 1.75)
    w_qkv = draw_w_qkv(jax.random.fold_in(arg_keys[22], 71), 0)
    w_proj = scatter_about(arg_keys[3], (HEADS * HDIM, WIDTH), (HEADS * HDIM) ** -0.5, 0.25)
    w_neck1 = scatter_about(arg_keys[4], (WIDTH, NECK), WIDTH ** -0.5, 0.15625)
    neck_gain1 = jnp.clip(1.0 + 0.15 * jax.random.normal(arg_keys[5], (NECK,), jnp.float32), 0.25, 1.75)
    w_neck2 = scatter_about(arg_keys[6], (9 * NECK, NECK), (9 * NECK) ** -0.5, 0.125)
    neck_gain2 = jnp.clip(1.0 + 0.15 * jax.random.normal(arg_keys[7], (NECK,), jnp.float32), 0.25, 1.75)
    pe_matrix = scatter_about(arg_keys[8], (2, NECK // 2), 1.0, 6.0, jnp.float32)
    query_bias = draw_query_bias(jax.random.fold_in(arg_keys[22], 71), 0)
    dec_qkv = draw_dec_qkv(jax.random.fold_in(arg_keys[22], 71), 0)
    dec_out = scatter_about(arg_keys[11], (ATTN_DIM, NECK), ATTN_DIM ** -0.5, 0.5, jnp.float32)
    dec_gains = jnp.clip(1.0 + 0.15 * jax.random.normal(arg_keys[12], (2, NECK), jnp.float32), 0.25, 1.75)
    w_mlp1 = scatter_about(arg_keys[13], (NECK, MLP_DIM), NECK ** -0.5, 0.375, jnp.float32)
    w_mlp2 = scatter_about(arg_keys[14], (MLP_DIM, NECK), (MLP_DIM // 2) ** -0.5, 0.1875, jnp.float32)
    w_hyper = scatter_about(arg_keys[15], (2, NECK, NECK), (NECK // 2) ** -0.5, 0.5, jnp.float32)
    w_hyper_out = scatter_about(arg_keys[16], (NECK, UP2), (NECK // 2) ** -0.5, 0.5, jnp.float32)
    w_up1 = scatter_about(arg_keys[17], (NECK, 4 * UP1), NECK ** -0.5, 0.375, jnp.float32)
    up_gain = jnp.clip(1.0 + 0.15 * jax.random.normal(arg_keys[18], (UP1,), jnp.float32), 0.25, 1.75)
    w_up2 = scatter_about(arg_keys[19], (UP1, 4 * UP2), UP1 ** -0.5, 0.75, jnp.float32)
    req_image_keys = jax.random.split(jax.random.fold_in(arg_keys[20], 1), (N_IMAGES * SLOTS) // SLOTS)
    req_image_turns = jax.random.permutation(jax.random.fold_in(arg_keys[20], 3), (N_IMAGES * SLOTS) // SLOTS)
    req_image = jax.vmap(lambda own, number: deal_out(jax.random.fold_in(arg_keys[20], 2), own, number, SLOTS, N_IMG, 1, CAP, 2))(req_image_keys, req_image_turns).reshape((N_IMAGES * SLOTS, 1))
    points = set_ends(jax.random.randint(arg_keys[21], (N_IMAGES * SLOTS, 2), 0, IMG_SIDE), jax.random.fold_in(arg_keys[21], 1), 0, IMG_SIDE - 1).astype(jnp.int32)
    return {"tokens": tokens, "ln_gain": ln_gain, "w_qkv": w_qkv, "w_proj": w_proj, "w_neck1": w_neck1, "neck_gain1": neck_gain1, "w_neck2": w_neck2, "neck_gain2": neck_gain2, "pe_matrix": pe_matrix, "query_bias": query_bias, "dec_qkv": dec_qkv, "dec_out": dec_out, "dec_gains": dec_gains, "w_mlp1": w_mlp1, "w_mlp2": w_mlp2, "w_hyper": w_hyper, "w_hyper_out": w_hyper_out, "w_up1": w_up1, "up_gain": up_gain, "w_up2": w_up2, "req_image": req_image, "points": points}


highest_precision = lax.Precision.HIGHEST

def layer_norm(tensor, gain_vec, epsilon):
    average = lax.optimization_barrier(jnp.mean(tensor, axis=-1, keepdims=True))
    centred = tensor - average
    spread = lax.optimization_barrier(jnp.mean(centred * centred, axis=-1, keepdims=True))
    return centred * lax.rsqrt(spread + epsilon) * gain_vec

def fourier(coords, pe_matrix):
    angles = 2.0 * math.pi * jnp.dot(coords, pe_matrix, precision=highest_precision)
    return jnp.concatenate([jnp.sin(angles), jnp.cos(angles)], axis=-1)

def grid_codes(first_row, grid_rows, pe_matrix):
    row_ids = (first_row + jnp.arange(grid_rows, dtype=jnp.int32)).astype(jnp.float32)
    col_ids = jnp.arange(GRID, dtype=jnp.int32).astype(jnp.float32)
    ycoord = (row_ids + 0.5) / GRID * 2.0 - 1.0
    xcoord = (col_ids + 0.5) / GRID * 2.0 - 1.0
    coords = jnp.stack([jnp.broadcast_to(xcoord[None, :], (grid_rows, GRID)), jnp.broadcast_to(ycoord[:, None], (grid_rows, GRID))], axis=-1)
    return fourier(coords.reshape(grid_rows * GRID, 2), pe_matrix)

def attention_core(projected, heads):
    length = projected.shape[0]
    inner_width = heads * HDIM
    factor = 1.0 / math.sqrt(HDIM)
    block_rows = min(length, 1024)

    def one_head(head_no):
        offset = (head_no * HDIM).astype(jnp.int32)
        query_matrix = lax.dynamic_slice_in_dim(projected, offset, HDIM, 1)
        key_rows = lax.dynamic_slice_in_dim(projected, offset + inner_width, HDIM, 1)
        values = lax.dynamic_slice_in_dim(projected, offset + 2 * inner_width, HDIM, 1)
        pieces = []
        for first_query in range(0, length, block_rows):
            query_rows = query_matrix[first_query:first_query + block_rows]
            attention_scores = lax.dot_general(query_rows, key_rows, (((1,), (1,)), ((), ())), preferred_element_type=jnp.float32) * factor
            maxima = lax.optimization_barrier(jnp.max(attention_scores, axis=1, keepdims=True))
            attention_weights = jnp.exp(attention_scores - maxima)
            totals = lax.optimization_barrier(jnp.sum(attention_weights, axis=1, keepdims=True))
            mixed_values = jnp.dot(attention_weights.astype(jnp.bfloat16), values, preferred_element_type=jnp.float32)
            pieces.append(mixed_values / totals)
        return jnp.concatenate(pieces, axis=0).astype(jnp.bfloat16)
    stacked = lax.map(one_head, jnp.arange(heads, dtype=jnp.int32))
    return jnp.transpose(stacked, (1, 0, 2)).reshape(length, inner_width)

def upscale(embedding, grid_rows, w_up1, up_gain, w_up2):
    first_out = jnp.dot(embedding, w_up1, precision=highest_precision).reshape(grid_rows * GRID * 4, UP1)
    first_out = jax.nn.gelu(layer_norm(first_out, up_gain, 1e-06), approximate=False)
    second = jax.nn.gelu(jnp.dot(first_out, w_up2, precision=highest_precision), approximate=False)
    second = second.reshape(grid_rows, GRID, 2, 2, 2, 2, UP2)
    second = jnp.transpose(second, (6, 0, 2, 4, 1, 3, 5))
    return second.reshape(UP2, grid_rows * GRID * 16)

def token_side(query_tok, attended, dec_out, dec_gains, w_mlp1, w_mlp2, w_hyper, w_hyper_out):
    first_out = layer_norm(query_tok + jnp.dot(attended, dec_out, precision=highest_precision), dec_gains[0], 1e-05)
    hidden = jax.nn.relu(jnp.dot(first_out, w_mlp1, precision=highest_precision))
    second = layer_norm(first_out + jnp.dot(hidden, w_mlp2, precision=highest_precision), dec_gains[1], 1e-05)
    hyper_vec = jax.nn.relu(jnp.dot(second, w_hyper[0], precision=highest_precision))
    hyper_vec = jax.nn.relu(jnp.dot(hyper_vec, w_hyper[1], precision=highest_precision))
    return jnp.dot(hyper_vec, w_hyper_out, precision=highest_precision)

def reference(tokens, ln_gain, w_qkv, w_proj, w_neck1, neck_gain1, w_neck2, neck_gain2, pe_matrix, query_bias, dec_qkv, dec_out, dec_gains, w_mlp1, w_mlp2, w_hyper, w_hyper_out, w_up1, up_gain, w_up2, req_image, points):

    def encode_one(picture):
        normed = layer_norm(picture.astype(jnp.float32), ln_gain, 1e-06).astype(jnp.bfloat16)
        projected = jnp.dot(normed, w_qkv, preferred_element_type=jnp.float32).astype(jnp.bfloat16)
        attended = attention_core(projected, HEADS)
        block_out = (picture.astype(jnp.float32) + jnp.dot(attended, w_proj, preferred_element_type=jnp.float32)).astype(jnp.bfloat16)
        narrow = layer_norm(jnp.dot(block_out, w_neck1, preferred_element_type=jnp.float32), neck_gain1, 1e-06)
        narrow = narrow.astype(jnp.bfloat16).reshape(GRID, GRID, NECK)
        framed = jnp.pad(narrow, ((1, 1), (1, 1), (0, 0)))
        columns = jnp.concatenate([framed[row_off:row_off + GRID, col_off:col_off + GRID] for row_off in range(3) for col_off in range(3)], axis=-1)
        columns = columns.reshape(TOKENS, 9 * NECK)
        embedding = layer_norm(jnp.dot(columns, w_neck2, preferred_element_type=jnp.float32), neck_gain2, 1e-06)
        positional = grid_codes(0, GRID, pe_matrix)
        dec_keys = jnp.dot(embedding + positional, dec_qkv[1], precision=highest_precision)
        dec_values = jnp.dot(embedding, dec_qkv[2], precision=highest_precision)
        upscaled = upscale(embedding, GRID, w_up1, up_gain, w_up2)
        return (dec_keys, dec_values, upscaled)
    keys_all, values_all, upscaled_all = lax.map(encode_one, tokens)
    head_size = ATTN_DIM // DEC_HEADS
    decoder_scale = 1.0 / math.sqrt(head_size)

    def decode_one(request):
        picture_no = req_image[request, 0]
        located = points[request].astype(jnp.float32)
        query_tok = query_bias + fourier(((located + 0.5) / IMG_SIDE * 2.0 - 1.0)[None, :], pe_matrix)
        query_matrix = jnp.dot(query_tok, dec_qkv[0], precision=highest_precision).reshape(DEC_HEADS, head_size)
        key_projected = keys_all[picture_no].reshape(TOKENS, DEC_HEADS, head_size)
        value_projected = values_all[picture_no].reshape(TOKENS, DEC_HEADS, head_size)
        attention_scores = jnp.einsum('hd,khd->hk', query_matrix, key_projected, precision=highest_precision) * decoder_scale
        maxima = lax.optimization_barrier(jnp.max(attention_scores, axis=1, keepdims=True))
        attention_weights = jnp.exp(attention_scores - maxima)
        mixed_values = jnp.einsum('hk,khd->hd', attention_weights, value_projected, precision=highest_precision) / lax.optimization_barrier(jnp.sum(attention_weights, axis=1))[:, None]
        hyper_vec = token_side(query_tok, mixed_values.reshape(1, ATTN_DIM), dec_out, dec_gains, w_mlp1, w_mlp2, w_hyper, w_hyper_out)
        return jnp.dot(hyper_vec, upscaled_all[picture_no], precision=highest_precision)[0]
    return lax.map(decode_one, jnp.arange(N_IMG * SLOTS, dtype=jnp.int32))
```

```python
import functools
import math

import jax
import jax.numpy as jnp
import numpy as np
from jax import lax
from jax.experimental import pallas as pl
from jax.experimental.pallas import tpu as pltpu
from jax.sharding import PartitionSpec as P

HEADS = 8
HDIM = 80
GRID = 64
NECK = 256
ATTN_DIM = 128
DEC_HEADS = 8
UP1 = 64
UP2 = 32
IMG_SIDE = 1024
CAP = 4
LANES = 128
OFFSETS = 16
VMEM_BYTES = 56 << 20

highest_precision = lax.Precision.HIGHEST
TO_BASE2 = math.log2(math.e) / math.sqrt(HDIM)


def layer_norm(tensor, gain_vec, epsilon, axis=-1):
    average = jnp.mean(tensor, axis=axis, keepdims=True)
    centred = tensor - average
    spread = jnp.mean(centred * centred, axis=axis, keepdims=True)
    return centred * lax.rsqrt(spread + epsilon) * gain_vec


def gelu(tensor):
    return 0.5 * tensor * (1.0 + lax.erf(tensor * math.sqrt(0.5)))


def fourier(coords, pe_matrix):
    angles = 2.0 * math.pi * jnp.dot(coords, pe_matrix, precision=highest_precision)
    return jnp.concatenate([jnp.sin(angles), jnp.cos(angles)], axis=-1)


def grid_codes(first_row, grid_rows, pe_matrix):
    row_ids = (first_row + jnp.arange(grid_rows, dtype=jnp.int32)).astype(jnp.float32)
    col_ids = jnp.arange(GRID, dtype=jnp.int32).astype(jnp.float32)
    ycoord = (row_ids + 0.5) / GRID * 2.0 - 1.0
    xcoord = (col_ids + 0.5) / GRID * 2.0 - 1.0
    coords = jnp.stack(
        [
            jnp.broadcast_to(xcoord[None, :], (grid_rows, GRID)),
            jnp.broadcast_to(ycoord[:, None], (grid_rows, GRID)),
        ],
        axis=-1,
    )
    return fourier(coords.reshape(grid_rows * GRID, 2), pe_matrix)


def params(**extra):
    return pltpu.CompilerParams(vmem_limit_bytes=VMEM_BYTES, **extra)


def full_dot(left, right, dims=(((1,), (0,)), ((), ()))):
    return lax.dot_general(
        left, right, dims, precision=highest_precision, preferred_element_type=jnp.float32
    )


def head_span(span, ranks):
    first = span * ranks * HDIM
    start = first // LANES * LANES
    stop = -(-(first + ranks * HDIM) // LANES) * LANES
    return first, start, stop


def project_kernel(span, ranks, with_norm, me_ref, x_ref, gain_ref, w_ref, *refs):
    inner = HEADS * HDIM
    outs, normed_out = (refs[:ranks], refs[ranks]) if with_norm else (refs[:ranks], None)
    weights, rows_ref = refs[-2:]
    first, start, stop = head_span(span, ranks)
    width = stop - start

    @pl.when(pl.program_id(0) == 0)
    def _():
        for part in range(3):
            weights[part * width : (part + 1) * width, :] = w_ref[
                :, part * inner + start : part * inner + stop
            ].T

    if with_norm:
        normed = layer_norm(x_ref[...].astype(jnp.float32), gain_ref[...], 1e-06)
        normed = normed.astype(jnp.bfloat16)
        normed_out[...] = normed
    else:
        normed = x_ref[...]
    rows_ref[...] = lax.dot_general(
        weights[...], normed, (((1,), (1,)), ((), ())), preferred_element_type=jnp.float32
    ).astype(jnp.bfloat16)
    for shift, out in enumerate(outs):
        head = lax.rem(me_ref[0] + shift, ranks)
        for part in range(3):
            place = pl.multiple_of(head * HDIM + (part * width + first - start), 16)
            out[part * HDIM : (part + 1) * HDIM, :] = rows_ref[pl.ds(place, HDIM), :]


def project(span, ranks, me, source, ln_gain, w_qkv, with_norm):
    rows, model = source.shape
    block = min(rows, 256)
    _, start, stop = head_span(span, ranks)
    width = stop - start
    out_shape = [jax.ShapeDtypeStruct((3 * HDIM, rows), jnp.bfloat16)] * ranks
    out_specs = [pl.BlockSpec((3 * HDIM, block), lambda i: (0, i))] * ranks
    if with_norm:
        out_shape = out_shape + [jax.ShapeDtypeStruct((rows, model), jnp.bfloat16)]
        out_specs = out_specs + [pl.BlockSpec((block, model), lambda i: (i, 0))]
    return pl.pallas_call(
        functools.partial(project_kernel, span, ranks, with_norm),
        grid=(rows // block,),
        in_specs=[
            pl.BlockSpec(memory_space=pltpu.SMEM),
            pl.BlockSpec((block, model), lambda i: (i, 0)),
            pl.BlockSpec((1, model), lambda i: (0, 0)),
            pl.BlockSpec(w_qkv.shape, lambda i: (0, 0)),
        ],
        out_specs=out_specs,
        out_shape=out_shape,
        scratch_shapes=[
            pltpu.VMEM((3 * width, model), jnp.bfloat16),
            pltpu.VMEM((3 * width, block), jnp.bfloat16),
        ],
        compiler_params=params(),
        cost_estimate=pl.CostEstimate(
            flops=2 * rows * model * 3 * width, bytes_accessed=10 << 20, transcendentals=rows
        ),
        name="norm_and_projections" if with_norm else "projections",
    )(me, source, ln_gain, w_qkv)


def attention_kernel(spans, query_block, key_block, *refs):
    count = len(refs) // 2 - 2
    blocks, outs = refs[:count], refs[count : 2 * count]
    queries, keys, values, mixed_out = refs[2 * count :]
    rows = blocks[0].shape[1]
    total = count * rows
    per_block = queries.shape[0] // count
    for at, block in enumerate(blocks):
        keys[at * rows : (at + 1) * rows, :] = block[HDIM : 2 * HDIM, :].T
        values[:HDIM, at * rows : (at + 1) * rows] = block[2 * HDIM :, :]
        pieces = [block[:HDIM, first:stop] for first, stop in spans]
        joined = pieces[0] if len(pieces) == 1 else jnp.concatenate(pieces, axis=1)
        for step in range(per_block):
            queries[at * per_block + step] = joined[
                :, step * query_block : (step + 1) * query_block
            ]
    values[HDIM:, :] = jnp.ones((values.shape[0] - HDIM, total), jnp.bfloat16)
    steps = total // key_block

    def one_block(step, carry):
        query = queries[step]

        def scores_of(at):
            return lax.dot_general(
                keys[at * key_block : (at + 1) * key_block, :],
                query,
                (((1,), (0,)), ((), ())),
                preferred_element_type=jnp.float32,
            )

        maxima, mixed = None, None
        upcoming = scores_of(0)
        for at in range(steps):
            scores = upcoming
            if at + 1 < steps:
                upcoming = scores_of(at + 1)
            block_max = jnp.max(scores, axis=0, keepdims=True)
            new_max = block_max if maxima is None else jnp.maximum(maxima, block_max)
            weights = jnp.exp2((scores - new_max) * TO_BASE2).astype(jnp.bfloat16)
            share = jnp.dot(
                values[:, at * key_block : (at + 1) * key_block],
                weights,
                preferred_element_type=jnp.float32,
            )
            if maxima is None:
                mixed = share
            else:
                mixed = mixed * jnp.exp2((maxima - new_max) * TO_BASE2) + share
            maxima = new_max
        mixed_out[step] = (mixed[:HDIM, :] / mixed[HDIM : HDIM + 1, :]).astype(jnp.bfloat16)
        return carry

    lax.fori_loop(0, queries.shape[0], one_block, 0)
    for at, out in enumerate(outs):
        for step in range(per_block):
            out[:, step * query_block : (step + 1) * query_block] = mixed_out[at * per_block + step]


def attention(blocks, spans):
    count, rows = len(blocks), blocks[0].shape[1]
    wanted = sum(stop - first for first, stop in spans)
    query_block = min(wanted, 512)
    key_block = min(count * rows, 1024)
    tiles = count * wanted // query_block
    return pl.pallas_call(
        functools.partial(attention_kernel, spans, query_block, key_block),
        out_shape=[jax.ShapeDtypeStruct((HDIM, wanted), jnp.bfloat16)] * count,
        scratch_shapes=[
            pltpu.VMEM((tiles, HDIM, query_block), jnp.bfloat16),
            pltpu.VMEM((count * rows, HDIM), jnp.bfloat16),
            pltpu.VMEM((HDIM + 16, count * rows), jnp.bfloat16),
            pltpu.VMEM((tiles, HDIM, query_block), jnp.bfloat16),
        ],
        compiler_params=params(),
        cost_estimate=pl.CostEstimate(
            flops=12 * count * wanted * count * rows * HDIM,
            bytes_accessed=4 << 20,
            transcendentals=count * wanted * count * rows,
        ),
        name="head_attention",
    )(*blocks)


def neck_kernel(spans, ranks, me_ref, tok_ref, wp_ref, wn_ref, gain_ref, *refs):
    spans_count = HEADS // ranks
    heads = refs[: spans_count * ranks]
    out_ref, joined_ref = refs[-2:]
    wanted = out_ref.shape[0]

    def picked(ref, axis):
        if ref.shape[axis] == wanted:
            return ref[...]
        if axis == 0:
            pieces = [ref[first:stop, :] for first, stop in spans]
        else:
            pieces = [ref[:, first:stop] for first, stop in spans]
        return pieces[0] if len(pieces) == 1 else jnp.concatenate(pieces, axis=axis)

    for span in range(spans_count):
        for shift in range(ranks):
            head = lax.rem(me_ref[0] + shift, ranks) + span * ranks
            joined_ref[pl.ds(pl.multiple_of(head * HDIM, 16), HDIM), :] = picked(
                heads[span * ranks + shift], 1
            )
    attended = joined_ref[...].T
    block_out = picked(tok_ref, 0).astype(jnp.float32) + jnp.dot(
        attended, wp_ref[...], preferred_element_type=jnp.float32
    )
    narrow = jnp.dot(
        block_out.astype(jnp.bfloat16), wn_ref[...], preferred_element_type=jnp.float32
    )
    out_ref[...] = layer_norm(narrow, gain_ref[...], 1e-06).astype(jnp.bfloat16)


def neck(spans, ranks, me, tokens, w_proj, w_neck1, gain, heads):
    wanted = sum(stop - first for first, stop in spans)
    model = tokens.shape[1]
    vmem = pl.BlockSpec(memory_space=pltpu.VMEM)
    return pl.pallas_call(
        functools.partial(neck_kernel, spans, ranks),
        in_specs=[pl.BlockSpec(memory_space=pltpu.SMEM)] + [vmem] * (4 + len(heads)),
        out_specs=vmem,
        out_shape=jax.ShapeDtypeStruct((wanted, NECK), jnp.bfloat16),
        scratch_shapes=[pltpu.VMEM((HEADS * HDIM, wanted), jnp.bfloat16)],
        compiler_params=params(),
        cost_estimate=pl.CostEstimate(
            flops=2 * wanted * model * (HEADS * HDIM + NECK),
            bytes_accessed=6 << 20,
            transcendentals=wanted,
        ),
        name="proj_and_narrow",
    )(me, tokens, w_proj, w_neck1, gain, *heads)


def embed_kernel(
    prev_ref, next_ref, edge_ref, mid_ref, w_ref, gain_ref, kv_ref, code_ref, query_ref, *refs
):
    emb_ref, stats_ref, cells_ref = refs
    rows = emb_ref.shape[0]
    half = edge_ref.shape[0] // 2
    map_rows = jnp.concatenate(
        [prev_ref[...], edge_ref[:half, :], mid_ref[...], edge_ref[half:, :], next_ref[...]], axis=0
    )
    wide = map_rows.astype(jnp.float32)
    length = wide.shape[0]
    column = lax.rem(lax.broadcasted_iota(jnp.int32, (length, 1), 0), GRID)
    before = jnp.where(column == 0, 0.0, pltpu.roll(wide, 1, 0))
    after = jnp.where(column == GRID - 1, 0.0, pltpu.roll(wide, length - 1, 0))
    cells_ref[:, :NECK] = before.astype(jnp.bfloat16)
    cells_ref[:, NECK : 2 * NECK] = map_rows
    cells_ref[:, 2 * NECK :] = after.astype(jnp.bfloat16)
    total = None
    for row_off in range(3):
        share = jnp.dot(
            cells_ref[row_off * GRID : row_off * GRID + rows, :],
            w_ref[row_off * 3 * NECK : (row_off + 1) * 3 * NECK, :],
            preferred_element_type=jnp.float32,
        )
        total = share if total is None else total + share
    embedding = layer_norm(total, gain_ref[...], 1e-06)
    emb_ref[...] = embedding

    dec_keys = full_dot(embedding, kv_ref[1]) + code_ref[...]
    dec_values = full_dot(embedding, kv_ref[2])
    head_size = ATTN_DIM // DEC_HEADS
    scores = full_dot(query_ref[...], dec_keys, (((1,), (1,)), ((), ())))
    scores = scores * (1.0 / math.sqrt(head_size))
    maxima = jnp.max(scores, axis=1, keepdims=True)
    weights = jnp.exp(scores - maxima)
    totals = jnp.sum(weights, axis=1, keepdims=True)
    mixed = full_dot(weights, dec_values)
    number = stats_ref.shape[0] // 3
    lane_head = lax.broadcasted_iota(jnp.int32, (1, ATTN_DIM), 1) // head_size
    for at, stat in enumerate((mixed, maxima, totals)):
        picked = jnp.zeros((number, ATTN_DIM), jnp.float32)
        for head in range(DEC_HEADS):
            picked = jnp.where(
                lane_head == head, stat[head * number : (head + 1) * number, :], picked
            )
        stats_ref[at * number : (at + 1) * number, :] = picked


def embed(prev, following, edge, mid, w_neck2, gain, dec_qkv, code_keys, spread_queries):
    rows = edge.shape[0] + mid.shape[0]
    number = spread_queries.shape[0] // DEC_HEADS
    length = rows + prev.shape[0] + following.shape[0]
    return pl.pallas_call(
        embed_kernel,
        out_shape=[
            jax.ShapeDtypeStruct((rows, NECK), jnp.float32),
            jax.ShapeDtypeStruct((3 * number, ATTN_DIM), jnp.float32),
        ],
        scratch_shapes=[pltpu.VMEM((length, 3 * NECK), jnp.bfloat16)],
        compiler_params=params(),
        cost_estimate=pl.CostEstimate(
            flops=4 * rows * 9 * NECK * NECK, bytes_accessed=4 << 20, transcendentals=rows
        ),
        name="embedding_and_statistics",
    )(prev, following, edge, mid, w_neck2, gain, dec_qkv, code_keys, spread_queries)


def upscale_kernel(emb_ref, w1_ref, gain_ref, w2_ref, out_ref):
    first_out = full_dot(w1_ref[...], emb_ref[...], (((0,), (1,)), ((), ())))
    for corner in range(4):
        part = layer_norm(
            first_out[corner * UP1 : (corner + 1) * UP1, :], gain_ref[...], 1e-06, axis=0
        )
        second = full_dot(w2_ref[...], gelu(part), (((0,), (0,)), ((), ())))
        out_ref[corner * 4 * UP2 : (corner + 1) * 4 * UP2, :] = gelu(second).astype(jnp.bfloat16)


def upscale(embedding, w_up1, up_gain, w_up2):
    rows = embedding.shape[0]
    return pl.pallas_call(
        upscale_kernel,
        out_shape=jax.ShapeDtypeStruct((OFFSETS * UP2, rows), jnp.bfloat16),
        compiler_params=params(),
        cost_estimate=pl.CostEstimate(
            flops=20 * rows * NECK * NECK, bytes_accessed=4 << 20, transcendentals=rows * 768
        ),
        name="upscaled_channels",
    )(embedding, w_up1, up_gain, w_up2)


def masks_kernel(ranks, owners, *refs):
    stats = refs[:ranks]
    (tok_ref, wo_ref, gains_ref, w1_ref, w2_ref, wh_ref, who_ref, up_ref, out_ref) = refs[ranks:]
    number = tok_ref.shape[0]
    maxima = stats[0][number : 2 * number, :]
    for part in stats[1:]:
        maxima = jnp.maximum(maxima, part[number : 2 * number, :])
    mixed, totals = 0.0, 0.0
    for part in stats:
        scale = jnp.exp(part[number : 2 * number, :] - maxima)
        mixed = mixed + part[:number, :] * scale
        totals = totals + part[2 * number :, :] * scale
    cross = mixed / totals
    first_out = layer_norm(tok_ref[...] + full_dot(cross, wo_ref[...]), gains_ref[0:1, :], 1e-05)
    hidden = jnp.maximum(full_dot(first_out, w1_ref[...]), 0.0)
    second = layer_norm(first_out + full_dot(hidden, w2_ref[...]), gains_ref[1:2, :], 1e-05)
    hyper_vec = jnp.maximum(full_dot(second, wh_ref[0]), 0.0)
    hyper_vec = jnp.maximum(full_dot(hyper_vec, wh_ref[1]), 0.0)
    hyper_vec = full_dot(hyper_vec, who_ref[...]).astype(jnp.bfloat16)

    depth = OFFSETS * UP2
    span = OFFSETS * CAP
    channel = lax.broadcasted_iota(jnp.int32, (UP2, depth), 0)
    lane = lax.broadcasted_iota(jnp.int32, (UP2, depth), 1)
    repeat = jnp.where(lax.rem(lane, UP2) == channel, 1.0, 0.0).astype(jnp.bfloat16)
    tiled = jnp.dot(hyper_vec, repeat, preferred_element_type=jnp.float32).astype(jnp.bfloat16)
    row = lax.broadcasted_iota(jnp.int32, (owners * span, number), 0)
    slot = lax.broadcasted_iota(jnp.int32, (owners * span, number), 1)
    chosen = (row // span) * CAP + lax.rem(row, CAP)
    choose = jnp.where(chosen == slot, 1.0, 0.0).astype(jnp.bfloat16)
    spread = jnp.dot(choose, tiled, preferred_element_type=jnp.float32)
    row = lax.broadcasted_iota(jnp.int32, spread.shape, 0)
    lane = lax.broadcasted_iota(jnp.int32, spread.shape, 1)
    same = lax.rem(row, span) // CAP == lane // UP2
    spread = jnp.where(same, spread, 0.0).astype(jnp.bfloat16)
    for owner in range(owners):
        out_ref[owner] = jnp.dot(
            spread[owner * span : (owner + 1) * span, :],
            up_ref[...],
            preferred_element_type=jnp.float32,
        ).astype(jnp.bfloat16)


def mask_logits(stats, query_tok, owners, weights, upscaled):
    cells = upscaled.shape[1]
    return pl.pallas_call(
        functools.partial(masks_kernel, len(stats), owners),
        out_shape=jax.ShapeDtypeStruct((owners, OFFSETS * CAP, cells), jnp.bfloat16),
        compiler_params=params(),
        cost_estimate=pl.CostEstimate(
            flops=4 << 30, bytes_accessed=8 << 20, transcendentals=1 << 16
        ),
        name="token_side_and_masks",
    )(*stats, query_tok, *weights, upscaled)


def place_kernel(slots, recv_ref, choose_ref, order_ref, out_ref, tiles_ref):
    cells = recv_ref.shape[1]
    pairs = cells // LANES
    rows = jnp.dot(choose_ref[...], recv_ref[...], preferred_element_type=jnp.float32)
    rows = rows.astype(jnp.bfloat16)
    for top in range(2):
        for low in range(2):
            for pair in range(pairs):
                at = ((top * 2 + low) * pairs + pair) * slots
                for left in range(2):
                    for right in range(2):
                        offset = ((top * 2 + left) * 2 + low) * 2 + right
                        corner = left * 2 + right
                        tiles_ref[at : at + slots, corner * LANES : (corner + 1) * LANES] = rows[
                            offset * slots : (offset + 1) * slots,
                            pair * LANES : (pair + 1) * LANES,
                        ]
    ordered = jnp.dot(tiles_ref[...], order_ref[...], preferred_element_type=jnp.float32)
    width = 4 * GRID
    for top in range(2):
        for low in range(2):
            for pair in range(pairs):
                at = ((top * 2 + low) * pairs + pair) * slots
                for odd in range(2):
                    line = (2 * pair + odd) * 4 + top * 2 + low
                    out_ref[:, line * width : (line + 1) * width] = ordered[
                        at : at + slots, odd * width : (odd + 1) * width
                    ]


def place_rows(received, choose, order, slots):
    cells = received.shape[1]
    return pl.pallas_call(
        functools.partial(place_kernel, slots),
        out_shape=jax.ShapeDtypeStruct((slots, OFFSETS * cells), jnp.float32),
        scratch_shapes=[pltpu.VMEM((4 * (cells // LANES) * slots, 4 * LANES), jnp.bfloat16)],
        compiler_params=params(),
        cost_estimate=pl.CostEstimate(flops=1 << 30, bytes_accessed=4 << 20, transcendentals=0),
        name="rows_in_pixel_order",
    )(received, choose, order)


def pixel_order():
    source = np.arange(4 * LANES)
    corner, odd, column = source // LANES, source // GRID % 2, source % GRID
    target = odd * 4 * GRID + column * 4 + corner
    matrix = np.zeros((4 * LANES, 4 * LANES), np.float32)
    matrix[source, target] = 1.0
    return jnp.asarray(matrix, jnp.bfloat16)


def after(value, done):
    return lax.optimization_barrier((value, done))[0]


def shifted(block, shift, ranks):
    return lax.ppermute(block, "tok", [(i, (i + shift) % ranks) for i in range(ranks)])


def body(
    tokens,
    ln_gain,
    w_qkv,
    w_proj,
    w_neck1,
    neck_gain1,
    w_neck2,
    neck_gain2,
    pe_matrix,
    query_bias,
    dec_qkv,
    dec_out,
    dec_gains,
    w_mlp1,
    w_mlp2,
    w_hyper,
    w_hyper_out,
    w_up1,
    up_gain,
    w_up2,
    req_image,
    points,
):
    picture = tokens[0]
    tok_rows = picture.shape[0]
    grid_rows = tok_rows // GRID
    ranks = lax.axis_size("tok")
    owners = lax.axis_size("img")
    rank = lax.axis_index("tok")
    me = rank.astype(jnp.int32).reshape(1)
    edge = tok_rows // 4
    edge_spans = ((0, edge), (tok_rows - edge, tok_rows))
    mid_spans = ((edge, tok_rows - edge),)
    all_spans = ((0, tok_rows),)

    *first_blocks, normed = project(
        0, ranks, me, picture, ln_gain.reshape(1, -1), w_qkv, with_norm=True
    )
    first_in = [first_blocks[0]] + [
        shifted(first_blocks[shift], shift, ranks) for shift in range(1, ranks)
    ]
    second_blocks = project(
        1, ranks, me, normed, ln_gain.reshape(1, -1), w_qkv, with_norm=False
    )

    targets, spots, pe_late = after((req_image[:, 0], points, pe_matrix), first_blocks[0])
    slots = targets.shape[0]
    matches = (targets[:, None] == jnp.arange(owners, dtype=jnp.int32)[None, :]).astype(jnp.int32)
    order_no = jnp.sum((jnp.cumsum(matches, axis=0) - matches) * matches, axis=1)
    places = targets * CAP + order_no
    placing = (places[:, None] == jnp.arange(owners * CAP, dtype=jnp.int32)[None, :]).astype(
        jnp.float32
    )
    outgoing = jnp.einsum(
        "sp,sc->pc", placing, spots.astype(jnp.float32), precision=highest_precision
    )
    outgoing = outgoing.astype(jnp.int32).reshape(owners, CAP, 2)
    arrived = lax.all_to_all(outgoing, "img", split_axis=0, concat_axis=0, tiled=True)
    number = owners * CAP
    flattened = arrived.reshape(number, 2).astype(jnp.float32)
    query_tok = query_bias + fourier((flattened + 0.5) / IMG_SIDE * 2.0 - 1.0, pe_late)
    query_matrix = jnp.dot(query_tok, dec_qkv[0], precision=highest_precision)
    head_size = ATTN_DIM // DEC_HEADS
    head_mask = (
        jnp.arange(DEC_HEADS)[:, None] == jnp.arange(ATTN_DIM)[None, :] // head_size
    ).astype(jnp.float32)
    spread_queries = (head_mask[:, None, :] * query_matrix[None, :, :]).reshape(
        DEC_HEADS * number, ATTN_DIM
    )
    positional = grid_codes(rank * grid_rows, grid_rows, pe_late)
    code_keys = jnp.dot(positional, dec_qkv[1], precision=highest_precision)
    offset_eye = jnp.eye(OFFSETS, dtype=jnp.bfloat16)
    choose = (
        offset_eye[:, None, None, :, None]
        * placing.astype(jnp.bfloat16).reshape(1, slots, owners, 1, CAP)
    ).reshape(OFFSETS * slots, owners * OFFSETS * CAP)
    order = pixel_order()

    second_in = [second_blocks[0]] + [
        shifted(after(second_blocks[shift], first_in), shift, ranks) for shift in range(1, ranks)
    ]
    first_mixed = attention(first_in, all_spans)
    first_heads = [first_mixed[0]] + [
        shifted(after(first_mixed[shift], second_in), ranks - shift, ranks)
        for shift in range(1, ranks)
    ]
    edge_mixed = attention(second_in, edge_spans)
    edge_heads = [edge_mixed[0]] + [
        shifted(edge_mixed[shift], ranks - shift, ranks) for shift in range(1, ranks)
    ]
    mid_mixed = attention(second_in, mid_spans)
    mid_heads = [mid_mixed[0]] + [
        shifted(mid_mixed[shift], ranks - shift, ranks) for shift in range(1, ranks)
    ]
    gain1 = neck_gain1.reshape(1, -1)
    edge_narrow = neck(
        edge_spans, ranks, me, picture, w_proj, w_neck1, gain1, first_heads + edge_heads
    )
    ends = ranks - 1
    prev = lax.ppermute(edge_narrow[-GRID:], "tok", [(i, i + 1) for i in range(ends)])
    following = lax.ppermute(edge_narrow[:GRID], "tok", [(i + 1, i) for i in range(ends)])
    mid_narrow = neck(
        mid_spans, ranks, me, picture, w_proj, w_neck1, gain1, first_heads + mid_heads
    )

    embedding, stats = embed(
        prev,
        following,
        edge_narrow,
        mid_narrow,
        w_neck2,
        neck_gain2.reshape(1, -1),
        dec_qkv,
        code_keys,
        spread_queries,
    )
    all_stats = [stats] + [shifted(stats, shift, ranks) for shift in range(1, ranks)]
    upscaled = upscale(embedding, w_up1, up_gain.reshape(-1, 1), w_up2)
    outgoing = mask_logits(
        all_stats,
        query_tok,
        owners,
        (dec_out, dec_gains, w_mlp1, w_mlp2, w_hyper, w_hyper_out),
        upscaled,
    )
    answer = lax.all_to_all(outgoing, "img", split_axis=0, concat_axis=0, tiled=True)
    return place_rows(answer.reshape(number * OFFSETS, tok_rows), choose, order, slots)


def solution(mesh):
    placed = (
        (P("img", "tok", None),) + (P(),) * 19 + (P("img", None),) * 2
    )
    return jax.shard_map(
        body, mesh=mesh, in_specs=placed, out_specs=P("img", "tok"), check_vma=False
    )
```

```python
import functools
import math

import jax
import jax.numpy as jnp
import numpy as np
from jax import lax
from jax.experimental import pallas as pl
from jax.experimental.pallas import tpu as pltpu
from jax.sharding import PartitionSpec as P

HEADS = 8
HDIM = 80
GRID = 64
NECK = 256
ATTN_DIM = 128
DEC_HEADS = 8
UP1 = 64
UP2 = 32
IMG_SIDE = 1024
CAP = 4
LANES = 128
OFFSETS = 16
VMEM_BYTES = 56 << 20

highest_precision = lax.Precision.HIGHEST
TO_BASE2 = math.log2(math.e) / math.sqrt(HDIM)


def layer_norm(tensor, gain_vec, epsilon, axis=-1):
    average = jnp.mean(tensor, axis=axis, keepdims=True)
    centred = tensor - average
    spread = jnp.mean(centred * centred, axis=axis, keepdims=True)
    return centred * lax.rsqrt(spread + epsilon) * gain_vec


def gelu(tensor):
    return 0.5 * tensor * (1.0 + lax.erf(tensor * math.sqrt(0.5)))


def fourier(coords, pe_matrix):
    angles = 2.0 * math.pi * jnp.dot(coords, pe_matrix, precision=highest_precision)
    return jnp.concatenate([jnp.sin(angles), jnp.cos(angles)], axis=-1)


def grid_codes(first_row, grid_rows, pe_matrix):
    row_ids = (first_row + jnp.arange(grid_rows, dtype=jnp.int32)).astype(jnp.float32)
    col_ids = jnp.arange(GRID, dtype=jnp.int32).astype(jnp.float32)
    ycoord = (row_ids + 0.5) / GRID * 2.0 - 1.0
    xcoord = (col_ids + 0.5) / GRID * 2.0 - 1.0
    across = 2.0 * math.pi * (xcoord[:, None] * pe_matrix[0])
    down = 2.0 * math.pi * (ycoord[:, None] * pe_matrix[1])
    sin_x, cos_x = jnp.sin(across)[None], jnp.cos(across)[None]
    sin_y, cos_y = jnp.sin(down)[:, None], jnp.cos(down)[:, None]
    codes = jnp.concatenate(
        [sin_x * cos_y + cos_x * sin_y, cos_x * cos_y - sin_x * sin_y], axis=-1
    )
    return codes.reshape(grid_rows * GRID, 2 * pe_matrix.shape[1])


def params(**extra):
    return pltpu.CompilerParams(vmem_limit_bytes=VMEM_BYTES, **extra)


def split(tensor):
    high = tensor.astype(jnp.bfloat16)
    return high, (tensor - high.astype(jnp.float32)).astype(jnp.bfloat16)


def split_dot(left, right):
    rows = left.shape[0]
    both = jnp.dot(jnp.concatenate(split(left)), right, preferred_element_type=jnp.float32)
    return both[:rows] + both[rows:]


def head_span(span, ranks):
    first = span * ranks * HDIM
    start = first // LANES * LANES
    stop = -(-(first + ranks * HDIM) // LANES) * LANES
    return first, start, stop


def project_kernel(span, ranks, with_norm, parts, me_ref, x_ref, gain_ref, w_hbm, *refs):
    inner = HEADS * HDIM
    count = len(parts) * ranks
    outs = refs[:count]
    weights, rows_ref, sems = refs[-3:]
    first, start, stop = head_span(span, ranks)
    width = stop - start
    step = pl.program_id(0)
    copies = [
        pltpu.make_async_copy(
            w_hbm.at[:, pl.ds(part * inner + start, width)],
            weights.at[:, pl.ds(part * width, width)],
            sems.at[part],
        )
        for part in range(3)
    ]

    @pl.when(step == 0)
    def _():
        for copy in copies:
            copy.start()

    if with_norm:
        gain = gain_ref[...].reshape(1, -1)
        normed = layer_norm(x_ref[...].astype(jnp.float32), gain, 1e-06).astype(jnp.bfloat16)
        refs[count][...] = normed
    else:
        normed = x_ref[...]

    @pl.when(step == 0)
    def _():
        for copy in copies:
            copy.wait()

    rows_ref[...] = (
        jnp.dot(normed, weights[...], preferred_element_type=jnp.float32).astype(jnp.bfloat16).T
    )
    for index, wanted in enumerate(parts):
        for shift in range(ranks):
            out = outs[index * ranks + shift]
            columns = pl.ds(0, out.shape[1])
            if out.shape[1] < rows_ref.shape[1]:
                place = step if index == 0 else 1 - step
                columns = pl.ds(pl.multiple_of(place * out.shape[1], LANES), out.shape[1])
            head = lax.rem(me_ref[0] + shift, ranks)
            for at, part in enumerate(wanted):
                place = pl.multiple_of(head * HDIM + (part * width + first - start), 16)
                out[at * HDIM : (at + 1) * HDIM, :] = rows_ref[pl.ds(place, HDIM), columns]


def project(span, ranks, parts, me, source, ln_gain, w_qkv, with_norm):
    rows, model = source.shape
    block = rows // 2
    _, start, stop = head_span(span, ranks)
    width = stop - start
    sizes = [
        (len(wanted) * HDIM, block // parts.count(wanted))
        for wanted in parts
        for _ in range(ranks)
    ]
    out_shape = [jax.ShapeDtypeStruct((high, 2 * wide), jnp.bfloat16) for high, wide in sizes]
    out_specs = [pl.BlockSpec(size, lambda i: (0, i)) for size in sizes]
    if with_norm:
        out_shape = out_shape + [jax.ShapeDtypeStruct((rows, model), jnp.bfloat16)]
        out_specs = out_specs + [pl.BlockSpec((block, model), lambda i: (i, 0))]
    return pl.pallas_call(
        functools.partial(project_kernel, span, ranks, with_norm, parts),
        grid=(rows // block,),
        in_specs=[
            pl.BlockSpec(memory_space=pltpu.SMEM),
            pl.BlockSpec((block, model), lambda i: (i, 0)),
            pl.BlockSpec((model,), lambda i: (0,)),
            pl.BlockSpec(memory_space=pl.ANY),
        ],
        out_specs=out_specs,
        out_shape=out_shape,
        scratch_shapes=[
            pltpu.VMEM((model, 3 * width), jnp.bfloat16),
            pltpu.VMEM((3 * width, block), jnp.bfloat16),
            pltpu.SemaphoreType.DMA((3,)),
        ],
        compiler_params=params(),
        cost_estimate=pl.CostEstimate(
            flops=2 * rows * model * 3 * width, bytes_accessed=10 << 20, transcendentals=rows
        ),
        name="norm_and_projections" if with_norm else "projections",
    )(me, source, ln_gain, w_qkv)


def attention_kernel(query_block, key_block, ranks, *refs):
    sources = len(refs[: -4 - ranks]) // 2
    query_refs, kv_refs = refs[:sources], refs[sources : sources + ranks]
    outs = refs[sources + ranks : -4]
    queries, keys, values, mixed_out = refs[-4:]
    rows = kv_refs[0].shape[1]
    key_row = kv_refs[0].shape[0] - 2 * HDIM
    total = ranks * rows
    piece = min(query_block, 256)
    per_tile = query_block // piece

    columns = range(0, query_refs[0].shape[1], piece)
    places = [(source, at) for source in range(sources) for at in columns]
    for number, (source, at) in enumerate(places):
        tile, inside = number // per_tile, number % per_tile * piece
        queries[tile, :, inside : inside + piece] = query_refs[source][:HDIM, at : at + piece]
    for rank in range(ranks):
        span = slice(rank * rows, (rank + 1) * rows)
        keys[span, :] = kv_refs[rank][key_row : key_row + HDIM, :].T
        values[:HDIM, span] = kv_refs[rank][key_row + HDIM :, :]
    values[HDIM:, :] = jnp.ones((values.shape[0] - HDIM, total), jnp.bfloat16)
    steps = total // key_block

    def one_block(step, carry):
        query = queries[step]

        def scores_of(at):
            return lax.dot_general(
                keys[at * key_block : (at + 1) * key_block, :],
                query,
                (((1,), (0,)), ((), ())),
                preferred_element_type=jnp.float32,
            )

        maxima, mixed = None, None
        upcoming = scores_of(0)
        for at in range(steps):
            scores = upcoming
            if at + 1 < steps:
                upcoming = scores_of(at + 1)
            block_max = jnp.max(scores, axis=0, keepdims=True)
            new_max = block_max if maxima is None else jnp.maximum(maxima, block_max)
            weights = jnp.exp2((scores - new_max) * TO_BASE2).astype(jnp.bfloat16)
            share = jnp.dot(
                values[:, at * key_block : (at + 1) * key_block],
                weights,
                preferred_element_type=jnp.float32,
            )
            if maxima is None:
                mixed = share
            else:
                mixed = mixed * jnp.exp2((maxima - new_max) * TO_BASE2) + share
            maxima = new_max
        mixed_out[step] = (mixed[:HDIM, :] / mixed[HDIM : HDIM + 1, :]).astype(jnp.bfloat16)
        return carry

    if queries.shape[0] == 1:
        one_block(0, 0)
    else:
        lax.fori_loop(0, queries.shape[0], one_block, 0)
    for number, (source, at) in enumerate(places):
        tile, inside = number // per_tile, number % per_tile * piece
        outs[source][:, at : at + piece] = mixed_out[tile, :, inside : inside + piece]


def attention(queries, key_values):
    ranks, rows = len(key_values), key_values[0].shape[1]
    wanted = queries[0].shape[1]
    columns = len(queries) * wanted
    query_block = next(size for size in (1024, 768, 512, 256, columns) if columns % size == 0)
    key_block = min(ranks * rows, 512)
    tiles = columns // query_block
    return list(pl.pallas_call(
        functools.partial(attention_kernel, query_block, key_block, ranks),
        out_shape=[jax.ShapeDtypeStruct((HDIM, wanted), jnp.bfloat16)] * len(queries),
        scratch_shapes=[
            pltpu.VMEM((tiles, HDIM, query_block), jnp.bfloat16),
            pltpu.VMEM((ranks * rows, HDIM), jnp.bfloat16),
            pltpu.VMEM((HDIM + 16, ranks * rows), jnp.bfloat16),
            pltpu.VMEM((tiles, HDIM, query_block), jnp.bfloat16),
        ],
        compiler_params=params(),
        cost_estimate=pl.CostEstimate(
            flops=12 * columns * ranks * rows * HDIM,
            bytes_accessed=4 << 20,
            transcendentals=columns * ranks * rows,
        ),
        name="head_attention",
    )(*queries, *key_values))


def neck_kernel(ranks, me_ref, tok_ref, wp_ref, wn_ref, gain_ref, *refs):
    heads = refs[:-2]
    out_ref, joined_ref = refs[-2:]
    for number, part in enumerate(heads):
        span, shift = number // ranks, number % ranks
        head = lax.rem(me_ref[0] + shift, ranks) + span * ranks
        joined_ref[pl.ds(pl.multiple_of(head * HDIM, 16), HDIM), :] = part[...]
    attended = joined_ref[...].T
    block_out = tok_ref[...].astype(jnp.float32) + jnp.dot(
        attended, wp_ref[...], preferred_element_type=jnp.float32
    )
    narrow = jnp.dot(
        block_out.astype(jnp.bfloat16), wn_ref[...], preferred_element_type=jnp.float32
    )
    out_ref[...] = layer_norm(narrow, gain_ref[...].reshape(1, -1), 1e-06).astype(jnp.bfloat16)


def neck(first, step, block, ranks, me, tokens, w_proj, w_neck1, gain, heads):
    rows, model = tokens.shape

    def head_spec(part):
        if part.shape[1] == rows:
            return pl.BlockSpec((HDIM, block), lambda i: (0, first + i * step))
        return pl.BlockSpec((HDIM, block), lambda i: (0, i))

    return pl.pallas_call(
        functools.partial(neck_kernel, ranks),
        grid=(2,),
        in_specs=[
            pl.BlockSpec(memory_space=pltpu.SMEM),
            pl.BlockSpec((block, model), lambda i: (first + i * step, 0)),
            pl.BlockSpec(w_proj.shape, lambda i: (0, 0)),
            pl.BlockSpec(w_neck1.shape, lambda i: (0, 0)),
            pl.BlockSpec(gain.shape, lambda i: (0,)),
        ]
        + [head_spec(part) for part in heads],
        out_specs=pl.BlockSpec((block, NECK), lambda i: (i, 0)),
        out_shape=jax.ShapeDtypeStruct((2 * block, NECK), jnp.bfloat16),
        scratch_shapes=[pltpu.VMEM((HEADS * HDIM, block), jnp.bfloat16)],
        compiler_params=params(),
        cost_estimate=pl.CostEstimate(
            flops=4 * block * model * (HEADS * HDIM + NECK),
            bytes_accessed=6 << 20,
            transcendentals=block,
        ),
        name="proj_and_narrow",
    )(me, tokens, w_proj, w_neck1, gain, *heads)


def embed_kernel(
    prev_ref,
    next_ref,
    edge_ref,
    mid_ref,
    w_ref,
    gain_ref,
    kv_ref,
    key_low_ref,
    code_ref,
    query_ref,
    emb_ref,
    stats_ref,
    cells_ref,
):
    rows = emb_ref.shape[0]
    half = edge_ref.shape[0] // 2
    map_rows = jnp.concatenate(
        [prev_ref[...], edge_ref[:half, :], mid_ref[...], edge_ref[half:, :], next_ref[...]], axis=0
    )
    wide = map_rows.astype(jnp.float32)
    length = wide.shape[0]
    column = lax.rem(lax.broadcasted_iota(jnp.int32, (length, 1), 0), GRID)
    before = jnp.where(column == 0, 0.0, pltpu.roll(wide, 1, 0))
    after = jnp.where(column == GRID - 1, 0.0, pltpu.roll(wide, length - 1, 0))
    cells_ref[:, :NECK] = before.astype(jnp.bfloat16)
    cells_ref[:, NECK : 2 * NECK] = map_rows
    cells_ref[:, 2 * NECK :] = after.astype(jnp.bfloat16)
    total = None
    for row_off in range(3):
        share = jnp.dot(
            cells_ref[row_off * GRID : row_off * GRID + rows, :],
            w_ref[row_off * 3 * NECK : (row_off + 1) * 3 * NECK, :],
            preferred_element_type=jnp.float32,
        )
        total = share if total is None else total + share
    embedding = layer_norm(total, gain_ref[...].reshape(1, -1), 1e-06)
    high, low = split(embedding)
    emb_ref[...] = high

    both = jnp.dot(high, kv_ref[...], preferred_element_type=jnp.float32) + jnp.dot(
        low, kv_ref[...], preferred_element_type=jnp.float32
    )
    dec_keys = both[:, :ATTN_DIM] + jnp.dot(
        high, key_low_ref[...], preferred_element_type=jnp.float32
    )
    dec_keys = dec_keys + code_ref[...]
    dec_values = both[:, ATTN_DIM:].astype(jnp.bfloat16)
    head_size = ATTN_DIM // DEC_HEADS
    key_high, key_low = split(dec_keys)
    query_high, query_low = split(query_ref[...])
    across = (((1,), (1,)), ((), ()))
    scores = (
        lax.dot_general(query_high, key_high, across, preferred_element_type=jnp.float32)
        + lax.dot_general(query_low, key_high, across, preferred_element_type=jnp.float32)
        + lax.dot_general(query_high, key_low, across, preferred_element_type=jnp.float32)
    )
    scores = scores * (1.0 / math.sqrt(head_size))
    maxima = jnp.max(scores, axis=1, keepdims=True)
    weights = jnp.exp(scores - maxima)
    totals = jnp.sum(weights, axis=1, keepdims=True)
    mixed = jnp.dot(weights.astype(jnp.bfloat16), dec_values, preferred_element_type=jnp.float32)
    number = stats_ref.shape[0] // 3
    lane_head = lax.broadcasted_iota(jnp.int32, (1, ATTN_DIM), 1) // head_size
    for at, stat in enumerate((mixed, maxima, totals)):
        picked = jnp.zeros((number, ATTN_DIM), jnp.float32)
        for head in range(DEC_HEADS):
            picked = jnp.where(
                lane_head == head, stat[head * number : (head + 1) * number, :], picked
            )
        stats_ref[at * number : (at + 1) * number, :] = picked


def embed(prev, following, edge, mid, w_neck2, gain, kv, key_low, code_keys, spread_queries):
    rows = edge.shape[0] + mid.shape[0]
    number = spread_queries.shape[0] // DEC_HEADS
    length = rows + prev.shape[0] + following.shape[0]
    return pl.pallas_call(
        embed_kernel,
        out_shape=[
            jax.ShapeDtypeStruct((rows, NECK), jnp.bfloat16),
            jax.ShapeDtypeStruct((3 * number, ATTN_DIM), jnp.float32),
        ],
        scratch_shapes=[pltpu.VMEM((length, 3 * NECK), jnp.bfloat16)],
        compiler_params=params(),
        cost_estimate=pl.CostEstimate(
            flops=4 * rows * 9 * NECK * NECK, bytes_accessed=4 << 20, transcendentals=rows
        ),
        name="embedding_and_statistics",
    )(prev, following, edge, mid, w_neck2, gain, kv, key_low, code_keys, spread_queries)


def upscale_kernel(emb_ref, w1_ref, gain_ref, w2_ref, out_ref):
    first_out = lax.dot_general(
        w1_ref[...], emb_ref[...], (((0,), (1,)), ((), ())), preferred_element_type=jnp.float32
    )
    for corner in range(4):
        part = layer_norm(
            first_out[corner * UP1 : (corner + 1) * UP1, :], gain_ref[...], 1e-06, axis=0
        )
        second = lax.dot_general(
            w2_ref[...],
            gelu(part).astype(jnp.bfloat16),
            (((0,), (0,)), ((), ())),
            preferred_element_type=jnp.float32,
        )
        out_ref[corner * 4 * UP2 : (corner + 1) * 4 * UP2, :] = gelu(second).astype(jnp.bfloat16)


def upscale(embedding, w_up1, up_gain, w_up2):
    rows = embedding.shape[0]
    return pl.pallas_call(
        upscale_kernel,
        out_shape=jax.ShapeDtypeStruct((OFFSETS * UP2, rows), jnp.bfloat16),
        compiler_params=params(),
        cost_estimate=pl.CostEstimate(
            flops=20 * rows * NECK * NECK, bytes_accessed=4 << 20, transcendentals=rows * 768
        ),
        name="upscaled_channels",
    )(embedding, w_up1, up_gain, w_up2)


def masks_kernel(ranks, owners, *refs):
    stats = refs[:ranks]
    (tok_ref, wo_ref, gains_ref, w1_ref, w2_ref, wh_ref, who_ref, up_ref, out_ref) = refs[ranks:]
    number = tok_ref.shape[0]
    maxima = stats[0][number : 2 * number, :]
    for part in stats[1:]:
        maxima = jnp.maximum(maxima, part[number : 2 * number, :])
    mixed, totals = 0.0, 0.0
    for part in stats:
        scale = jnp.exp(part[number : 2 * number, :] - maxima)
        mixed = mixed + part[:number, :] * scale
        totals = totals + part[2 * number :, :] * scale
    cross = mixed / totals
    first_out = layer_norm(tok_ref[...] + split_dot(cross, wo_ref[...]), gains_ref[0:1, :], 1e-05)
    hidden = jnp.maximum(split_dot(first_out, w1_ref[...]), 0.0)
    second = layer_norm(first_out + split_dot(hidden, w2_ref[...]), gains_ref[1:2, :], 1e-05)
    hyper_vec = jnp.maximum(split_dot(second, wh_ref[0]), 0.0)
    hyper_vec = jnp.maximum(split_dot(hyper_vec, wh_ref[1]), 0.0)
    hyper_vec = split_dot(hyper_vec, who_ref[...]).astype(jnp.bfloat16)

    depth = OFFSETS * UP2
    span = OFFSETS * CAP
    channel = lax.broadcasted_iota(jnp.int32, (UP2, depth), 0)
    lane = lax.broadcasted_iota(jnp.int32, (UP2, depth), 1)
    repeat = jnp.where(lax.rem(lane, UP2) == channel, 1.0, 0.0).astype(jnp.bfloat16)
    tiled = jnp.dot(hyper_vec, repeat, preferred_element_type=jnp.float32).astype(jnp.bfloat16)
    row = lax.broadcasted_iota(jnp.int32, (owners * span, number), 0)
    slot = lax.broadcasted_iota(jnp.int32, (owners * span, number), 1)
    chosen = (row // span) * CAP + lax.rem(row, CAP)
    choose = jnp.where(chosen == slot, 1.0, 0.0).astype(jnp.bfloat16)
    spread = jnp.dot(choose, tiled, preferred_element_type=jnp.float32)
    row = lax.broadcasted_iota(jnp.int32, spread.shape, 0)
    lane = lax.broadcasted_iota(jnp.int32, spread.shape, 1)
    same = lax.rem(row, span) // CAP == lane // UP2
    spread = jnp.where(same, spread, 0.0).astype(jnp.bfloat16)
    for owner in range(owners):
        out_ref[owner] = jnp.dot(
            spread[owner * span : (owner + 1) * span, :],
            up_ref[...],
            preferred_element_type=jnp.float32,
        ).astype(jnp.bfloat16)


def mask_logits(stats, query_tok, owners, weights, upscaled):
    cells = upscaled.shape[1]
    return pl.pallas_call(
        functools.partial(masks_kernel, len(stats), owners),
        out_shape=jax.ShapeDtypeStruct((owners, OFFSETS * CAP, cells), jnp.bfloat16),
        compiler_params=params(),
        cost_estimate=pl.CostEstimate(
            flops=4 << 30, bytes_accessed=8 << 20, transcendentals=1 << 16
        ),
        name="token_side_and_masks",
    )(*stats, query_tok, *weights, upscaled)


def place_kernel(slots, recv_ref, choose_ref, order_ref, out_ref, tiles_ref):
    cells = recv_ref.shape[1]
    pairs = cells // LANES
    rows = jnp.dot(choose_ref[...], recv_ref[...], preferred_element_type=jnp.float32)
    rows = rows.astype(jnp.bfloat16)
    for top in range(2):
        for low in range(2):
            for pair in range(pairs):
                at = ((top * 2 + low) * pairs + pair) * slots
                for left in range(2):
                    for right in range(2):
                        offset = ((top * 2 + left) * 2 + low) * 2 + right
                        corner = left * 2 + right
                        tiles_ref[at : at + slots, corner * LANES : (corner + 1) * LANES] = rows[
                            offset * slots : (offset + 1) * slots,
                            pair * LANES : (pair + 1) * LANES,
                        ]
    ordered = jnp.dot(tiles_ref[...], order_ref[...], preferred_element_type=jnp.float32)
    width = 4 * GRID
    for top in range(2):
        for low in range(2):
            for pair in range(pairs):
                at = ((top * 2 + low) * pairs + pair) * slots
                for odd in range(2):
                    line = (2 * pair + odd) * 4 + top * 2 + low
                    out_ref[:, line * width : (line + 1) * width] = ordered[
                        at : at + slots, odd * width : (odd + 1) * width
                    ]


def place_rows(received, choose, order, slots):
    cells = received.shape[1]
    return pl.pallas_call(
        functools.partial(place_kernel, slots),
        out_shape=jax.ShapeDtypeStruct((slots, OFFSETS * cells), jnp.float32),
        scratch_shapes=[pltpu.VMEM((4 * (cells // LANES) * slots, 4 * LANES), jnp.bfloat16)],
        compiler_params=params(),
        cost_estimate=pl.CostEstimate(flops=1 << 30, bytes_accessed=4 << 20, transcendentals=0),
        name="rows_in_pixel_order",
    )(received, choose, order)


def pixel_order():
    source = np.arange(4 * LANES)
    corner, odd, column = source // LANES, source // GRID % 2, source % GRID
    target = odd * 4 * GRID + column * 4 + corner
    matrix = np.zeros((4 * LANES, 4 * LANES), np.float32)
    matrix[source, target] = 1.0
    return jnp.asarray(matrix, jnp.bfloat16)


def after(value, done):
    return lax.optimization_barrier((value, done))[0]


def shifted(block, shift, ranks):
    return lax.ppermute(block, "tok", [(i, (i + shift) % ranks) for i in range(ranks)])


def exchanged(blocks, back=False):
    ranks = len(blocks)
    return [blocks[0]] + [
        shifted(blocks[shift], ranks - shift if back else shift, ranks)
        for shift in range(1, ranks)
    ]


def gathered(block, axis):
    count = lax.axis_size(axis)
    if count & (count - 1):
        return lax.all_gather(block, axis, axis=0, tiled=True)
    place = lax.axis_index(axis)
    reach = 1
    while reach < count:
        other = lax.ppermute(block, axis, [(i, i ^ reach) for i in range(count)])
        low = (place & reach) == 0
        block = jnp.concatenate([jnp.where(low, block, other), jnp.where(low, other, block)])
        reach *= 2
    return block


def body(
    tokens,
    ln_gain,
    w_qkv,
    w_proj,
    w_neck1,
    neck_gain1,
    w_neck2,
    neck_gain2,
    pe_matrix,
    query_bias,
    dec_qkv,
    dec_out,
    dec_gains,
    w_mlp1,
    w_mlp2,
    w_hyper,
    w_hyper_out,
    w_up1,
    up_gain,
    w_up2,
    req_image,
    points,
):
    picture = tokens[0]
    tok_rows = picture.shape[0]
    grid_rows = tok_rows // GRID
    ranks = lax.axis_size("tok")
    owners = lax.axis_size("img")
    rank = lax.axis_index("tok")
    me = rank.astype(jnp.int32).reshape(1)
    edge = tok_rows // 4
    *first_out, normed = project(
        0, ranks, ((0,), (1, 2)), me, picture, ln_gain, w_qkv, with_norm=True
    )
    first_kv = exchanged(first_out[ranks:])
    first_queries = exchanged(after(first_out[:ranks], first_kv[1:]))
    second_out = project(
        1, ranks, ((0,), (0,), (1, 2)), me, normed, ln_gain, w_qkv, with_norm=False
    )
    edge_out, mid_out, kv_out = (second_out[at * ranks : (at + 1) * ranks] for at in range(3))

    (targets, spots, pe_late, decoder) = after(
        (
            req_image[:, 0],
            points,
            pe_matrix,
            (dec_out, w_mlp1, w_mlp2, w_hyper, w_hyper_out, w_up1, w_up2, dec_qkv),
        ),
        edge_out[0],
    )
    dec_qkv = decoder[-1]
    rounded = [weight.astype(jnp.bfloat16) for weight in decoder]
    key_value = jnp.concatenate([rounded[-1][1], rounded[-1][2]], axis=1)
    key_low = split(dec_qkv[1])[1]
    slots = targets.shape[0]
    asked = jnp.concatenate([targets[:, None], spots], axis=1)
    everyone = gathered(asked[None], "img")
    here = (everyone[:, :, 0] == lax.axis_index("img")).astype(jnp.int32)
    turn = jnp.cumsum(here, axis=1) - here
    filling = here[:, :, None] * (turn[:, :, None] == jnp.arange(CAP)[None, None, :])
    arrived = jnp.sum(filling[:, :, :, None] * everyone[:, :, None, 1:], axis=1)
    matches = (targets[:, None] == jnp.arange(owners, dtype=jnp.int32)[None, :]).astype(jnp.int32)
    order_no = jnp.sum((jnp.cumsum(matches, axis=0) - matches) * matches, axis=1)
    places = targets * CAP + order_no
    placing = places[:, None] == jnp.arange(owners * CAP, dtype=jnp.int32)[None, :]
    number = owners * CAP
    flattened = arrived.reshape(number, 2).astype(jnp.float32)
    query_tok = query_bias + fourier((flattened + 0.5) / IMG_SIDE * 2.0 - 1.0, pe_late)
    query_matrix = jnp.dot(query_tok, dec_qkv[0], precision=highest_precision)
    head_size = ATTN_DIM // DEC_HEADS
    head_mask = (
        jnp.arange(DEC_HEADS)[:, None] == jnp.arange(ATTN_DIM)[None, :] // head_size
    ).astype(jnp.float32)
    spread_queries = (head_mask[:, None, :] * query_matrix[None, :, :]).reshape(
        DEC_HEADS * number, ATTN_DIM
    )
    positional = grid_codes(rank * grid_rows, grid_rows, pe_late)
    code_high, code_low = split(positional)
    key_high = rounded[-1][1]
    code_keys = jnp.dot(
        jnp.concatenate([code_high, code_low, code_high], axis=1),
        jnp.concatenate([key_high, key_high, key_low]),
        preferred_element_type=jnp.float32,
    )
    offset_eye = jnp.eye(OFFSETS, dtype=jnp.bfloat16)
    choose = (
        offset_eye[:, None, None, :, None]
        * placing.astype(jnp.bfloat16).reshape(1, slots, owners, 1, CAP)
    ).reshape(OFFSETS * slots, owners * OFFSETS * CAP)
    order = pixel_order()

    kv_in = exchanged(after(kv_out, first_queries[1:]))
    own_first = attention(first_queries[:1], first_kv)
    first_mixed = own_first + attention(first_queries[1:], first_kv)
    edge_in = exchanged(after(edge_out, (kv_in[1:], first_mixed)))
    own_edge, own_mid = attention(after([edge_out[0], mid_out[0]], first_mixed), kv_in)
    mid_in = exchanged(after(mid_out, (edge_in[1:], own_edge)))
    edge_mixed = [own_edge] + attention(edge_in[1:], kv_in)
    first_heads = exchanged(after(first_mixed, (mid_in[1:], edge_mixed)), back=True)
    edge_heads = exchanged(edge_mixed, back=True)
    mid_mixed = [own_mid] + attention(mid_in[1:], kv_in)
    mid_heads = exchanged(mid_mixed, back=True)
    neck_args = (edge, ranks, me, picture, w_proj, w_neck1, neck_gain1)
    edge_narrow = neck(0, 3, *neck_args, first_heads + edge_heads)
    ends = ranks - 1
    prev = lax.ppermute(edge_narrow[-GRID:], "tok", [(i, i + 1) for i in range(ends)])
    following = lax.ppermute(edge_narrow[:GRID], "tok", [(i + 1, i) for i in range(ends)])
    mid_narrow = neck(1, 1, *neck_args, first_heads + mid_heads)

    embedding, stats = embed(
        prev,
        following,
        edge_narrow,
        mid_narrow,
        w_neck2,
        neck_gain2,
        key_value,
        key_low,
        code_keys,
        spread_queries,
    )
    all_stats = exchanged([stats] * ranks)
    upscaled = upscale(embedding, rounded[5], up_gain.reshape(-1, 1), rounded[6])
    outgoing = mask_logits(
        all_stats,
        query_tok,
        owners,
        (rounded[0], dec_gains, *rounded[1:5]),
        upscaled,
    )
    answer = lax.all_to_all(outgoing, "img", split_axis=0, concat_axis=0, tiled=True)
    return place_rows(answer.reshape(number * OFFSETS, tok_rows), choose, order, slots)


def solution(mesh):
    placed = (
        (P("img", "tok", None),) + (P(),) * 19 + (P("img", None),) * 2
    )
    return jax.shard_map(
        body, mesh=mesh, in_specs=placed, out_specs=P("img", "tok"), check_vma=False
    )
```

```python
import functools
import math

import jax
import jax.numpy as jnp
import numpy as np
from jax import lax
from jax.experimental import pallas as pl
from jax.experimental.pallas import tpu as pltpu
from jax.sharding import PartitionSpec as P

HEADS = 8
HDIM = 80
GRID = 64
NECK = 256
ATTN_DIM = 128
DEC_HEADS = 8
UP1 = 64
UP2 = 32
IMG_SIDE = 1024
CAP = 4
LANES = 128
OFFSETS = 16
VMEM_BYTES = 24 << 20
WHOLE_VMEM_BYTES = 56 << 20

highest_precision = lax.Precision.HIGHEST
SMALL = pl.CostEstimate(flops=1 << 10, bytes_accessed=1 << 10, transcendentals=0)
TO_BASE2 = math.log2(math.e) / math.sqrt(HDIM)


def layer_norm(tensor, gain_vec, epsilon, axis=-1):
    average = jnp.mean(tensor, axis=axis, keepdims=True)
    centred = tensor - average
    spread = jnp.mean(centred * centred, axis=axis, keepdims=True)
    return centred * lax.rsqrt(spread + epsilon) * gain_vec


def gelu(tensor):
    return 0.5 * tensor * (1.0 + lax.erf(tensor * math.sqrt(0.5)))


def fourier(coords, pe_matrix):
    angles = 2.0 * math.pi * jnp.dot(coords, pe_matrix, precision=highest_precision)
    return jnp.concatenate([jnp.sin(angles), jnp.cos(angles)], axis=-1)


def grid_sines(first_row, grid_rows, pe_matrix):
    row_ids = (first_row + jnp.arange(grid_rows, dtype=jnp.int32)).astype(jnp.float32)
    col_ids = jnp.arange(GRID, dtype=jnp.int32).astype(jnp.float32)
    ycoord = (row_ids + 0.5) / GRID * 2.0 - 1.0
    xcoord = (col_ids + 0.5) / GRID * 2.0 - 1.0
    angles = jnp.concatenate([xcoord[:, None] * pe_matrix[0], ycoord[:, None] * pe_matrix[1]])
    angles = 2.0 * math.pi * angles
    return jnp.concatenate([jnp.sin(angles), jnp.cos(angles)], axis=1)


def params(**extra):
    return pltpu.CompilerParams(vmem_limit_bytes=VMEM_BYTES, **extra)


def split(tensor):
    high = tensor.astype(jnp.bfloat16)
    return high, (tensor - high.astype(jnp.float32)).astype(jnp.bfloat16)


def split_dot(left, right):
    rows = left.shape[0]
    both = jnp.dot(jnp.concatenate(split(left)), right, preferred_element_type=jnp.float32)
    return both[:rows] + both[rows:]


def prepare_kernel(
    sines_ref,
    qkv_ref,
    wo_ref,
    w1_ref,
    w2_ref,
    wh_ref,
    who_ref,
    up1_ref,
    up2_ref,
    token_ref,
    up_ref,
    key_value_ref,
    code_ref,
    codes_ref,
):
    hidden = w1_ref.shape[1]
    for block in range(hidden // NECK):
        columns = slice(block * NECK, (block + 1) * NECK)
        token_ref[columns, :] = w1_ref[:, columns].astype(jnp.bfloat16)
    token_ref[hidden : 2 * hidden, :] = w2_ref[...].astype(jnp.bfloat16)
    at = 2 * hidden
    for layer in range(2):
        token_ref[at : at + NECK, :] = wh_ref[layer].astype(jnp.bfloat16)
        at += NECK
    token_ref[at : at + NECK, :UP2] = who_ref[...].astype(jnp.bfloat16)
    at += NECK
    token_ref[at:, :] = wo_ref[...].astype(jnp.bfloat16)
    up_ref[:NECK, :] = up1_ref[...].astype(jnp.bfloat16)
    up_ref[NECK:, : 4 * UP2] = up2_ref[...].astype(jnp.bfloat16)
    key_high, key_low = split(qkv_ref[1])
    key_value_ref[:, :ATTN_DIM] = key_high
    key_value_ref[:, ATTN_DIM : 2 * ATTN_DIM] = qkv_ref[2].astype(jnp.bfloat16)
    key_value_ref[:, 2 * ATTN_DIM :] = key_low
    half = sines_ref.shape[1] // 2
    sin_x, cos_x = sines_ref[:GRID, :half], sines_ref[:GRID, half:]
    for row in range(sines_ref.shape[0] - GRID):
        sin_y = sines_ref[GRID + row : GRID + row + 1, :half]
        cos_y = sines_ref[GRID + row : GRID + row + 1, half:]
        at = row * GRID
        codes_ref[at : at + GRID, :half] = sin_x * cos_y + cos_x * sin_y
        codes_ref[at : at + GRID, half:] = cos_x * cos_y - sin_x * sin_y
    code_high, code_low = split(codes_ref[...])
    code_ref[...] = (
        jnp.dot(code_high, key_high, preferred_element_type=jnp.float32)
        + jnp.dot(code_low, key_high, preferred_element_type=jnp.float32)
        + jnp.dot(code_high, key_low, preferred_element_type=jnp.float32)
    )


def prepare(sines, dec_qkv, dec_out, w_mlp1, w_mlp2, *weights):
    cells = (sines.shape[0] - GRID) * GRID
    rows = 2 * w_mlp1.shape[1] + 3 * NECK + ATTN_DIM
    return pl.pallas_call(
        prepare_kernel,
        out_shape=[
            jax.ShapeDtypeStruct((rows, NECK), jnp.bfloat16),
            jax.ShapeDtypeStruct((NECK + UP1, NECK), jnp.bfloat16),
            jax.ShapeDtypeStruct((NECK, 3 * ATTN_DIM), jnp.bfloat16),
            jax.ShapeDtypeStruct((cells, ATTN_DIM), jnp.float32),
        ],
        scratch_shapes=[pltpu.VMEM((cells, NECK), jnp.float32)],
        compiler_params=pltpu.CompilerParams(vmem_limit_bytes=WHOLE_VMEM_BYTES),
        cost_estimate=SMALL,
        name="decoder_weights",
    )(sines, dec_qkv, dec_out, w_mlp1, w_mlp2, *weights)


def head_span(span, ranks):
    first = span * ranks * HDIM
    start = first // LANES * LANES
    stop = -(-(first + ranks * HDIM) // LANES) * LANES
    return first, start, stop


def project_kernel(span, ranks, with_norm, parts, me_ref, x_ref, gain_ref, w_hbm, *refs):
    inner = HEADS * HDIM
    count = len(parts) * ranks
    outs = refs[:count]
    weights, rows_ref, sems = refs[-3:]
    first, start, stop = head_span(span, ranks)
    width = stop - start
    step = pl.program_id(0)
    copies = [
        pltpu.make_async_copy(
            w_hbm.at[:, pl.ds(part * inner + start, width)],
            weights.at[:, pl.ds(part * width, width)],
            sems.at[part],
        )
        for part in range(3)
    ]

    @pl.when(step == 0)
    def _():
        for copy in copies:
            copy.start()

    if with_norm:
        gain = gain_ref[...].reshape(1, -1)
        normed = layer_norm(x_ref[...].astype(jnp.float32), gain, 1e-06).astype(jnp.bfloat16)
        refs[count][...] = normed
    else:
        normed = x_ref[...]

    @pl.when(step == 0)
    def _():
        for copy in copies:
            copy.wait()

    rows_ref[...] = (
        jnp.dot(normed, weights[...], preferred_element_type=jnp.float32).astype(jnp.bfloat16).T
    )
    for index, wanted in enumerate(parts):
        for shift in range(ranks):
            out = outs[index * ranks + shift]
            head = lax.rem(me_ref[0] + shift, ranks)
            for at, part in enumerate(wanted):
                place = pl.multiple_of(head * HDIM + (part * width + first - start), 16)
                out[at * HDIM : (at + 1) * HDIM, :] = rows_ref[pl.ds(place, HDIM), :]


def project(span, ranks, parts, me, source, ln_gain, w_qkv, with_norm):
    rows, model = source.shape
    block = rows // 2
    _, start, stop = head_span(span, ranks)
    width = stop - start
    sizes = [len(wanted) * HDIM for wanted in parts for _ in range(ranks)]
    out_shape = [jax.ShapeDtypeStruct((size, rows), jnp.bfloat16) for size in sizes]
    out_specs = [pl.BlockSpec((size, block), lambda i: (0, i)) for size in sizes]
    if with_norm:
        out_shape = out_shape + [jax.ShapeDtypeStruct((rows, model), jnp.bfloat16)]
        out_specs = out_specs + [pl.BlockSpec((block, model), lambda i: (i, 0))]
    return pl.pallas_call(
        functools.partial(project_kernel, span, ranks, with_norm, parts),
        grid=(rows // block,),
        in_specs=[
            pl.BlockSpec(memory_space=pltpu.SMEM),
            pl.BlockSpec((block, model), lambda i: (i, 0)),
            pl.BlockSpec((model,), lambda i: (0,)),
            pl.BlockSpec(memory_space=pl.ANY),
        ],
        out_specs=out_specs,
        out_shape=out_shape,
        scratch_shapes=[
            pltpu.VMEM((model, 3 * width), jnp.bfloat16),
            pltpu.VMEM((3 * width, block), jnp.bfloat16),
            pltpu.SemaphoreType.DMA((3,)),
        ],
        compiler_params=pltpu.CompilerParams(
            vmem_limit_bytes=WHOLE_VMEM_BYTES if with_norm else VMEM_BYTES
        ),
        cost_estimate=SMALL,
        name="norm_and_projections" if with_norm else "projections",
    )(me, source, ln_gain, w_qkv)


def attention_kernel(spans, query_block, key_block, sources, ranks, *refs):
    query_refs, kv_refs = refs[:sources], refs[sources : sources + ranks]
    beside, outs = refs[sources + ranks : -4 - sources], refs[-4 - sources : -4]
    queries, keys, values, mixed_out = refs[-4:]
    rows = kv_refs[0].shape[1]
    key_row = kv_refs[0].shape[0] - 2 * HDIM
    total = ranks * rows
    piece = min(query_block, 256)
    per_tile = query_block // piece

    columns = [at for first, stop in spans for at in range(first, stop, piece)]
    places = [
        (source, at, index * piece)
        for source in range(sources)
        for index, at in enumerate(columns)
    ]
    for number, (source, at, _) in enumerate(places):
        tile, inside = number // per_tile, number % per_tile * piece
        queries[tile, :, inside : inside + piece] = query_refs[source][:HDIM, at : at + piece]
    for rank in range(ranks):
        span = slice(rank * rows, (rank + 1) * rows)
        keys[span, :] = kv_refs[rank][key_row : key_row + HDIM, :].T
        values[:HDIM, span] = kv_refs[rank][key_row + HDIM :, :]
    values[HDIM:, :] = jnp.ones((values.shape[0] - HDIM, total), jnp.bfloat16)
    steps = total // key_block

    def one_block(step, carry):
        query = queries[step]

        def scores_of(at):
            return lax.dot_general(
                keys[at * key_block : (at + 1) * key_block, :],
                query,
                (((1,), (0,)), ((), ())),
                preferred_element_type=jnp.float32,
            )

        maxima, mixed = None, None
        upcoming = scores_of(0)
        for at in range(steps):
            scores = upcoming
            if at + 1 < steps:
                upcoming = scores_of(at + 1)
            block_max = jnp.max(scores, axis=0, keepdims=True)
            new_max = block_max if maxima is None else jnp.maximum(maxima, block_max)
            weights = jnp.exp2((scores - new_max) * TO_BASE2).astype(jnp.bfloat16)
            share = jnp.dot(
                values[:, at * key_block : (at + 1) * key_block],
                weights,
                preferred_element_type=jnp.float32,
            )
            if maxima is None:
                mixed = share
            else:
                mixed = mixed * jnp.exp2((maxima - new_max) * TO_BASE2) + share
            maxima = new_max
        mixed_out[step] = (mixed[:HDIM, :] / mixed[HDIM : HDIM + 1, :]).astype(jnp.bfloat16)
        return carry

    if queries.shape[0] <= 2:
        for step in range(queries.shape[0]):
            one_block(step, 0)
    else:
        lax.fori_loop(0, queries.shape[0], one_block, 0)
    base = 0
    if beside:
        base = len(columns) * piece
        for number, (source, at, place) in enumerate(places):
            outs[source][:, place : place + piece] = beside[source][:, at : at + piece]
    for number, (source, _, place) in enumerate(places):
        tile, inside = number // per_tile, number % per_tile * piece
        outs[source][:, base + place : base + place + piece] = mixed_out[
            tile, :, inside : inside + piece
        ]


def attention(queries, key_values, spans, beside=()):
    ranks, rows = len(key_values), key_values[0].shape[1]
    wanted = sum(stop - first for first, stop in spans)
    columns = len(queries) * wanted
    query_block = next(size for size in (1024, 768, 512, 256, columns) if columns % size == 0)
    key_block = min(ranks * rows, 512)
    tiles = columns // query_block
    return list(pl.pallas_call(
        functools.partial(
            attention_kernel, spans, query_block, key_block, len(queries), ranks
        ),
        out_shape=[
            jax.ShapeDtypeStruct((HDIM, 2 * wanted if beside else wanted), jnp.bfloat16)
        ]
        * len(queries),
        scratch_shapes=[
            pltpu.VMEM((tiles, HDIM, query_block), jnp.bfloat16),
            pltpu.VMEM((ranks * rows, HDIM), jnp.bfloat16),
            pltpu.VMEM((HDIM + 16, ranks * rows), jnp.bfloat16),
            pltpu.VMEM((tiles, HDIM, query_block), jnp.bfloat16),
        ],
        compiler_params=params(),
        cost_estimate=SMALL,
        name="head_attention",
    )(*queries, *key_values, *beside))


def neck_kernel(ranks, me_ref, tok_ref, wp_ref, wn_ref, gain_ref, *refs):
    heads = refs[:-2]
    out_ref, joined_ref = refs[-2:]
    for number, part in enumerate(heads):
        span, shift = number // ranks, number % ranks
        head = lax.rem(me_ref[0] + shift, ranks) + span * ranks
        joined_ref[pl.ds(pl.multiple_of(head * HDIM, 16), HDIM), :] = part[...]
    attended = joined_ref[...].T
    block_out = tok_ref[...].astype(jnp.float32) + jnp.dot(
        attended, wp_ref[...], preferred_element_type=jnp.float32
    )
    narrow = jnp.dot(
        block_out.astype(jnp.bfloat16), wn_ref[...], preferred_element_type=jnp.float32
    )
    out_ref[...] = layer_norm(narrow, gain_ref[...].reshape(1, -1), 1e-06).astype(jnp.bfloat16)


def neck(first, step, block, ranks, me, tokens, w_proj, w_neck1, gain, own, returned):
    model = tokens.shape[1]
    own_spec = pl.BlockSpec((HDIM, block), lambda i: (0, first + i * step))
    heads, head_specs = [], []
    for span, mine in enumerate(own):
        heads += [mine] + returned
        head_specs += [own_spec] + [
            pl.BlockSpec((HDIM, block), lambda i, at=2 * span: (0, at + i)) for _ in returned
        ]
    return pl.pallas_call(
        functools.partial(neck_kernel, ranks),
        grid=(2,),
        in_specs=[
            pl.BlockSpec(memory_space=pltpu.SMEM),
            pl.BlockSpec((block, model), lambda i: (first + i * step, 0)),
            pl.BlockSpec(w_proj.shape, lambda i: (0, 0)),
            pl.BlockSpec(w_neck1.shape, lambda i: (0, 0)),
            pl.BlockSpec(gain.shape, lambda i: (0,)),
        ]
        + head_specs,
        out_specs=pl.BlockSpec((block, NECK), lambda i: (i, 0)),
        out_shape=jax.ShapeDtypeStruct((2 * block, NECK), jnp.bfloat16),
        scratch_shapes=[pltpu.VMEM((HEADS * HDIM, block), jnp.bfloat16)],
        compiler_params=params(),
        cost_estimate=SMALL,
        name="proj_and_narrow",
    )(me, tokens, w_proj, w_neck1, gain, *heads)


def embed_kernel(
    prev_ref,
    next_ref,
    edge_ref,
    mid_ref,
    w_ref,
    gain_ref,
    kv_ref,
    code_ref,
    query_ref,
    emb_ref,
    stats_ref,
    cells_ref,
):
    rows = emb_ref.shape[0]
    half = edge_ref.shape[0] // 2
    map_rows = jnp.concatenate(
        [prev_ref[...], edge_ref[:half, :], mid_ref[...], edge_ref[half:, :], next_ref[...]], axis=0
    )
    wide = map_rows.astype(jnp.float32)
    length = wide.shape[0]
    column = lax.rem(lax.broadcasted_iota(jnp.int32, (length, 1), 0), GRID)
    before = jnp.where(column == 0, 0.0, pltpu.roll(wide, 1, 0))
    after = jnp.where(column == GRID - 1, 0.0, pltpu.roll(wide, length - 1, 0))
    cells_ref[:, :NECK] = before.astype(jnp.bfloat16)
    cells_ref[:, NECK : 2 * NECK] = map_rows
    cells_ref[:, 2 * NECK :] = after.astype(jnp.bfloat16)
    total = None
    for row_off in range(3):
        share = jnp.dot(
            cells_ref[row_off * GRID : row_off * GRID + rows, :],
            w_ref[row_off * 3 * NECK : (row_off + 1) * 3 * NECK, :],
            preferred_element_type=jnp.float32,
        )
        total = share if total is None else total + share
    embedding = layer_norm(total, gain_ref[...].reshape(1, -1), 1e-06)
    high, low = split(embedding)
    emb_ref[...] = high

    from_high = jnp.dot(high, kv_ref[...], preferred_element_type=jnp.float32)
    from_low = jnp.dot(low, kv_ref[:, :ATTN_DIM], preferred_element_type=jnp.float32)
    dec_keys = from_high[:, :ATTN_DIM] + from_high[:, 2 * ATTN_DIM :] + from_low + code_ref[...]
    dec_values = from_high[:, ATTN_DIM : 2 * ATTN_DIM].astype(jnp.bfloat16)
    head_size = ATTN_DIM // DEC_HEADS
    key_high, key_low = split(dec_keys)
    query_high, query_low = split(query_ref[...])
    across = (((1,), (1,)), ((), ()))
    scores = (
        lax.dot_general(query_high, key_high, across, preferred_element_type=jnp.float32)
        + lax.dot_general(query_low, key_high, across, preferred_element_type=jnp.float32)
        + lax.dot_general(query_high, key_low, across, preferred_element_type=jnp.float32)
    )
    scores = scores * (1.0 / math.sqrt(head_size))
    maxima = jnp.max(scores, axis=1, keepdims=True)
    weights = jnp.exp(scores - maxima)
    totals = jnp.sum(weights, axis=1, keepdims=True)
    mixed = jnp.dot(weights.astype(jnp.bfloat16), dec_values, preferred_element_type=jnp.float32)
    number = stats_ref.shape[0] // 3
    lane_head = lax.broadcasted_iota(jnp.int32, (1, ATTN_DIM), 1) // head_size
    for at, stat in enumerate((mixed, maxima, totals)):
        picked = jnp.zeros((number, ATTN_DIM), jnp.float32)
        for head in range(DEC_HEADS):
            picked = jnp.where(
                lane_head == head, stat[head * number : (head + 1) * number, :], picked
            )
        stats_ref[at * number : (at + 1) * number, :] = picked


def embed(prev, following, edge, mid, w_neck2, gain, key_value, code_keys, spread_queries):
    rows = edge.shape[0] + mid.shape[0]
    number = spread_queries.shape[0] // DEC_HEADS
    length = rows + prev.shape[0] + following.shape[0]
    return pl.pallas_call(
        embed_kernel,
        out_shape=[
            jax.ShapeDtypeStruct((rows, NECK), jnp.bfloat16),
            jax.ShapeDtypeStruct((3 * number, ATTN_DIM), jnp.float32),
        ],
        scratch_shapes=[pltpu.VMEM((length, 3 * NECK), jnp.bfloat16)],
        compiler_params=params(),
        cost_estimate=SMALL,
        name="embedding_and_statistics",
    )(prev, following, edge, mid, w_neck2, gain, key_value, code_keys, spread_queries)


def upscale_kernel(emb_ref, weights_ref, gain_ref, out_ref):
    first_out = lax.dot_general(
        weights_ref[:NECK, :],
        emb_ref[...],
        (((0,), (1,)), ((), ())),
        preferred_element_type=jnp.float32,
    )
    for corner in range(4):
        part = layer_norm(
            first_out[corner * UP1 : (corner + 1) * UP1, :], gain_ref[...], 1e-06, axis=0
        )
        second = lax.dot_general(
            weights_ref[NECK:, : 4 * UP2],
            gelu(part).astype(jnp.bfloat16),
            (((0,), (0,)), ((), ())),
            preferred_element_type=jnp.float32,
        )
        out_ref[corner * 4 * UP2 : (corner + 1) * 4 * UP2, :] = gelu(second).astype(jnp.bfloat16)


def upscale(embedding, weights, up_gain):
    rows = embedding.shape[0]
    return pl.pallas_call(
        upscale_kernel,
        out_shape=jax.ShapeDtypeStruct((OFFSETS * UP2, rows), jnp.bfloat16),
        compiler_params=params(),
        cost_estimate=SMALL,
        name="upscaled_channels",
    )(embedding, weights, up_gain)


def masks_kernel(ranks, owners, *refs):
    stats = refs[:ranks]
    tok_ref, gains_ref, weights_ref, up_ref, out_ref = refs[ranks:]
    number = tok_ref.shape[0]
    maxima = stats[0][number : 2 * number, :]
    for part in stats[1:]:
        maxima = jnp.maximum(maxima, part[number : 2 * number, :])
    mixed, totals = 0.0, 0.0
    for part in stats:
        scale = jnp.exp(part[number : 2 * number, :] - maxima)
        mixed = mixed + part[:number, :] * scale
        totals = totals + part[2 * number :, :] * scale
    cross = mixed / totals
    top = weights_ref.shape[0] - ATTN_DIM
    wide = (top - 3 * NECK) // 2
    wh_at = 2 * wide
    first_out = layer_norm(
        tok_ref[...] + split_dot(cross, weights_ref[top:, :]), gains_ref[0:1, :], 1e-05
    )
    halves = jnp.concatenate(split(first_out))
    mixed = 0.0
    for block in range(0, wide, NECK):
        hidden = jnp.dot(
            halves, weights_ref[block : block + NECK, :], preferred_element_type=jnp.float32
        )
        hidden = jnp.maximum(hidden[:number] + hidden[number:], 0.0)
        mixed = mixed + split_dot(hidden, weights_ref[wide + block : wide + block + NECK, :])
    second = layer_norm(first_out + mixed, gains_ref[1:2, :], 1e-05)
    hyper_vec = jnp.maximum(split_dot(second, weights_ref[wh_at : wh_at + NECK, :]), 0.0)
    wh_at += NECK
    hyper_vec = jnp.maximum(split_dot(hyper_vec, weights_ref[wh_at : wh_at + NECK, :]), 0.0)
    wh_at += NECK
    hyper_vec = split_dot(hyper_vec, weights_ref[wh_at : wh_at + NECK, :UP2])
    hyper_vec = hyper_vec.astype(jnp.bfloat16)

    depth = OFFSETS * UP2
    span = OFFSETS * CAP
    channel = lax.broadcasted_iota(jnp.int32, (UP2, depth), 0)
    lane = lax.broadcasted_iota(jnp.int32, (UP2, depth), 1)
    repeat = jnp.where(lax.rem(lane, UP2) == channel, 1.0, 0.0).astype(jnp.bfloat16)
    tiled = jnp.dot(hyper_vec, repeat, preferred_element_type=jnp.float32).astype(jnp.bfloat16)
    row = lax.broadcasted_iota(jnp.int32, (owners * span, number), 0)
    slot = lax.broadcasted_iota(jnp.int32, (owners * span, number), 1)
    chosen = (row // span) * CAP + lax.rem(row, CAP)
    choose = jnp.where(chosen == slot, 1.0, 0.0).astype(jnp.bfloat16)
    spread = jnp.dot(choose, tiled, preferred_element_type=jnp.float32)
    row = lax.broadcasted_iota(jnp.int32, spread.shape, 0)
    lane = lax.broadcasted_iota(jnp.int32, spread.shape, 1)
    same = lax.rem(row, span) // CAP == lane // UP2
    spread = jnp.where(same, spread, 0.0).astype(jnp.bfloat16)
    for owner in range(owners):
        out_ref[owner] = jnp.dot(
            spread[owner * span : (owner + 1) * span, :],
            up_ref[...],
            preferred_element_type=jnp.float32,
        ).astype(jnp.bfloat16)


def mask_logits(stats, query_tok, owners, gains, weights, upscaled):
    cells = upscaled.shape[1]
    return pl.pallas_call(
        functools.partial(masks_kernel, len(stats), owners),
        out_shape=jax.ShapeDtypeStruct((owners, OFFSETS * CAP, cells), jnp.bfloat16),
        compiler_params=params(),
        cost_estimate=SMALL,
        name="token_side_and_masks",
    )(*stats, query_tok, gains, weights, upscaled)


def place_kernel(slots, recv_ref, choose_ref, order_ref, out_ref, tiles_ref):
    cells = recv_ref.shape[1]
    pairs = cells // LANES
    rows = jnp.dot(choose_ref[...], recv_ref[...], preferred_element_type=jnp.float32)
    rows = rows.astype(jnp.bfloat16)
    for top in range(2):
        for low in range(2):
            for pair in range(pairs):
                at = ((top * 2 + low) * pairs + pair) * slots
                for left in range(2):
                    for right in range(2):
                        offset = ((top * 2 + left) * 2 + low) * 2 + right
                        corner = left * 2 + right
                        tiles_ref[at : at + slots, corner * LANES : (corner + 1) * LANES] = rows[
                            offset * slots : (offset + 1) * slots,
                            pair * LANES : (pair + 1) * LANES,
                        ]
    ordered = jnp.dot(tiles_ref[...], order_ref[...], preferred_element_type=jnp.float32)
    width = 4 * GRID
    for top in range(2):
        for low in range(2):
            for pair in range(pairs):
                at = ((top * 2 + low) * pairs + pair) * slots
                for odd in range(2):
                    line = (2 * pair + odd) * 4 + top * 2 + low
                    out_ref[:, line * width : (line + 1) * width] = ordered[
                        at : at + slots, odd * width : (odd + 1) * width
                    ]


def place_rows(received, choose, order, slots):
    cells = received.shape[1]
    return pl.pallas_call(
        functools.partial(place_kernel, slots),
        out_shape=jax.ShapeDtypeStruct((slots, OFFSETS * cells), jnp.float32),
        scratch_shapes=[pltpu.VMEM((4 * (cells // LANES) * slots, 4 * LANES), jnp.bfloat16)],
        compiler_params=params(),
        cost_estimate=SMALL,
        name="rows_in_pixel_order",
    )(received, choose, order)


def pixel_order():
    source = np.arange(4 * LANES)
    corner, odd, column = source // LANES, source // GRID % 2, source % GRID
    target = odd * 4 * GRID + column * 4 + corner
    matrix = np.zeros((4 * LANES, 4 * LANES), np.float32)
    matrix[source, target] = 1.0
    return jnp.asarray(matrix, jnp.bfloat16)


def after(value, done):
    return lax.optimization_barrier((value, done))[0]


def shifted(block, shift, ranks):
    return lax.ppermute(block, "tok", [(i, (i + shift) % ranks) for i in range(ranks)])


def exchanged(blocks, back=False):
    ranks = len(blocks)
    return [blocks[0]] + [
        shifted(blocks[shift], ranks - shift if back else shift, ranks)
        for shift in range(1, ranks)
    ]


def gathered(block, axis):
    count = lax.axis_size(axis)
    if count & (count - 1):
        return lax.all_gather(block, axis, axis=0, tiled=True)
    place = lax.axis_index(axis)
    reach = 1
    while reach < count:
        other = lax.ppermute(block, axis, [(i, i ^ reach) for i in range(count)])
        low = (place & reach) == 0
        block = jnp.concatenate([jnp.where(low, block, other), jnp.where(low, other, block)])
        reach *= 2
    return block


def body(
    tokens,
    ln_gain,
    w_qkv,
    w_proj,
    w_neck1,
    neck_gain1,
    w_neck2,
    neck_gain2,
    pe_matrix,
    query_bias,
    dec_qkv,
    dec_out,
    dec_gains,
    w_mlp1,
    w_mlp2,
    w_hyper,
    w_hyper_out,
    w_up1,
    up_gain,
    w_up2,
    req_image,
    points,
):
    picture = tokens[0]
    tok_rows = picture.shape[0]
    grid_rows = tok_rows // GRID
    ranks = lax.axis_size("tok")
    owners = lax.axis_size("img")
    rank = lax.axis_index("tok")
    me = rank.astype(jnp.int32).reshape(1)
    edge = tok_rows // 4
    all_spans = ((0, tok_rows),)
    edge_spans = ((0, edge), (tok_rows - edge, tok_rows))
    mid_spans = ((edge, tok_rows - edge),)
    *first_out, normed = project(
        0, ranks, ((0, 1, 2),), me, picture, ln_gain, w_qkv, with_norm=True
    )
    first_in = exchanged(first_out)
    second_out = project(1, ranks, ((0,), (1, 2)), me, normed, ln_gain, w_qkv, with_norm=False)
    query_out, kv_out = second_out[:ranks], second_out[ranks:]

    targets, spots, pe_late = after((req_image[:, 0], points, pe_matrix), normed)
    slots = targets.shape[0]
    asked = jnp.concatenate([targets[:, None], spots], axis=1)
    everyone = gathered(asked[None], "img")
    here = (everyone[:, :, 0] == lax.axis_index("img")).astype(jnp.int32)
    turn = jnp.cumsum(here, axis=1) - here
    filling = here[:, :, None] * (turn[:, :, None] == jnp.arange(CAP)[None, None, :])
    arrived = jnp.sum(filling[:, :, :, None] * everyone[:, :, None, 1:], axis=1)
    matches = (targets[:, None] == jnp.arange(owners, dtype=jnp.int32)[None, :]).astype(jnp.int32)
    order_no = jnp.sum((jnp.cumsum(matches, axis=0) - matches) * matches, axis=1)
    places = targets * CAP + order_no
    placing = places[:, None] == jnp.arange(owners * CAP, dtype=jnp.int32)[None, :]
    number = owners * CAP
    flattened = arrived.reshape(number, 2).astype(jnp.float32)
    query_tok = query_bias + fourier((flattened + 0.5) / IMG_SIDE * 2.0 - 1.0, pe_late)
    query_matrix = jnp.dot(query_tok, dec_qkv[0], precision=highest_precision)
    head_size = ATTN_DIM // DEC_HEADS
    head_mask = (
        jnp.arange(DEC_HEADS)[:, None] == jnp.arange(ATTN_DIM)[None, :] // head_size
    ).astype(jnp.float32)
    spread_queries = (head_mask[:, None, :] * query_matrix[None, :, :]).reshape(
        DEC_HEADS * number, ATTN_DIM
    )
    offset_eye = jnp.eye(OFFSETS, dtype=jnp.bfloat16)
    choose = (
        offset_eye[:, None, None, :, None]
        * placing.astype(jnp.bfloat16).reshape(1, slots, owners, 1, CAP)
    ).reshape(OFFSETS * slots, owners * OFFSETS * CAP)
    order = pixel_order()

    kv_in = exchanged(after(kv_out, first_in[1:]))
    sines, decoder = after(
        (
            grid_sines(rank * grid_rows, grid_rows, pe_late),
            (dec_qkv, dec_out, w_mlp1, w_mlp2, w_hyper, w_hyper_out, w_up1, w_up2),
        ),
        normed,
    )
    prepared = prepare(sines, *decoder)
    up_column = after(up_gain, normed).reshape(-1, 1)
    first_in, prepared, spread_queries, query_tok, up_column = lax.optimization_barrier(
        (first_in, prepared, spread_queries, query_tok, up_column)
    )
    token_weights, up_weights, key_value, code_keys = prepared
    first_mixed = attention(first_in, first_in, all_spans)
    query_in = exchanged(after(query_out, (kv_in[1:], first_mixed)))
    own_mixed = attention(after(query_out[:1], first_mixed), kv_in, all_spans)
    edge_mixed = attention(
        after(query_in[1:], own_mixed), kv_in, edge_spans, beside=first_mixed[1:]
    )
    edge_heads = exchanged(own_mixed + edge_mixed, back=True)[1:]
    mid_mixed = attention(
        after(query_in[1:], edge_mixed), kv_in, mid_spans, beside=first_mixed[1:]
    )
    mid_heads = exchanged(own_mixed + mid_mixed, back=True)[1:]
    own = first_mixed[:1] + own_mixed
    neck_args = (edge, ranks, me, picture, w_proj, w_neck1, neck_gain1, own)
    edge_narrow = neck(0, 3, *neck_args, edge_heads)
    ends = ranks - 1
    prev = lax.ppermute(edge_narrow[-GRID:], "tok", [(i, i + 1) for i in range(ends)])
    following = lax.ppermute(edge_narrow[:GRID], "tok", [(i + 1, i) for i in range(ends)])
    mid_narrow = neck(1, 1, *neck_args, mid_heads)

    embedding, stats = embed(
        prev,
        following,
        edge_narrow,
        mid_narrow,
        w_neck2,
        neck_gain2,
        key_value,
        code_keys,
        spread_queries,
    )
    all_stats = exchanged([stats] * ranks)
    upscaled = upscale(embedding, up_weights, up_column)
    outgoing = mask_logits(
        all_stats,
        query_tok,
        owners,
        dec_gains,
        token_weights,
        upscaled,
    )
    answer = lax.all_to_all(outgoing, "img", split_axis=0, concat_axis=0, tiled=True)
    return place_rows(answer.reshape(number * OFFSETS, tok_rows), choose, order, slots)


def solution(mesh):
    placed = (
        (P("img", "tok", None),) + (P(),) * 19 + (P("img", None),) * 2
    )
    return jax.shard_map(
        body, mesh=mesh, in_specs=placed, out_specs=P("img", "tok"), check_vma=False
    )
```

```python
import functools
import math

import jax
import jax.numpy as jnp
import numpy as np
from jax import lax
from jax.experimental import pallas as pl
from jax.experimental.pallas import tpu as pltpu
from jax.sharding import PartitionSpec as P

HEADS = 8
HDIM = 80
GRID = 64
NECK = 256
ATTN_DIM = 128
DEC_HEADS = 8
UP1 = 64
UP2 = 32
IMG_SIDE = 1024
CAP = 4
LANES = 128
OFFSETS = 16
VMEM_BYTES = 24 << 20
WHOLE_VMEM_BYTES = 56 << 20

highest_precision = lax.Precision.HIGHEST
SMALL = pl.CostEstimate(flops=1 << 10, bytes_accessed=1 << 10, transcendentals=0)
TO_BASE2 = math.log2(math.e) / math.sqrt(HDIM)


def layer_norm(tensor, gain_vec, epsilon, axis=-1):
    average = jnp.mean(tensor, axis=axis, keepdims=True)
    centred = tensor - average
    spread = jnp.mean(centred * centred, axis=axis, keepdims=True)
    return centred * lax.rsqrt(spread + epsilon) * gain_vec


def gelu(tensor):
    return 0.5 * tensor * (1.0 + lax.erf(tensor * math.sqrt(0.5)))


def fourier(coords, pe_matrix):
    angles = 2.0 * math.pi * jnp.dot(coords, pe_matrix, precision=highest_precision)
    return jnp.concatenate([jnp.sin(angles), jnp.cos(angles)], axis=-1)


def grid_sines(first_row, grid_rows, pe_matrix):
    row_ids = (first_row + jnp.arange(grid_rows, dtype=jnp.int32)).astype(jnp.float32)
    col_ids = jnp.arange(GRID, dtype=jnp.int32).astype(jnp.float32)
    ycoord = (row_ids + 0.5) / GRID * 2.0 - 1.0
    xcoord = (col_ids + 0.5) / GRID * 2.0 - 1.0
    angles = jnp.concatenate([xcoord[:, None] * pe_matrix[0], ycoord[:, None] * pe_matrix[1]])
    angles = 2.0 * math.pi * angles
    return jnp.concatenate([jnp.sin(angles), jnp.cos(angles)], axis=1)


def params(**extra):
    return pltpu.CompilerParams(vmem_limit_bytes=VMEM_BYTES, **extra)


def split(tensor):
    high = tensor.astype(jnp.bfloat16)
    return high, (tensor - high.astype(jnp.float32)).astype(jnp.bfloat16)


def split_dot(left, right):
    rows = left.shape[0]
    both = jnp.dot(jnp.concatenate(split(left)), right, preferred_element_type=jnp.float32)
    return both[:rows] + both[rows:]


def prepare_kernel(
    sines_ref,
    qkv_ref,
    wo_ref,
    w1_ref,
    w2_ref,
    wh_ref,
    who_ref,
    up1_ref,
    up2_ref,
    token_ref,
    up_ref,
    key_value_ref,
    code_ref,
    codes_ref,
):
    hidden = w1_ref.shape[1]
    for block in range(hidden // NECK):
        columns = slice(block * NECK, (block + 1) * NECK)
        token_ref[columns, :] = w1_ref[:, columns].astype(jnp.bfloat16)
    token_ref[hidden : 2 * hidden, :] = w2_ref[...].astype(jnp.bfloat16)
    at = 2 * hidden
    for layer in range(2):
        token_ref[at : at + NECK, :] = wh_ref[layer].astype(jnp.bfloat16)
        at += NECK
    token_ref[at : at + NECK, :UP2] = who_ref[...].astype(jnp.bfloat16)
    at += NECK
    token_ref[at:, :] = wo_ref[...].astype(jnp.bfloat16)
    up_ref[:NECK, :] = up1_ref[...].astype(jnp.bfloat16)
    up_ref[NECK:, : 4 * UP2] = up2_ref[...].astype(jnp.bfloat16)
    key_high, key_low = split(qkv_ref[1])
    key_value_ref[:, :ATTN_DIM] = key_high
    key_value_ref[:, ATTN_DIM : 2 * ATTN_DIM] = qkv_ref[2].astype(jnp.bfloat16)
    key_value_ref[:, 2 * ATTN_DIM :] = key_low
    half = sines_ref.shape[1] // 2
    sin_x, cos_x = sines_ref[:GRID, :half], sines_ref[:GRID, half:]
    for row in range(sines_ref.shape[0] - GRID):
        sin_y = sines_ref[GRID + row : GRID + row + 1, :half]
        cos_y = sines_ref[GRID + row : GRID + row + 1, half:]
        at = row * GRID
        codes_ref[at : at + GRID, :half] = sin_x * cos_y + cos_x * sin_y
        codes_ref[at : at + GRID, half:] = cos_x * cos_y - sin_x * sin_y
    code_high, code_low = split(codes_ref[...])
    code_ref[...] = (
        jnp.dot(code_high, key_high, preferred_element_type=jnp.float32)
        + jnp.dot(code_low, key_high, preferred_element_type=jnp.float32)
        + jnp.dot(code_high, key_low, preferred_element_type=jnp.float32)
    )


def prepare(sines, dec_qkv, dec_out, w_mlp1, w_mlp2, *weights):
    cells = (sines.shape[0] - GRID) * GRID
    rows = 2 * w_mlp1.shape[1] + 3 * NECK + ATTN_DIM
    return pl.pallas_call(
        prepare_kernel,
        out_shape=[
            jax.ShapeDtypeStruct((rows, NECK), jnp.bfloat16),
            jax.ShapeDtypeStruct((NECK + UP1, NECK), jnp.bfloat16),
            jax.ShapeDtypeStruct((NECK, 3 * ATTN_DIM), jnp.bfloat16),
            jax.ShapeDtypeStruct((cells, ATTN_DIM), jnp.float32),
        ],
        scratch_shapes=[pltpu.VMEM((cells, NECK), jnp.float32)],
        compiler_params=pltpu.CompilerParams(vmem_limit_bytes=WHOLE_VMEM_BYTES),
        cost_estimate=SMALL,
        name="decoder_weights",
    )(sines, dec_qkv, dec_out, w_mlp1, w_mlp2, *weights)


def head_span(span, ranks):
    first = span * ranks * HDIM
    start = first // LANES * LANES
    stop = -(-(first + ranks * HDIM) // LANES) * LANES
    return first, start, stop


def project_kernel(span, ranks, parts, me_ref, x_ref, gain_ref, w_hbm, *refs):
    inner = HEADS * HDIM
    count = len(parts) * ranks
    outs = refs[:count]
    weights, rows_ref, sems = refs[-3:]
    first, start, stop = head_span(span, ranks)
    width = stop - start
    step = pl.program_id(0)
    copies = [
        pltpu.make_async_copy(
            w_hbm.at[:, pl.ds(part * inner + start, width)],
            weights.at[:, pl.ds(part * width, width)],
            sems.at[part],
        )
        for part in range(3)
    ]

    @pl.when(step == 0)
    def _():
        for copy in copies:
            copy.start()

    gain = gain_ref[...].reshape(1, -1)
    normed = layer_norm(x_ref[...].astype(jnp.float32), gain, 1e-06).astype(jnp.bfloat16)

    @pl.when(step == 0)
    def _():
        for copy in copies:
            copy.wait()

    rows_ref[...] = (
        jnp.dot(normed, weights[...], preferred_element_type=jnp.float32).astype(jnp.bfloat16).T
    )
    for index, wanted in enumerate(parts):
        for shift in range(ranks):
            out = outs[index * ranks + shift]
            columns = slice(None)
            if out.shape[1] < rows_ref.shape[1]:
                quarter = step if index == 0 else 1 - step
                columns = pl.ds(pl.multiple_of(quarter * out.shape[1], LANES), out.shape[1])
            head = lax.rem(me_ref[0] + shift, ranks)
            for at, part in enumerate(wanted):
                place = pl.multiple_of(head * HDIM + (part * width + first - start), 16)
                out[at * HDIM : (at + 1) * HDIM, :] = rows_ref[pl.ds(place, HDIM), columns]


def project(span, ranks, parts, me, source, ln_gain, w_qkv):
    rows, model = source.shape
    block = rows // 2
    _, start, stop = head_span(span, ranks)
    width = stop - start
    sizes = [
        (len(wanted) * HDIM, block // parts.count(wanted))
        for wanted in parts
        for _ in range(ranks)
    ]
    out_shape = [jax.ShapeDtypeStruct((high, 2 * wide), jnp.bfloat16) for high, wide in sizes]
    out_specs = [pl.BlockSpec(size, lambda i: (0, i)) for size in sizes]
    return pl.pallas_call(
        functools.partial(project_kernel, span, ranks, parts),
        grid=(rows // block,),
        in_specs=[
            pl.BlockSpec(memory_space=pltpu.SMEM),
            pl.BlockSpec((block, model), lambda i: (i, 0)),
            pl.BlockSpec((model,), lambda i: (0,)),
            pl.BlockSpec(memory_space=pl.ANY),
        ],
        out_specs=out_specs,
        out_shape=out_shape,
        scratch_shapes=[
            pltpu.VMEM((model, 3 * width), jnp.bfloat16),
            pltpu.VMEM((3 * width, block), jnp.bfloat16),
            pltpu.SemaphoreType.DMA((3,)),
        ],
        compiler_params=pltpu.CompilerParams(
            vmem_limit_bytes=VMEM_BYTES if span else WHOLE_VMEM_BYTES
        ),
        cost_estimate=SMALL,
        name="norm_and_projections",
    )(me, source, ln_gain, w_qkv)


def attention_kernel(spans, query_block, key_block, sources, ranks, *refs):
    query_refs, kv_refs = refs[:sources], refs[sources : sources + ranks]
    beside, outs = refs[sources + ranks : -4 - sources], refs[-4 - sources : -4]
    queries, keys, values, mixed_out = refs[-4:]
    rows = kv_refs[0].shape[1]
    key_row = kv_refs[0].shape[0] - 2 * HDIM
    total = ranks * rows
    piece = min(query_block, 256)
    per_tile = query_block // piece

    columns = [at for first, stop in spans for at in range(first, stop, piece)]
    places = [
        (source, at, index * piece)
        for source in range(sources)
        for index, at in enumerate(columns)
    ]
    for number, (source, _, at) in enumerate(places):
        tile, inside = number // per_tile, number % per_tile * piece
        queries[tile, :, inside : inside + piece] = query_refs[source][:HDIM, at : at + piece]
    for rank in range(ranks):
        span = slice(rank * rows, (rank + 1) * rows)
        keys[span, :] = kv_refs[rank][key_row : key_row + HDIM, :].T
        values[:HDIM, span] = kv_refs[rank][key_row + HDIM :, :]
    values[HDIM:, :] = jnp.ones((values.shape[0] - HDIM, total), jnp.bfloat16)
    steps = total // key_block

    def one_block(step, carry):
        query = queries[step]

        def scores_of(at):
            return lax.dot_general(
                keys[at * key_block : (at + 1) * key_block, :],
                query,
                (((1,), (0,)), ((), ())),
                preferred_element_type=jnp.float32,
            )

        maxima, mixed = None, None
        upcoming = scores_of(0)
        for at in range(steps):
            scores = upcoming
            if at + 1 < steps:
                upcoming = scores_of(at + 1)
            block_max = jnp.max(scores, axis=0, keepdims=True)
            new_max = block_max if maxima is None else jnp.maximum(maxima, block_max)
            weights = jnp.exp2((scores - new_max) * TO_BASE2).astype(jnp.bfloat16)
            share = jnp.dot(
                values[:, at * key_block : (at + 1) * key_block],
                weights,
                preferred_element_type=jnp.float32,
            )
            if maxima is None:
                mixed = share
            else:
                mixed = mixed * jnp.exp2((maxima - new_max) * TO_BASE2) + share
            maxima = new_max
        mixed_out[step] = (mixed[:HDIM, :] / mixed[HDIM : HDIM + 1, :]).astype(jnp.bfloat16)
        return carry

    if queries.shape[0] <= 2:
        for step in range(queries.shape[0]):
            one_block(step, 0)
    else:
        lax.fori_loop(0, queries.shape[0], one_block, 0)
    base = 0
    if beside:
        base = len(columns) * piece
        for number, (source, at, place) in enumerate(places):
            outs[source][:, place : place + piece] = beside[source][:, at : at + piece]
    for number, (source, _, place) in enumerate(places):
        tile, inside = number // per_tile, number % per_tile * piece
        outs[source][:, base + place : base + place + piece] = mixed_out[
            tile, :, inside : inside + piece
        ]


def attention(queries, key_values, spans, beside=()):
    ranks, rows = len(key_values), key_values[0].shape[1]
    wanted = sum(stop - first for first, stop in spans)
    columns = len(queries) * wanted
    query_block = next(size for size in (1024, 768, 512, 256, columns) if columns % size == 0)
    key_block = min(ranks * rows, 512)
    tiles = columns // query_block
    return list(pl.pallas_call(
        functools.partial(
            attention_kernel, spans, query_block, key_block, len(queries), ranks
        ),
        out_shape=[
            jax.ShapeDtypeStruct((HDIM, 2 * wanted if beside else wanted), jnp.bfloat16)
        ]
        * len(queries),
        scratch_shapes=[
            pltpu.VMEM((tiles, HDIM, query_block), jnp.bfloat16),
            pltpu.VMEM((ranks * rows, HDIM), jnp.bfloat16),
            pltpu.VMEM((HDIM + 16, ranks * rows), jnp.bfloat16),
            pltpu.VMEM((tiles, HDIM, query_block), jnp.bfloat16),
        ],
        compiler_params=params(),
        cost_estimate=SMALL,
        name="head_attention",
    )(*queries, *key_values, *beside))


def neck_kernel(ranks, me_ref, tok_ref, wp_ref, wn_ref, gain_ref, *refs):
    heads = refs[:-2]
    out_ref, joined_ref = refs[-2:]
    for number, part in enumerate(heads):
        span, shift = number // ranks, number % ranks
        head = lax.rem(me_ref[0] + shift, ranks) + span * ranks
        joined_ref[pl.ds(pl.multiple_of(head * HDIM, 16), HDIM), :] = part[...]
    attended = joined_ref[...].T
    block_out = tok_ref[...].astype(jnp.float32) + jnp.dot(
        attended, wp_ref[...], preferred_element_type=jnp.float32
    )
    narrow = jnp.dot(
        block_out.astype(jnp.bfloat16), wn_ref[...], preferred_element_type=jnp.float32
    )
    out_ref[...] = layer_norm(narrow, gain_ref[...].reshape(1, -1), 1e-06).astype(jnp.bfloat16)


def neck(first, step, block, ranks, me, tokens, w_proj, w_neck1, gain, own, returned):
    model = tokens.shape[1]
    own_specs = [
        pl.BlockSpec((HDIM, block), lambda i: (0, first + i * step)),
        pl.BlockSpec((HDIM, block), lambda i: (0, i)),
    ]
    heads, head_specs = [], []
    for span, mine in enumerate(own):
        heads += [mine] + returned
        head_specs += [own_specs[span]] + [
            pl.BlockSpec((HDIM, block), lambda i, at=2 * span: (0, at + i)) for _ in returned
        ]
    return pl.pallas_call(
        functools.partial(neck_kernel, ranks),
        grid=(2,),
        in_specs=[
            pl.BlockSpec(memory_space=pltpu.SMEM),
            pl.BlockSpec((block, model), lambda i: (first + i * step, 0)),
            pl.BlockSpec(w_proj.shape, lambda i: (0, 0)),
            pl.BlockSpec(w_neck1.shape, lambda i: (0, 0)),
            pl.BlockSpec(gain.shape, lambda i: (0,)),
        ]
        + head_specs,
        out_specs=pl.BlockSpec((block, NECK), lambda i: (i, 0)),
        out_shape=jax.ShapeDtypeStruct((2 * block, NECK), jnp.bfloat16),
        scratch_shapes=[pltpu.VMEM((HEADS * HDIM, block), jnp.bfloat16)],
        compiler_params=params(),
        cost_estimate=SMALL,
        name="proj_and_narrow",
    )(me, tokens, w_proj, w_neck1, gain, *heads)


def embed_kernel(
    prev_ref,
    next_ref,
    edge_ref,
    mid_ref,
    w_ref,
    gain_ref,
    kv_ref,
    code_ref,
    query_ref,
    emb_ref,
    stats_ref,
    cells_ref,
):
    rows = emb_ref.shape[0]
    half = edge_ref.shape[0] // 2
    map_rows = jnp.concatenate(
        [prev_ref[...], edge_ref[:half, :], mid_ref[...], edge_ref[half:, :], next_ref[...]], axis=0
    )
    wide = map_rows.astype(jnp.float32)
    length = wide.shape[0]
    column = lax.rem(lax.broadcasted_iota(jnp.int32, (length, 1), 0), GRID)
    before = jnp.where(column == 0, 0.0, pltpu.roll(wide, 1, 0))
    after = jnp.where(column == GRID - 1, 0.0, pltpu.roll(wide, length - 1, 0))
    cells_ref[:, :NECK] = before.astype(jnp.bfloat16)
    cells_ref[:, NECK : 2 * NECK] = map_rows
    cells_ref[:, 2 * NECK :] = after.astype(jnp.bfloat16)
    total = None
    for row_off in range(3):
        share = jnp.dot(
            cells_ref[row_off * GRID : row_off * GRID + rows, :],
            w_ref[row_off * 3 * NECK : (row_off + 1) * 3 * NECK, :],
            preferred_element_type=jnp.float32,
        )
        total = share if total is None else total + share
    embedding = layer_norm(total, gain_ref[...].reshape(1, -1), 1e-06)
    high, low = split(embedding)
    emb_ref[...] = high

    from_high = jnp.dot(high, kv_ref[...], preferred_element_type=jnp.float32)
    from_low = jnp.dot(low, kv_ref[:, :ATTN_DIM], preferred_element_type=jnp.float32)
    dec_keys = from_high[:, :ATTN_DIM] + from_high[:, 2 * ATTN_DIM :] + from_low + code_ref[...]
    dec_values = from_high[:, ATTN_DIM : 2 * ATTN_DIM].astype(jnp.bfloat16)
    head_size = ATTN_DIM // DEC_HEADS
    key_high, key_low = split(dec_keys)
    query_high, query_low = split(query_ref[...])
    across = (((1,), (1,)), ((), ()))
    scores = (
        lax.dot_general(query_high, key_high, across, preferred_element_type=jnp.float32)
        + lax.dot_general(query_low, key_high, across, preferred_element_type=jnp.float32)
        + lax.dot_general(query_high, key_low, across, preferred_element_type=jnp.float32)
    )
    scores = scores * (1.0 / math.sqrt(head_size))
    maxima = jnp.max(scores, axis=1, keepdims=True)
    weights = jnp.exp(scores - maxima)
    totals = jnp.sum(weights, axis=1, keepdims=True)
    mixed = jnp.dot(weights.astype(jnp.bfloat16), dec_values, preferred_element_type=jnp.float32)
    number = stats_ref.shape[0] // 3
    lane_head = lax.broadcasted_iota(jnp.int32, (1, ATTN_DIM), 1) // head_size
    for at, stat in enumerate((mixed, maxima, totals)):
        picked = jnp.zeros((number, ATTN_DIM), jnp.float32)
        for head in range(DEC_HEADS):
            picked = jnp.where(
                lane_head == head, stat[head * number : (head + 1) * number, :], picked
            )
        stats_ref[at * number : (at + 1) * number, :] = picked


def embed(prev, following, edge, mid, w_neck2, gain, key_value, code_keys, spread_queries):
    rows = edge.shape[0] + mid.shape[0]
    number = spread_queries.shape[0] // DEC_HEADS
    length = rows + prev.shape[0] + following.shape[0]
    return pl.pallas_call(
        embed_kernel,
        out_shape=[
            jax.ShapeDtypeStruct((rows, NECK), jnp.bfloat16),
            jax.ShapeDtypeStruct((3 * number, ATTN_DIM), jnp.float32),
        ],
        scratch_shapes=[pltpu.VMEM((length, 3 * NECK), jnp.bfloat16)],
        compiler_params=params(),
        cost_estimate=SMALL,
        name="embedding_and_statistics",
    )(prev, following, edge, mid, w_neck2, gain, key_value, code_keys, spread_queries)


def upscale_kernel(emb_ref, weights_ref, gain_ref, out_ref):
    first_out = lax.dot_general(
        weights_ref[:NECK, :],
        emb_ref[...],
        (((0,), (1,)), ((), ())),
        preferred_element_type=jnp.float32,
    )
    for corner in range(4):
        part = layer_norm(
            first_out[corner * UP1 : (corner + 1) * UP1, :], gain_ref[...], 1e-06, axis=0
        )
        second = lax.dot_general(
            weights_ref[NECK:, : 4 * UP2],
            gelu(part).astype(jnp.bfloat16),
            (((0,), (0,)), ((), ())),
            preferred_element_type=jnp.float32,
        )
        out_ref[corner * 4 * UP2 : (corner + 1) * 4 * UP2, :] = gelu(second).astype(jnp.bfloat16)


def upscale(embedding, weights, up_gain):
    rows = embedding.shape[0]
    return pl.pallas_call(
        upscale_kernel,
        out_shape=jax.ShapeDtypeStruct((OFFSETS * UP2, rows), jnp.bfloat16),
        compiler_params=params(),
        cost_estimate=SMALL,
        name="upscaled_channels",
    )(embedding, weights, up_gain)


def masks_kernel(ranks, owners, *refs):
    stats = refs[:ranks]
    tok_ref, gains_ref, weights_ref, up_ref, out_ref = refs[ranks:]
    number = tok_ref.shape[0]
    maxima = stats[0][number : 2 * number, :]
    for part in stats[1:]:
        maxima = jnp.maximum(maxima, part[number : 2 * number, :])
    mixed, totals = 0.0, 0.0
    for part in stats:
        scale = jnp.exp(part[number : 2 * number, :] - maxima)
        mixed = mixed + part[:number, :] * scale
        totals = totals + part[2 * number :, :] * scale
    cross = mixed / totals
    top = weights_ref.shape[0] - ATTN_DIM
    wide = (top - 3 * NECK) // 2
    wh_at = 2 * wide
    first_out = layer_norm(
        tok_ref[...] + split_dot(cross, weights_ref[top:, :]), gains_ref[0:1, :], 1e-05
    )
    halves = jnp.concatenate(split(first_out))
    mixed = 0.0
    for block in range(0, wide, NECK):
        hidden = jnp.dot(
            halves, weights_ref[block : block + NECK, :], preferred_element_type=jnp.float32
        )
        hidden = jnp.maximum(hidden[:number] + hidden[number:], 0.0)
        mixed = mixed + split_dot(hidden, weights_ref[wide + block : wide + block + NECK, :])
    second = layer_norm(first_out + mixed, gains_ref[1:2, :], 1e-05)
    hyper_vec = jnp.maximum(split_dot(second, weights_ref[wh_at : wh_at + NECK, :]), 0.0)
    wh_at += NECK
    hyper_vec = jnp.maximum(split_dot(hyper_vec, weights_ref[wh_at : wh_at + NECK, :]), 0.0)
    wh_at += NECK
    hyper_vec = split_dot(hyper_vec, weights_ref[wh_at : wh_at + NECK, :UP2])
    hyper_vec = hyper_vec.astype(jnp.bfloat16)

    depth = OFFSETS * UP2
    span = OFFSETS * CAP
    channel = lax.broadcasted_iota(jnp.int32, (UP2, depth), 0)
    lane = lax.broadcasted_iota(jnp.int32, (UP2, depth), 1)
    repeat = jnp.where(lax.rem(lane, UP2) == channel, 1.0, 0.0).astype(jnp.bfloat16)
    tiled = jnp.dot(hyper_vec, repeat, preferred_element_type=jnp.float32).astype(jnp.bfloat16)
    row = lax.broadcasted_iota(jnp.int32, (owners * span, number), 0)
    slot = lax.broadcasted_iota(jnp.int32, (owners * span, number), 1)
    chosen = (row // span) * CAP + lax.rem(row, CAP)
    choose = jnp.where(chosen == slot, 1.0, 0.0).astype(jnp.bfloat16)
    spread = jnp.dot(choose, tiled, preferred_element_type=jnp.float32)
    row = lax.broadcasted_iota(jnp.int32, spread.shape, 0)
    lane = lax.broadcasted_iota(jnp.int32, spread.shape, 1)
    same = lax.rem(row, span) // CAP == lane // UP2
    spread = jnp.where(same, spread, 0.0).astype(jnp.bfloat16)
    logits = jnp.dot(spread, up_ref[...], preferred_element_type=jnp.float32).astype(jnp.bfloat16)
    for owner in range(owners):
        out_ref[owner] = logits[owner * span : (owner + 1) * span, :]


def mask_logits(stats, query_tok, owners, gains, weights, upscaled):
    cells = upscaled.shape[1]
    return pl.pallas_call(
        functools.partial(masks_kernel, len(stats), owners),
        out_shape=jax.ShapeDtypeStruct((owners, OFFSETS * CAP, cells), jnp.bfloat16),
        compiler_params=params(),
        cost_estimate=SMALL,
        name="token_side_and_masks",
    )(*stats, query_tok, gains, weights, upscaled)


def place_kernel(slots, recv_ref, choose_ref, order_ref, out_ref, tiles_ref):
    cells = recv_ref.shape[1]
    pairs = cells // LANES
    rows = jnp.dot(choose_ref[...], recv_ref[...], preferred_element_type=jnp.float32)
    rows = rows.astype(jnp.bfloat16)
    for top in range(2):
        for low in range(2):
            for pair in range(pairs):
                at = ((top * 2 + low) * pairs + pair) * slots
                for left in range(2):
                    for right in range(2):
                        offset = ((top * 2 + left) * 2 + low) * 2 + right
                        corner = left * 2 + right
                        tiles_ref[at : at + slots, corner * LANES : (corner + 1) * LANES] = rows[
                            offset * slots : (offset + 1) * slots,
                            pair * LANES : (pair + 1) * LANES,
                        ]
    ordered = jnp.dot(tiles_ref[...], order_ref[...], preferred_element_type=jnp.float32)
    width = 4 * GRID
    for top in range(2):
        for low in range(2):
            for pair in range(pairs):
                at = ((top * 2 + low) * pairs + pair) * slots
                for odd in range(2):
                    line = (2 * pair + odd) * 4 + top * 2 + low
                    out_ref[:, line * width : (line + 1) * width] = ordered[
                        at : at + slots, odd * width : (odd + 1) * width
                    ]


def place_rows(received, choose, order, slots):
    cells = received.shape[1]
    return pl.pallas_call(
        functools.partial(place_kernel, slots),
        out_shape=jax.ShapeDtypeStruct((slots, OFFSETS * cells), jnp.float32),
        scratch_shapes=[pltpu.VMEM((4 * (cells // LANES) * slots, 4 * LANES), jnp.bfloat16)],
        compiler_params=params(),
        cost_estimate=SMALL,
        name="rows_in_pixel_order",
    )(received, choose, order)


def pixel_order():
    source = np.arange(4 * LANES)
    corner, odd, column = source // LANES, source // GRID % 2, source % GRID
    target = odd * 4 * GRID + column * 4 + corner
    matrix = np.zeros((4 * LANES, 4 * LANES), np.float32)
    matrix[source, target] = 1.0
    return jnp.asarray(matrix, jnp.bfloat16)


def after(value, done):
    return lax.optimization_barrier((value, done))[0]


def shifted(block, shift, ranks):
    return lax.ppermute(block, "tok", [(i, (i + shift) % ranks) for i in range(ranks)])


def exchanged(blocks, back=False):
    ranks = len(blocks)
    return [blocks[0]] + [
        shifted(blocks[shift], ranks - shift if back else shift, ranks)
        for shift in range(1, ranks)
    ]


def gathered(block, axis):
    count = lax.axis_size(axis)
    if count & (count - 1):
        return lax.all_gather(block, axis, axis=0, tiled=True)
    place = lax.axis_index(axis)
    reach = 1
    while reach < count:
        other = lax.ppermute(block, axis, [(i, i ^ reach) for i in range(count)])
        low = (place & reach) == 0
        block = jnp.concatenate([jnp.where(low, block, other), jnp.where(low, other, block)])
        reach *= 2
    return block


def body(
    tokens,
    ln_gain,
    w_qkv,
    w_proj,
    w_neck1,
    neck_gain1,
    w_neck2,
    neck_gain2,
    pe_matrix,
    query_bias,
    dec_qkv,
    dec_out,
    dec_gains,
    w_mlp1,
    w_mlp2,
    w_hyper,
    w_hyper_out,
    w_up1,
    up_gain,
    w_up2,
    req_image,
    points,
):
    picture = tokens[0]
    tok_rows = picture.shape[0]
    grid_rows = tok_rows // GRID
    ranks = lax.axis_size("tok")
    owners = lax.axis_size("img")
    rank = lax.axis_index("tok")
    me = rank.astype(jnp.int32).reshape(1)
    edge = tok_rows // 4
    all_spans = ((0, tok_rows),)
    edge_spans = ((0, edge), (tok_rows - edge, tok_rows))
    mid_spans = ((edge, tok_rows - edge),)
    first_out = project(0, ranks, ((0, 1, 2),), me, picture, ln_gain, w_qkv)
    first_in = exchanged(first_out)
    second_out = project(
        1, ranks, ((0,), (0,), (1, 2)), me, after(picture, first_out[0]), ln_gain, w_qkv
    )
    edge_out, mid_out, kv_out = (second_out[at * ranks : (at + 1) * ranks] for at in range(3))

    targets, spots, pe_late = after((req_image[:, 0], points, pe_matrix), first_out[0])
    slots = targets.shape[0]
    asked = jnp.concatenate([targets[:, None], spots], axis=1)
    everyone = gathered(asked[None], "img")
    here = (everyone[:, :, 0] == lax.axis_index("img")).astype(jnp.int32)
    turn = jnp.cumsum(here, axis=1) - here
    filling = here[:, :, None] * (turn[:, :, None] == jnp.arange(CAP)[None, None, :])
    arrived = jnp.sum(filling[:, :, :, None] * everyone[:, :, None, 1:], axis=1)
    matches = (targets[:, None] == jnp.arange(owners, dtype=jnp.int32)[None, :]).astype(jnp.int32)
    order_no = jnp.sum((jnp.cumsum(matches, axis=0) - matches) * matches, axis=1)
    places = targets * CAP + order_no
    placing = places[:, None] == jnp.arange(owners * CAP, dtype=jnp.int32)[None, :]
    number = owners * CAP
    flattened = arrived.reshape(number, 2).astype(jnp.float32)
    query_tok = query_bias + fourier((flattened + 0.5) / IMG_SIDE * 2.0 - 1.0, pe_late)
    query_matrix = jnp.dot(query_tok, dec_qkv[0], precision=highest_precision)
    head_size = ATTN_DIM // DEC_HEADS
    head_mask = (
        jnp.arange(DEC_HEADS)[:, None] == jnp.arange(ATTN_DIM)[None, :] // head_size
    ).astype(jnp.float32)
    spread_queries = (head_mask[:, None, :] * query_matrix[None, :, :]).reshape(
        DEC_HEADS * number, ATTN_DIM
    )
    offset_eye = jnp.eye(OFFSETS, dtype=jnp.bfloat16)
    choose = (
        offset_eye[:, None, None, :, None]
        * placing.astype(jnp.bfloat16).reshape(1, slots, owners, 1, CAP)
    ).reshape(OFFSETS * slots, owners * OFFSETS * CAP)
    order = pixel_order()

    kv_in = exchanged(after(kv_out, first_in[1:]))
    sines, decoder = after(
        (
            grid_sines(rank * grid_rows, grid_rows, pe_late),
            (dec_qkv, dec_out, w_mlp1, w_mlp2, w_hyper, w_hyper_out, w_up1, w_up2),
        ),
        first_out[0],
    )
    prepared = prepare(sines, *decoder)
    up_column = after(up_gain, first_out[0]).reshape(-1, 1)
    first_in, prepared, spread_queries, query_tok, up_column = lax.optimization_barrier(
        (first_in, prepared, spread_queries, query_tok, up_column)
    )
    token_weights, up_weights, key_value, code_keys = prepared
    first_mixed = attention(first_in, first_in, all_spans)
    edge_in = exchanged(after(edge_out, (kv_in[1:], first_mixed)))
    own_edge, own_mid = attention(
        after([edge_out[0], mid_out[0]], first_mixed), kv_in, ((0, 2 * edge),)
    )
    mid_in = exchanged(after(mid_out, (edge_in[1:], own_edge)))
    edge_mixed = attention(
        after(edge_in[1:], own_edge), kv_in, edge_spans, beside=first_mixed[1:]
    )
    edge_heads = exchanged(after([own_edge] + edge_mixed, mid_in[1:]), back=True)[1:]
    mid_mixed = attention(
        after(mid_in[1:], edge_mixed), kv_in, mid_spans, beside=first_mixed[1:]
    )
    mid_heads = exchanged([own_mid] + mid_mixed, back=True)[1:]
    neck_args = (edge, ranks, me, picture, w_proj, w_neck1, neck_gain1)
    edge_narrow = neck(0, 3, *neck_args, (first_mixed[0], own_edge), edge_heads)
    ends = ranks - 1
    prev = lax.ppermute(edge_narrow[-GRID:], "tok", [(i, i + 1) for i in range(ends)])
    following = lax.ppermute(edge_narrow[:GRID], "tok", [(i + 1, i) for i in range(ends)])
    mid_narrow = neck(1, 1, *neck_args, (first_mixed[0], own_mid), mid_heads)

    embedding, stats = embed(
        prev,
        following,
        edge_narrow,
        mid_narrow,
        w_neck2,
        neck_gain2,
        key_value,
        code_keys,
        spread_queries,
    )
    all_stats = exchanged([stats] * ranks)
    upscaled = upscale(embedding, up_weights, up_column)
    outgoing = mask_logits(
        all_stats,
        query_tok,
        owners,
        dec_gains,
        token_weights,
        upscaled,
    )
    answer = lax.all_to_all(outgoing, "img", split_axis=0, concat_axis=0, tiled=True)
    return place_rows(answer.reshape(number * OFFSETS, tok_rows), choose, order, slots)


def solution(mesh):
    placed = (
        (P("img", "tok", None),) + (P(),) * 19 + (P("img", None),) * 2
    )
    return jax.shard_map(
        body, mesh=mesh, in_specs=placed, out_specs=P("img", "tok"), check_vma=False
    )
```

```python
import functools
import math

import jax
import jax.numpy as jnp
import numpy as np
from jax import lax
from jax.experimental import pallas as pl
from jax.experimental.pallas import tpu as pltpu
from jax.sharding import PartitionSpec as P

HEADS = 8
HDIM = 80
GRID = 64
NECK = 256
ATTN_DIM = 128
DEC_HEADS = 8
UP1 = 64
UP2 = 32
IMG_SIDE = 1024
CAP = 4
LANES = 128
OFFSETS = 16
VMEM_BYTES = 24 << 20
WHOLE_VMEM_BYTES = 56 << 20

highest_precision = lax.Precision.HIGHEST
SMALL = pl.CostEstimate(flops=1 << 10, bytes_accessed=1 << 10, transcendentals=0)
TO_BASE2 = math.log2(math.e) / math.sqrt(HDIM)


def layer_norm(tensor, gain_vec, epsilon, axis=-1):
    average = jnp.mean(tensor, axis=axis, keepdims=True)
    centred = tensor - average
    spread = jnp.mean(centred * centred, axis=axis, keepdims=True)
    return centred * lax.rsqrt(spread + epsilon) * gain_vec


def gelu(tensor):
    return 0.5 * tensor * (1.0 + lax.erf(tensor * math.sqrt(0.5)))


def fourier(coords, pe_matrix):
    angles = 2.0 * math.pi * jnp.dot(coords, pe_matrix, precision=highest_precision)
    return jnp.concatenate([jnp.sin(angles), jnp.cos(angles)], axis=-1)


def grid_sines(first_row, grid_rows, pe_matrix):
    row_ids = (first_row + jnp.arange(grid_rows, dtype=jnp.int32)).astype(jnp.float32)
    col_ids = jnp.arange(GRID, dtype=jnp.int32).astype(jnp.float32)
    ycoord = (row_ids + 0.5) / GRID * 2.0 - 1.0
    xcoord = (col_ids + 0.5) / GRID * 2.0 - 1.0
    angles = jnp.concatenate([xcoord[:, None] * pe_matrix[0], ycoord[:, None] * pe_matrix[1]])
    angles = 2.0 * math.pi * angles
    return jnp.concatenate([jnp.sin(angles), jnp.cos(angles)], axis=1)


def params(**extra):
    return pltpu.CompilerParams(vmem_limit_bytes=VMEM_BYTES, **extra)


def split(tensor):
    high = tensor.astype(jnp.bfloat16)
    return high, (tensor - high.astype(jnp.float32)).astype(jnp.bfloat16)


def split_dot(left, right):
    rows = left.shape[0]
    both = jnp.dot(jnp.concatenate(split(left)), right, preferred_element_type=jnp.float32)
    return both[:rows] + both[rows:]


def prepare_kernel(
    sines_ref,
    qkv_ref,
    wo_ref,
    w1_ref,
    w2_ref,
    wh_ref,
    who_ref,
    up1_ref,
    up2_ref,
    token_ref,
    up_ref,
    key_value_ref,
    code_ref,
    codes_ref,
):
    hidden = w1_ref.shape[1]
    for block in range(hidden // NECK):
        columns = slice(block * NECK, (block + 1) * NECK)
        token_ref[columns, :] = w1_ref[:, columns].astype(jnp.bfloat16)
    token_ref[hidden : 2 * hidden, :] = w2_ref[...].astype(jnp.bfloat16)
    at = 2 * hidden
    for layer in range(2):
        token_ref[at : at + NECK, :] = wh_ref[layer].astype(jnp.bfloat16)
        at += NECK
    token_ref[at : at + NECK, :UP2] = who_ref[...].astype(jnp.bfloat16)
    at += NECK
    token_ref[at:, :] = wo_ref[...].astype(jnp.bfloat16)
    up_ref[:NECK, :] = up1_ref[...].astype(jnp.bfloat16)
    up_ref[NECK:, : 4 * UP2] = up2_ref[...].astype(jnp.bfloat16)
    key_high, key_low = split(qkv_ref[1])
    key_value_ref[:, :ATTN_DIM] = key_high
    key_value_ref[:, ATTN_DIM : 2 * ATTN_DIM] = qkv_ref[2].astype(jnp.bfloat16)
    key_value_ref[:, 2 * ATTN_DIM :] = key_low
    half = sines_ref.shape[1] // 2
    sin_x, cos_x = sines_ref[:GRID, :half], sines_ref[:GRID, half:]
    for row in range(sines_ref.shape[0] - GRID):
        sin_y = sines_ref[GRID + row : GRID + row + 1, :half]
        cos_y = sines_ref[GRID + row : GRID + row + 1, half:]
        at = row * GRID
        codes_ref[at : at + GRID, :half] = sin_x * cos_y + cos_x * sin_y
        codes_ref[at : at + GRID, half:] = cos_x * cos_y - sin_x * sin_y
    code_high, code_low = split(codes_ref[...])
    code_ref[...] = (
        jnp.dot(code_high, key_high, preferred_element_type=jnp.float32)
        + jnp.dot(code_low, key_high, preferred_element_type=jnp.float32)
        + jnp.dot(code_high, key_low, preferred_element_type=jnp.float32)
    )


def prepare(sines, dec_qkv, dec_out, w_mlp1, w_mlp2, *weights):
    cells = (sines.shape[0] - GRID) * GRID
    rows = 2 * w_mlp1.shape[1] + 3 * NECK + ATTN_DIM
    return pl.pallas_call(
        prepare_kernel,
        out_shape=[
            jax.ShapeDtypeStruct((rows, NECK), jnp.bfloat16),
            jax.ShapeDtypeStruct((NECK + UP1, NECK), jnp.bfloat16),
            jax.ShapeDtypeStruct((NECK, 3 * ATTN_DIM), jnp.bfloat16),
            jax.ShapeDtypeStruct((cells, ATTN_DIM), jnp.float32),
        ],
        scratch_shapes=[pltpu.VMEM((cells, NECK), jnp.float32)],
        compiler_params=pltpu.CompilerParams(vmem_limit_bytes=WHOLE_VMEM_BYTES),
        cost_estimate=SMALL,
        name="decoder_weights",
    )(sines, dec_qkv, dec_out, w_mlp1, w_mlp2, *weights)


def head_span(span, ranks):
    first = span * ranks * HDIM
    start = first // LANES * LANES
    stop = -(-(first + ranks * HDIM) // LANES) * LANES
    return first, start, stop


def project_kernel(span, ranks, parts, me_ref, x_ref, gain_ref, w_hbm, *refs):
    inner = HEADS * HDIM
    count = len(parts) * ranks
    outs = refs[:count]
    weights, rows_ref, sems = refs[-3:]
    first, start, stop = head_span(span, ranks)
    width = stop - start
    step = pl.program_id(0)
    copies = [
        pltpu.make_async_copy(
            w_hbm.at[:, pl.ds(part * inner + start, width)],
            weights.at[:, pl.ds(part * width, width)],
            sems.at[part],
        )
        for part in range(3)
    ]

    @pl.when(step == 0)
    def _():
        for copy in copies:
            copy.start()

    gain = gain_ref[...].reshape(1, -1)
    normed = layer_norm(x_ref[...].astype(jnp.float32), gain, 1e-06).astype(jnp.bfloat16)

    @pl.when(step == 0)
    def _():
        for copy in copies:
            copy.wait()

    rows_ref[...] = (
        jnp.dot(normed, weights[...], preferred_element_type=jnp.float32).astype(jnp.bfloat16).T
    )
    for index, wanted in enumerate(parts):
        for shift in range(ranks):
            out = outs[index * ranks + shift]
            columns = slice(None)
            if out.shape[1] < rows_ref.shape[1]:
                quarter = step if index == 0 else 1 - step
                columns = pl.ds(pl.multiple_of(quarter * out.shape[1], LANES), out.shape[1])
            head = lax.rem(me_ref[0] + shift, ranks)
            for at, part in enumerate(wanted):
                place = pl.multiple_of(head * HDIM + (part * width + first - start), 16)
                out[at * HDIM : (at + 1) * HDIM, :] = rows_ref[pl.ds(place, HDIM), columns]


def project(span, ranks, parts, me, source, ln_gain, w_qkv):
    rows, model = source.shape
    block = rows // 2
    _, start, stop = head_span(span, ranks)
    width = stop - start
    sizes = [
        (len(wanted) * HDIM, block // parts.count(wanted))
        for wanted in parts
        for _ in range(ranks)
    ]
    out_shape = [jax.ShapeDtypeStruct((high, 2 * wide), jnp.bfloat16) for high, wide in sizes]
    out_specs = [pl.BlockSpec(size, lambda i: (0, i)) for size in sizes]
    return pl.pallas_call(
        functools.partial(project_kernel, span, ranks, parts),
        grid=(rows // block,),
        in_specs=[
            pl.BlockSpec(memory_space=pltpu.SMEM),
            pl.BlockSpec((block, model), lambda i: (i, 0)),
            pl.BlockSpec((model,), lambda i: (0,)),
            pl.BlockSpec(memory_space=pl.ANY),
        ],
        out_specs=out_specs,
        out_shape=out_shape,
        scratch_shapes=[
            pltpu.VMEM((model, 3 * width), jnp.bfloat16),
            pltpu.VMEM((3 * width, block), jnp.bfloat16),
            pltpu.SemaphoreType.DMA((3,)),
        ],
        compiler_params=pltpu.CompilerParams(
            vmem_limit_bytes=VMEM_BYTES if span else WHOLE_VMEM_BYTES
        ),
        cost_estimate=SMALL,
        name="norm_and_projections",
    )(me, source, ln_gain, w_qkv)


def attention_kernel(spans, query_block, key_block, sources, ranks, *refs):
    query_refs, kv_refs = refs[:sources], refs[sources : sources + ranks]
    beside, outs = refs[sources + ranks : -4 - sources], refs[-4 - sources : -4]
    queries, keys, values, mixed_out = refs[-4:]
    rows = kv_refs[0].shape[1]
    key_row = kv_refs[0].shape[0] - 2 * HDIM
    total = ranks * rows
    base = sum(stop - first for first, stop in spans) if beside else 0
    piece = min(query_block, 256)
    per_tile = query_block // piece

    places = [
        (source, at)
        for source in range(sources)
        for at in range(0, outs[0].shape[1] - base, piece)
    ]
    for number, (source, at) in enumerate(places):
        tile, inside = number // per_tile, number % per_tile * piece
        queries[tile, :, inside : inside + piece] = query_refs[source][:HDIM, at : at + piece]
    for rank in range(ranks):
        span = slice(rank * rows, (rank + 1) * rows)
        keys[span, :] = kv_refs[rank][key_row : key_row + HDIM, :].T
        values[:HDIM, span] = kv_refs[rank][key_row + HDIM :, :]
    values[HDIM:, :] = jnp.ones((values.shape[0] - HDIM, total), jnp.bfloat16)
    steps = total // key_block

    def one_block(step, carry):
        query = queries[step]

        def scores_of(at):
            return lax.dot_general(
                keys[at * key_block : (at + 1) * key_block, :],
                query,
                (((1,), (0,)), ((), ())),
                preferred_element_type=jnp.float32,
            )

        maxima, mixed = None, None
        upcoming = scores_of(0)
        for at in range(steps):
            scores = upcoming
            if at + 1 < steps:
                upcoming = scores_of(at + 1)
            block_max = jnp.max(scores, axis=0, keepdims=True)
            new_max = block_max if maxima is None else jnp.maximum(maxima, block_max)
            weights = jnp.exp2((scores - new_max) * TO_BASE2).astype(jnp.bfloat16)
            share = jnp.dot(
                values[:, at * key_block : (at + 1) * key_block],
                weights,
                preferred_element_type=jnp.float32,
            )
            if maxima is None:
                mixed = share
            else:
                mixed = mixed * jnp.exp2((maxima - new_max) * TO_BASE2) + share
            maxima = new_max
        mixed_out[step] = (mixed[:HDIM, :] / mixed[HDIM : HDIM + 1, :]).astype(jnp.bfloat16)
        return carry

    if queries.shape[0] <= 2:
        for step in range(queries.shape[0]):
            one_block(step, 0)
    else:
        lax.fori_loop(0, queries.shape[0], one_block, 0)
    for source, part in enumerate(beside):
        place = 0
        for first, stop in spans:
            outs[source][:, place : place + stop - first] = part[:, first:stop]
            place += stop - first
    for number, (source, at) in enumerate(places):
        tile, inside = number // per_tile, number % per_tile * piece
        outs[source][:, base + at : base + at + piece] = mixed_out[
            tile, :, inside : inside + piece
        ]


def attention(queries, key_values, wanted, beside=(), spans=()):
    ranks, rows = len(key_values), key_values[0].shape[1]
    extra = sum(stop - first for first, stop in spans)
    columns = len(queries) * wanted
    query_block = next(size for size in (1024, 768, 512, 256, columns) if columns % size == 0)
    key_block = min(ranks * rows, 512)
    tiles = columns // query_block
    return list(pl.pallas_call(
        functools.partial(
            attention_kernel, spans, query_block, key_block, len(queries), ranks
        ),
        out_shape=[jax.ShapeDtypeStruct((HDIM, extra + wanted), jnp.bfloat16)] * len(queries),
        scratch_shapes=[
            pltpu.VMEM((tiles, HDIM, query_block), jnp.bfloat16),
            pltpu.VMEM((ranks * rows, HDIM), jnp.bfloat16),
            pltpu.VMEM((HDIM + 16, ranks * rows), jnp.bfloat16),
            pltpu.VMEM((tiles, HDIM, query_block), jnp.bfloat16),
        ],
        compiler_params=params(),
        cost_estimate=SMALL,
        name="head_attention",
    )(*queries, *key_values, *beside))


def neck_kernel(ranks, paired, me_ref, tok_ref, wp_ref, wn_ref, gain_ref, *refs):
    heads = refs[:-2]
    out_ref, joined_ref = refs[-2:]
    for number in range(HEADS):
        span, shift = number // ranks, number % ranks
        head = lax.rem(me_ref[0] + shift, ranks) + span * ranks
        rows = pl.ds(pl.multiple_of(head * HDIM, 16), HDIM)
        joined_ref[rows, :] = heads[number][...]
        if number in paired:

            @pl.when(pl.program_id(0) == 1)
            def _(rows=rows, number=number):
                joined_ref[rows, :] = heads[HEADS + paired.index(number)][...]

    attended = joined_ref[...].T
    block_out = tok_ref[...].astype(jnp.float32) + jnp.dot(
        attended, wp_ref[...], preferred_element_type=jnp.float32
    )
    narrow = jnp.dot(
        block_out.astype(jnp.bfloat16), wn_ref[...], preferred_element_type=jnp.float32
    )
    out_ref[...] = layer_norm(narrow, gain_ref[...].reshape(1, -1), 1e-06).astype(jnp.bfloat16)


def neck(first, step, block, ranks, me, tokens, w_proj, w_neck1, gain, heads):
    model = tokens.shape[1]
    paired = [number for number, head in enumerate(heads) if len(head) == 4]
    parts = [(head[0], head[1], head[1] if len(head) == 4 else head[2]) for head in heads]
    parts += [(heads[number][2], heads[number][3], heads[number][3]) for number in paired]
    head_specs = [
        pl.BlockSpec((HDIM, block), lambda i, at=at, by=to - at: (0, at + i * by))
        for _, at, to in parts
    ]
    heads = [part for part, _, _ in parts]
    return pl.pallas_call(
        functools.partial(neck_kernel, ranks, paired),
        grid=(2,),
        in_specs=[
            pl.BlockSpec(memory_space=pltpu.SMEM),
            pl.BlockSpec((block, model), lambda i: (first + i * step, 0)),
            pl.BlockSpec(w_proj.shape, lambda i: (0, 0)),
            pl.BlockSpec(w_neck1.shape, lambda i: (0, 0)),
            pl.BlockSpec(gain.shape, lambda i: (0,)),
        ]
        + head_specs,
        out_specs=pl.BlockSpec((block, NECK), lambda i: (i, 0)),
        out_shape=jax.ShapeDtypeStruct((2 * block, NECK), jnp.bfloat16),
        scratch_shapes=[pltpu.VMEM((HEADS * HDIM, block), jnp.bfloat16)],
        compiler_params=params(),
        cost_estimate=SMALL,
        name="proj_and_narrow",
    )(me, tokens, w_proj, w_neck1, gain, *heads)


def embed_kernel(
    prev_ref,
    next_ref,
    edge_ref,
    mid_ref,
    w_ref,
    gain_ref,
    kv_ref,
    code_ref,
    query_ref,
    emb_ref,
    stats_ref,
    cells_ref,
):
    rows = emb_ref.shape[0]
    half = edge_ref.shape[0] // 2
    map_rows = jnp.concatenate(
        [prev_ref[...], edge_ref[:half, :], mid_ref[...], edge_ref[half:, :], next_ref[...]], axis=0
    )
    wide = map_rows.astype(jnp.float32)
    length = wide.shape[0]
    column = lax.rem(lax.broadcasted_iota(jnp.int32, (length, 1), 0), GRID)
    before = jnp.where(column == 0, 0.0, pltpu.roll(wide, 1, 0))
    after = jnp.where(column == GRID - 1, 0.0, pltpu.roll(wide, length - 1, 0))
    cells_ref[:, :NECK] = before.astype(jnp.bfloat16)
    cells_ref[:, NECK : 2 * NECK] = map_rows
    cells_ref[:, 2 * NECK :] = after.astype(jnp.bfloat16)
    total = None
    for row_off in range(3):
        share = jnp.dot(
            cells_ref[row_off * GRID : row_off * GRID + rows, :],
            w_ref[row_off * 3 * NECK : (row_off + 1) * 3 * NECK, :],
            preferred_element_type=jnp.float32,
        )
        total = share if total is None else total + share
    embedding = layer_norm(total, gain_ref[...].reshape(1, -1), 1e-06)
    high, low = split(embedding)
    emb_ref[...] = high

    from_high = jnp.dot(high, kv_ref[...], preferred_element_type=jnp.float32)
    from_low = jnp.dot(low, kv_ref[:, :ATTN_DIM], preferred_element_type=jnp.float32)
    dec_keys = from_high[:, :ATTN_DIM] + from_high[:, 2 * ATTN_DIM :] + from_low + code_ref[...]
    dec_values = from_high[:, ATTN_DIM : 2 * ATTN_DIM].astype(jnp.bfloat16)
    head_size = ATTN_DIM // DEC_HEADS
    key_high, key_low = split(dec_keys)
    query_high, query_low = split(query_ref[...])
    across = (((1,), (1,)), ((), ()))
    scores = (
        lax.dot_general(query_high, key_high, across, preferred_element_type=jnp.float32)
        + lax.dot_general(query_low, key_high, across, preferred_element_type=jnp.float32)
        + lax.dot_general(query_high, key_low, across, preferred_element_type=jnp.float32)
    )
    scores = scores * (1.0 / math.sqrt(head_size))
    maxima = jnp.max(scores, axis=1, keepdims=True)
    weights = jnp.exp(scores - maxima)
    totals = jnp.sum(weights, axis=1, keepdims=True)
    mixed = jnp.dot(weights.astype(jnp.bfloat16), dec_values, preferred_element_type=jnp.float32)
    number = stats_ref.shape[0] // 3
    lane_head = lax.broadcasted_iota(jnp.int32, (1, ATTN_DIM), 1) // head_size
    for at, stat in enumerate((mixed, maxima, totals)):
        picked = jnp.zeros((number, ATTN_DIM), jnp.float32)
        for head in range(DEC_HEADS):
            picked = jnp.where(
                lane_head == head, stat[head * number : (head + 1) * number, :], picked
            )
        stats_ref[at * number : (at + 1) * number, :] = picked


def embed(prev, following, edge, mid, w_neck2, gain, key_value, code_keys, spread_queries):
    rows = edge.shape[0] + mid.shape[0]
    number = spread_queries.shape[0] // DEC_HEADS
    length = rows + prev.shape[0] + following.shape[0]
    return pl.pallas_call(
        embed_kernel,
        out_shape=[
            jax.ShapeDtypeStruct((rows, NECK), jnp.bfloat16),
            jax.ShapeDtypeStruct((3 * number, ATTN_DIM), jnp.float32),
        ],
        scratch_shapes=[pltpu.VMEM((length, 3 * NECK), jnp.bfloat16)],
        compiler_params=params(),
        cost_estimate=SMALL,
        name="embedding_and_statistics",
    )(prev, following, edge, mid, w_neck2, gain, key_value, code_keys, spread_queries)


def upscale_kernel(emb_ref, weights_ref, gain_ref, out_ref):
    first_out = lax.dot_general(
        weights_ref[:NECK, :],
        emb_ref[...],
        (((0,), (1,)), ((), ())),
        preferred_element_type=jnp.float32,
    )
    for corner in range(4):
        part = layer_norm(
            first_out[corner * UP1 : (corner + 1) * UP1, :], gain_ref[...], 1e-06, axis=0
        )
        second = lax.dot_general(
            weights_ref[NECK:, : 4 * UP2],
            gelu(part).astype(jnp.bfloat16),
            (((0,), (0,)), ((), ())),
            preferred_element_type=jnp.float32,
        )
        out_ref[corner * 4 * UP2 : (corner + 1) * 4 * UP2, :] = gelu(second).astype(jnp.bfloat16)


def upscale(embedding, weights, up_gain):
    rows = embedding.shape[0]
    return pl.pallas_call(
        upscale_kernel,
        out_shape=jax.ShapeDtypeStruct((OFFSETS * UP2, rows), jnp.bfloat16),
        compiler_params=params(),
        cost_estimate=SMALL,
        name="upscaled_channels",
    )(embedding, weights, up_gain)


def masks_kernel(ranks, owners, *refs):
    stats = refs[:ranks]
    tok_ref, gains_ref, weights_ref, up_ref, out_ref = refs[ranks:]
    number = tok_ref.shape[0]
    maxima = stats[0][number : 2 * number, :]
    for part in stats[1:]:
        maxima = jnp.maximum(maxima, part[number : 2 * number, :])
    mixed, totals = 0.0, 0.0
    for part in stats:
        scale = jnp.exp(part[number : 2 * number, :] - maxima)
        mixed = mixed + part[:number, :] * scale
        totals = totals + part[2 * number :, :] * scale
    cross = mixed / totals
    top = weights_ref.shape[0] - ATTN_DIM
    wide = (top - 3 * NECK) // 2
    wh_at = 2 * wide
    first_out = layer_norm(
        tok_ref[...] + split_dot(cross, weights_ref[top:, :]), gains_ref[0:1, :], 1e-05
    )
    halves = jnp.concatenate(split(first_out))
    mixed = 0.0
    for block in range(0, wide, NECK):
        hidden = jnp.dot(
            halves, weights_ref[block : block + NECK, :], preferred_element_type=jnp.float32
        )
        hidden = jnp.maximum(hidden[:number] + hidden[number:], 0.0)
        mixed = mixed + split_dot(hidden, weights_ref[wide + block : wide + block + NECK, :])
    second = layer_norm(first_out + mixed, gains_ref[1:2, :], 1e-05)
    hyper_vec = jnp.maximum(split_dot(second, weights_ref[wh_at : wh_at + NECK, :]), 0.0)
    wh_at += NECK
    hyper_vec = jnp.maximum(split_dot(hyper_vec, weights_ref[wh_at : wh_at + NECK, :]), 0.0)
    wh_at += NECK
    hyper_vec = split_dot(hyper_vec, weights_ref[wh_at : wh_at + NECK, :UP2])
    hyper_vec = hyper_vec.astype(jnp.bfloat16)

    depth = OFFSETS * UP2
    span = OFFSETS * CAP
    channel = lax.broadcasted_iota(jnp.int32, (UP2, depth), 0)
    lane = lax.broadcasted_iota(jnp.int32, (UP2, depth), 1)
    repeat = jnp.where(lax.rem(lane, UP2) == channel, 1.0, 0.0).astype(jnp.bfloat16)
    tiled = jnp.dot(hyper_vec, repeat, preferred_element_type=jnp.float32).astype(jnp.bfloat16)
    row = lax.broadcasted_iota(jnp.int32, (owners * span, number), 0)
    slot = lax.broadcasted_iota(jnp.int32, (owners * span, number), 1)
    chosen = (row // span) * CAP + lax.rem(row, CAP)
    choose = jnp.where(chosen == slot, 1.0, 0.0).astype(jnp.bfloat16)
    spread = jnp.dot(choose, tiled, preferred_element_type=jnp.float32)
    row = lax.broadcasted_iota(jnp.int32, spread.shape, 0)
    lane = lax.broadcasted_iota(jnp.int32, spread.shape, 1)
    same = lax.rem(row, span) // CAP == lane // UP2
    spread = jnp.where(same, spread, 0.0).astype(jnp.bfloat16)
    logits = jnp.dot(spread, up_ref[...], preferred_element_type=jnp.float32).astype(jnp.bfloat16)
    for owner in range(owners):
        out_ref[owner] = logits[owner * span : (owner + 1) * span, :]


def mask_logits(stats, query_tok, owners, gains, weights, upscaled):
    cells = upscaled.shape[1]
    return pl.pallas_call(
        functools.partial(masks_kernel, len(stats), owners),
        out_shape=jax.ShapeDtypeStruct((owners, OFFSETS * CAP, cells), jnp.bfloat16),
        compiler_params=params(),
        cost_estimate=SMALL,
        name="token_side_and_masks",
    )(*stats, query_tok, gains, weights, upscaled)


def place_kernel(slots, recv_ref, choose_ref, order_ref, out_ref, tiles_ref):
    cells = recv_ref.shape[1]
    pairs = cells // LANES
    rows = jnp.dot(choose_ref[...], recv_ref[...], preferred_element_type=jnp.float32)
    rows = rows.astype(jnp.bfloat16)
    for top in range(2):
        for low in range(2):
            for pair in range(pairs):
                at = ((top * 2 + low) * pairs + pair) * slots
                for left in range(2):
                    for right in range(2):
                        offset = ((top * 2 + left) * 2 + low) * 2 + right
                        corner = left * 2 + right
                        tiles_ref[at : at + slots, corner * LANES : (corner + 1) * LANES] = rows[
                            offset * slots : (offset + 1) * slots,
                            pair * LANES : (pair + 1) * LANES,
                        ]
    ordered = jnp.dot(tiles_ref[...], order_ref[...], preferred_element_type=jnp.float32)
    width = 4 * GRID
    for top in range(2):
        for low in range(2):
            for pair in range(pairs):
                at = ((top * 2 + low) * pairs + pair) * slots
                for odd in range(2):
                    line = (2 * pair + odd) * 4 + top * 2 + low
                    out_ref[:, line * width : (line + 1) * width] = ordered[
                        at : at + slots, odd * width : (odd + 1) * width
                    ]


def place_rows(received, choose, order, slots):
    cells = received.shape[1]
    return pl.pallas_call(
        functools.partial(place_kernel, slots),
        out_shape=jax.ShapeDtypeStruct((slots, OFFSETS * cells), jnp.float32),
        scratch_shapes=[pltpu.VMEM((4 * (cells // LANES) * slots, 4 * LANES), jnp.bfloat16)],
        compiler_params=params(),
        cost_estimate=SMALL,
        name="rows_in_pixel_order",
    )(received, choose, order)


def pixel_order():
    source = np.arange(4 * LANES)
    corner, odd, column = source // LANES, source // GRID % 2, source % GRID
    target = odd * 4 * GRID + column * 4 + corner
    matrix = np.zeros((4 * LANES, 4 * LANES), np.float32)
    matrix[source, target] = 1.0
    return jnp.asarray(matrix, jnp.bfloat16)


def after(value, done):
    return lax.optimization_barrier((value, done))[0]


def shifted(block, shift, ranks):
    return lax.ppermute(block, "tok", [(i, (i + shift) % ranks) for i in range(ranks)])


def exchanged(blocks, back=False):
    ranks = len(blocks)
    return [blocks[0]] + [
        shifted(blocks[shift], ranks - shift if back else shift, ranks)
        for shift in range(1, ranks)
    ]


def gathered(block, axis):
    count = lax.axis_size(axis)
    if count & (count - 1):
        return lax.all_gather(block, axis, axis=0, tiled=True)
    place = lax.axis_index(axis)
    reach = 1
    while reach < count:
        other = lax.ppermute(block, axis, [(i, i ^ reach) for i in range(count)])
        low = (place & reach) == 0
        block = jnp.concatenate([jnp.where(low, block, other), jnp.where(low, other, block)])
        reach *= 2
    return block


def body(
    tokens,
    ln_gain,
    w_qkv,
    w_proj,
    w_neck1,
    neck_gain1,
    w_neck2,
    neck_gain2,
    pe_matrix,
    query_bias,
    dec_qkv,
    dec_out,
    dec_gains,
    w_mlp1,
    w_mlp2,
    w_hyper,
    w_hyper_out,
    w_up1,
    up_gain,
    w_up2,
    req_image,
    points,
):
    picture = tokens[0]
    tok_rows = picture.shape[0]
    grid_rows = tok_rows // GRID
    ranks = lax.axis_size("tok")
    owners = lax.axis_size("img")
    rank = lax.axis_index("tok")
    me = rank.astype(jnp.int32).reshape(1)
    edge = tok_rows // 4

    first_out = project(0, ranks, ((0, 1, 2),), me, picture, ln_gain, w_qkv)
    first_in = exchanged(first_out)
    second_out = project(
        1, ranks, ((0,), (0,), (1, 2)), me, after(picture, first_out[0]), ln_gain, w_qkv
    )
    edge_out, mid_out, kv_out = (second_out[at * ranks : (at + 1) * ranks] for at in range(3))

    targets, spots, pe_late = after((req_image[:, 0], points, pe_matrix), first_out[0])
    slots = targets.shape[0]
    asked = jnp.concatenate([targets[:, None], spots], axis=1)
    everyone = gathered(asked[None], "img")
    here = (everyone[:, :, 0] == lax.axis_index("img")).astype(jnp.int32)
    turn = jnp.cumsum(here, axis=1) - here
    filling = here[:, :, None] * (turn[:, :, None] == jnp.arange(CAP)[None, None, :])
    arrived = jnp.sum(filling[:, :, :, None] * everyone[:, :, None, 1:], axis=1)
    matches = (targets[:, None] == jnp.arange(owners, dtype=jnp.int32)[None, :]).astype(jnp.int32)
    order_no = jnp.sum((jnp.cumsum(matches, axis=0) - matches) * matches, axis=1)
    places = targets * CAP + order_no
    placing = places[:, None] == jnp.arange(owners * CAP, dtype=jnp.int32)[None, :]
    number = owners * CAP
    flattened = arrived.reshape(number, 2).astype(jnp.float32)
    query_tok = query_bias + fourier((flattened + 0.5) / IMG_SIDE * 2.0 - 1.0, pe_late)
    query_matrix = jnp.dot(query_tok, dec_qkv[0], precision=highest_precision)
    head_size = ATTN_DIM // DEC_HEADS
    head_mask = (
        jnp.arange(DEC_HEADS)[:, None] == jnp.arange(ATTN_DIM)[None, :] // head_size
    ).astype(jnp.float32)
    spread_queries = (head_mask[:, None, :] * query_matrix[None, :, :]).reshape(
        DEC_HEADS * number, ATTN_DIM
    )
    offset_eye = jnp.eye(OFFSETS, dtype=jnp.bfloat16)
    choose = (
        offset_eye[:, None, None, :, None]
        * placing.astype(jnp.bfloat16).reshape(1, slots, owners, 1, CAP)
    ).reshape(OFFSETS * slots, owners * OFFSETS * CAP)
    order = pixel_order()

    kv_in = exchanged(after(kv_out, first_in[1:]))
    sines, decoder = after(
        (
            grid_sines(rank * grid_rows, grid_rows, pe_late),
            (dec_qkv, dec_out, w_mlp1, w_mlp2, w_hyper, w_hyper_out, w_up1, w_up2),
        ),
        first_out[0],
    )
    prepared = prepare(sines, *decoder)
    up_column = after(up_gain, first_out[0]).reshape(-1, 1)
    first_in, prepared, spread_queries, query_tok, up_column = lax.optimization_barrier(
        (first_in, prepared, spread_queries, query_tok, up_column)
    )
    token_weights, up_weights, key_value, code_keys = prepared
    first_mixed = attention(first_in, first_in, tok_rows)
    edge_in = exchanged(after(edge_out, (kv_in[1:], first_mixed)))
    own_edge, own_mid = attention(
        after([edge_out[0], mid_out[0]], first_mixed), kv_in, 2 * edge
    )
    quarter = after([mixed[:, :edge] for mixed in first_mixed], kv_in[1:])
    mid_out = [mid_out[0]] + [
        jnp.concatenate([mid_out[shift], quarter[ranks - shift]], axis=1)
        for shift in range(1, ranks)
    ]
    mid_in = exchanged(after(mid_out, (edge_in[1:], own_edge)))
    edge_mixed = attention(
        after(edge_in[1:], own_edge),
        kv_in,
        2 * edge,
        beside=first_mixed[1:],
        spans=((tok_rows - edge, tok_rows),),
    )
    edge_heads = exchanged(after([own_edge] + edge_mixed, mid_in[1:]), back=True)[1:]
    mid_mixed = attention(
        after(mid_in[1:], edge_mixed),
        kv_in,
        2 * edge,
        beside=first_mixed[1:],
        spans=((edge, tok_rows - edge),),
    )
    mid_heads = exchanged([own_mid] + mid_mixed, back=True)[1:]
    neck_args = (edge, ranks, me, picture, w_proj, w_neck1, neck_gain1)
    edge_narrow = neck(
        0,
        3,
        *neck_args,
        [(first_mixed[0], 0, 3)]
        + [(early, 2, late, 0) for early, late in zip(mid_in[:0:-1], edge_heads)]
        + [(own_edge, 0, 1)]
        + [(part, 1, 2) for part in edge_heads],
    )
    ends = ranks - 1
    prev = lax.ppermute(edge_narrow[-GRID:], "tok", [(i, i + 1) for i in range(ends)])
    following = lax.ppermute(edge_narrow[:GRID], "tok", [(i + 1, i) for i in range(ends)])
    mid_narrow = neck(
        1,
        1,
        *neck_args,
        [(first_mixed[0], 1, 2)]
        + [(part, 0, 1) for part in mid_heads]
        + [(own_mid, 0, 1)]
        + [(part, 2, 3) for part in mid_heads],
    )

    embedding, stats = embed(
        prev,
        following,
        edge_narrow,
        mid_narrow,
        w_neck2,
        neck_gain2,
        key_value,
        code_keys,
        spread_queries,
    )
    all_stats = exchanged([stats] * ranks)
    upscaled = upscale(embedding, up_weights, up_column)
    outgoing = mask_logits(
        all_stats,
        query_tok,
        owners,
        dec_gains,
        token_weights,
        upscaled,
    )
    answer = lax.all_to_all(outgoing, "img", split_axis=0, concat_axis=0, tiled=True)
    return place_rows(answer.reshape(number * OFFSETS, tok_rows), choose, order, slots)


def solution(mesh):
    placed = (
        (P("img", "tok", None),) + (P(),) * 19 + (P("img", None),) * 2
    )
    return jax.shard_map(
        body, mesh=mesh, in_specs=placed, out_specs=P("img", "tok"), check_vma=False
    )
```

```python
import functools
import math

import jax
import jax.numpy as jnp
import numpy as np
from jax import lax
from jax.experimental import pallas as pl
from jax.experimental.pallas import tpu as pltpu
from jax.sharding import PartitionSpec as P

HEADS = 8
HDIM = 80
GRID = 64
NECK = 256
ATTN_DIM = 128
DEC_HEADS = 8
UP1 = 64
UP2 = 32
IMG_SIDE = 1024
CAP = 4
LANES = 128
OFFSETS = 16
VMEM_BYTES = 24 << 20
WHOLE_VMEM_BYTES = 56 << 20

highest_precision = lax.Precision.HIGHEST
SMALL = pl.CostEstimate(flops=1 << 10, bytes_accessed=1 << 10, transcendentals=0)
TO_BASE2 = math.log2(math.e) / math.sqrt(HDIM)


def layer_norm(tensor, gain_vec, epsilon, axis=-1):
    average = jnp.mean(tensor, axis=axis, keepdims=True)
    centred = tensor - average
    spread = jnp.mean(centred * centred, axis=axis, keepdims=True)
    return centred * lax.rsqrt(spread + epsilon) * gain_vec


def gelu(tensor):
    return 0.5 * tensor * (1.0 + lax.erf(tensor * math.sqrt(0.5)))


def fourier(coords, pe_matrix):
    angles = 2.0 * math.pi * jnp.dot(coords, pe_matrix, precision=highest_precision)
    return jnp.concatenate([jnp.sin(angles), jnp.cos(angles)], axis=-1)


def grid_sines(first_row, grid_rows, pe_matrix):
    row_ids = (first_row + jnp.arange(grid_rows, dtype=jnp.int32)).astype(jnp.float32)
    col_ids = jnp.arange(GRID, dtype=jnp.int32).astype(jnp.float32)
    ycoord = (row_ids + 0.5) / GRID * 2.0 - 1.0
    xcoord = (col_ids + 0.5) / GRID * 2.0 - 1.0
    angles = jnp.concatenate([xcoord[:, None] * pe_matrix[0], ycoord[:, None] * pe_matrix[1]])
    angles = 2.0 * math.pi * angles
    return jnp.concatenate([jnp.sin(angles), jnp.cos(angles)], axis=1)


def params(**extra):
    return pltpu.CompilerParams(vmem_limit_bytes=VMEM_BYTES, **extra)


def split(tensor):
    high = tensor.astype(jnp.bfloat16)
    return high, (tensor - high.astype(jnp.float32)).astype(jnp.bfloat16)


def split_dot(left, right):
    rows = left.shape[0]
    both = jnp.dot(jnp.concatenate(split(left)), right, preferred_element_type=jnp.float32)
    return both[:rows] + both[rows:]


def prepare_kernel(
    sines_ref,
    qkv_ref,
    wo_ref,
    w1_ref,
    w2_ref,
    wh_ref,
    who_ref,
    up1_ref,
    up2_ref,
    token_ref,
    up_ref,
    key_value_ref,
    code_ref,
    codes_ref,
):
    hidden = w1_ref.shape[1]
    for block in range(hidden // NECK):
        columns = slice(block * NECK, (block + 1) * NECK)
        token_ref[columns, :] = w1_ref[:, columns].astype(jnp.bfloat16)
    token_ref[hidden : 2 * hidden, :] = w2_ref[...].astype(jnp.bfloat16)
    at = 2 * hidden
    for layer in range(2):
        token_ref[at : at + NECK, :] = wh_ref[layer].astype(jnp.bfloat16)
        at += NECK
    token_ref[at : at + NECK, :UP2] = who_ref[...].astype(jnp.bfloat16)
    at += NECK
    token_ref[at:, :] = wo_ref[...].astype(jnp.bfloat16)
    up_ref[:NECK, :] = up1_ref[...].astype(jnp.bfloat16)
    up_ref[NECK:, : 4 * UP2] = up2_ref[...].astype(jnp.bfloat16)
    key_high, key_low = split(qkv_ref[1])
    key_value_ref[:, :ATTN_DIM] = key_high
    key_value_ref[:, ATTN_DIM : 2 * ATTN_DIM] = qkv_ref[2].astype(jnp.bfloat16)
    key_value_ref[:, 2 * ATTN_DIM :] = key_low
    half = sines_ref.shape[1] // 2
    sin_x, cos_x = sines_ref[:GRID, :half], sines_ref[:GRID, half:]
    for row in range(sines_ref.shape[0] - GRID):
        sin_y = sines_ref[GRID + row : GRID + row + 1, :half]
        cos_y = sines_ref[GRID + row : GRID + row + 1, half:]
        at = row * GRID
        codes_ref[at : at + GRID, :half] = sin_x * cos_y + cos_x * sin_y
        codes_ref[at : at + GRID, half:] = cos_x * cos_y - sin_x * sin_y
    code_high, code_low = split(codes_ref[...])
    code_ref[...] = (
        jnp.dot(code_high, key_high, preferred_element_type=jnp.float32)
        + jnp.dot(code_low, key_high, preferred_element_type=jnp.float32)
        + jnp.dot(code_high, key_low, preferred_element_type=jnp.float32)
    )


def prepare(sines, dec_qkv, dec_out, w_mlp1, w_mlp2, *weights):
    cells = (sines.shape[0] - GRID) * GRID
    rows = 2 * w_mlp1.shape[1] + 3 * NECK + ATTN_DIM
    return pl.pallas_call(
        prepare_kernel,
        out_shape=[
            jax.ShapeDtypeStruct((rows, NECK), jnp.bfloat16),
            jax.ShapeDtypeStruct((NECK + UP1, NECK), jnp.bfloat16),
            jax.ShapeDtypeStruct((NECK, 3 * ATTN_DIM), jnp.bfloat16),
            jax.ShapeDtypeStruct((cells, ATTN_DIM), jnp.float32),
        ],
        scratch_shapes=[pltpu.VMEM((cells, NECK), jnp.float32)],
        compiler_params=pltpu.CompilerParams(vmem_limit_bytes=WHOLE_VMEM_BYTES),
        cost_estimate=SMALL,
        name="decoder_weights",
    )(sines, dec_qkv, dec_out, w_mlp1, w_mlp2, *weights)


def head_span(span, ranks):
    first = span * ranks * HDIM
    start = first // LANES * LANES
    stop = -(-(first + ranks * HDIM) // LANES) * LANES
    return first, start, stop


def project_kernel(span, ranks, parts, me_ref, x_ref, gain_ref, w_hbm, *refs):
    inner = HEADS * HDIM
    count = len(parts) * ranks
    outs = refs[:count]
    weights, rows_ref, sems = refs[-3:]
    first, start, stop = head_span(span, ranks)
    width = stop - start
    step = pl.program_id(0)
    copies = [
        pltpu.make_async_copy(
            w_hbm.at[:, pl.ds(part * inner + start, width)],
            weights.at[:, pl.ds(part * width, width)],
            sems.at[part],
        )
        for part in range(3)
    ]

    @pl.when(step == 0)
    def _():
        for copy in copies:
            copy.start()

    gain = gain_ref[...].reshape(1, -1)
    normed = layer_norm(x_ref[...].astype(jnp.float32), gain, 1e-06).astype(jnp.bfloat16)

    @pl.when(step == 0)
    def _():
        for copy in copies:
            copy.wait()

    rows_ref[...] = (
        jnp.dot(normed, weights[...], preferred_element_type=jnp.float32).astype(jnp.bfloat16).T
    )
    for index, wanted in enumerate(parts):
        for shift in range(ranks):
            out = outs[index * ranks + shift]
            columns = slice(None)
            if out.shape[1] < rows_ref.shape[1]:
                quarter = step if index == 0 else 1 - step
                columns = pl.ds(pl.multiple_of(quarter * out.shape[1], LANES), out.shape[1])
            head = lax.rem(me_ref[0] + shift, ranks)
            for at, part in enumerate(wanted):
                place = pl.multiple_of(head * HDIM + (part * width + first - start), 16)
                out[at * HDIM : (at + 1) * HDIM, :] = rows_ref[pl.ds(place, HDIM), columns]


def project(span, ranks, parts, me, source, ln_gain, w_qkv):
    rows, model = source.shape
    block = rows // 2
    _, start, stop = head_span(span, ranks)
    width = stop - start
    sizes = [
        (len(wanted) * HDIM, block // parts.count(wanted))
        for wanted in parts
        for _ in range(ranks)
    ]
    out_shape = [jax.ShapeDtypeStruct((high, 2 * wide), jnp.bfloat16) for high, wide in sizes]
    out_specs = [pl.BlockSpec(size, lambda i: (0, i)) for size in sizes]
    return pl.pallas_call(
        functools.partial(project_kernel, span, ranks, parts),
        grid=(rows // block,),
        in_specs=[
            pl.BlockSpec(memory_space=pltpu.SMEM),
            pl.BlockSpec((block, model), lambda i: (i, 0)),
            pl.BlockSpec((model,), lambda i: (0,)),
            pl.BlockSpec(memory_space=pl.ANY),
        ],
        out_specs=out_specs,
        out_shape=out_shape,
        scratch_shapes=[
            pltpu.VMEM((model, 3 * width), jnp.bfloat16),
            pltpu.VMEM((3 * width, block), jnp.bfloat16),
            pltpu.SemaphoreType.DMA((3,)),
        ],
        compiler_params=pltpu.CompilerParams(
            vmem_limit_bytes=VMEM_BYTES if span else WHOLE_VMEM_BYTES
        ),
        cost_estimate=SMALL,
        name="norm_and_projections",
    )(me, source, ln_gain, w_qkv)


def attention_kernel(spans, query_block, key_block, sources, ranks, *refs):
    query_refs, kv_refs = refs[:sources], refs[sources : sources + ranks]
    beside, outs = refs[sources + ranks : -4 - sources], refs[-4 - sources : -4]
    queries, keys, values, mixed_out = refs[-4:]
    rows = kv_refs[0].shape[1]
    key_row = kv_refs[0].shape[0] - 2 * HDIM
    total = ranks * rows
    base = sum(stop - first for first, stop in spans) if beside else 0
    piece = min(query_block, 256)
    per_tile = query_block // piece

    places = [
        (source, at)
        for source in range(sources)
        for at in range(0, outs[0].shape[1] - base, piece)
    ]
    for number, (source, at) in enumerate(places):
        tile, inside = number // per_tile, number % per_tile * piece
        queries[tile, :, inside : inside + piece] = query_refs[source][:HDIM, at : at + piece]
    for rank in range(ranks):
        span = slice(rank * rows, (rank + 1) * rows)
        keys[span, :] = kv_refs[rank][key_row : key_row + HDIM, :].T
        values[:HDIM, span] = kv_refs[rank][key_row + HDIM :, :]
    values[HDIM:, :] = jnp.ones((values.shape[0] - HDIM, total), jnp.bfloat16)
    steps = total // key_block

    def one_block(step, carry):
        query = queries[step]

        def scores_of(at):
            return lax.dot_general(
                keys[at * key_block : (at + 1) * key_block, :],
                query,
                (((1,), (0,)), ((), ())),
                preferred_element_type=jnp.float32,
            )

        maxima, mixed = None, None
        upcoming = scores_of(0)
        for at in range(steps):
            scores = upcoming
            if at + 1 < steps:
                upcoming = scores_of(at + 1)
            block_max = jnp.max(scores, axis=0, keepdims=True)
            new_max = block_max if maxima is None else jnp.maximum(maxima, block_max)
            weights = jnp.exp2((scores - new_max) * TO_BASE2).astype(jnp.bfloat16)
            share = jnp.dot(
                values[:, at * key_block : (at + 1) * key_block],
                weights,
                preferred_element_type=jnp.float32,
            )
            if maxima is None:
                mixed = share
            else:
                mixed = mixed * jnp.exp2((maxima - new_max) * TO_BASE2) + share
            maxima = new_max
        mixed_out[step] = (mixed[:HDIM, :] / mixed[HDIM : HDIM + 1, :]).astype(jnp.bfloat16)
        return carry

    if queries.shape[0] <= 2:
        for step in range(queries.shape[0]):
            one_block(step, 0)
    else:
        lax.fori_loop(0, queries.shape[0], one_block, 0)
    for source, part in enumerate(beside):
        place = 0
        for first, stop in spans:
            outs[source][:, place : place + stop - first] = part[:, first:stop]
            place += stop - first
    for number, (source, at) in enumerate(places):
        tile, inside = number // per_tile, number % per_tile * piece
        outs[source][:, base + at : base + at + piece] = mixed_out[
            tile, :, inside : inside + piece
        ]


def attention(queries, key_values, wanted, beside=(), spans=()):
    ranks, rows = len(key_values), key_values[0].shape[1]
    extra = sum(stop - first for first, stop in spans)
    columns = len(queries) * wanted
    query_block = next(size for size in (1024, 768, 512, 256, columns) if columns % size == 0)
    key_block = min(ranks * rows, 512)
    tiles = columns // query_block
    return list(pl.pallas_call(
        functools.partial(
            attention_kernel, spans, query_block, key_block, len(queries), ranks
        ),
        out_shape=[jax.ShapeDtypeStruct((HDIM, extra + wanted), jnp.bfloat16)] * len(queries),
        scratch_shapes=[
            pltpu.VMEM((tiles, HDIM, query_block), jnp.bfloat16),
            pltpu.VMEM((ranks * rows, HDIM), jnp.bfloat16),
            pltpu.VMEM((HDIM + 16, ranks * rows), jnp.bfloat16),
            pltpu.VMEM((tiles, HDIM, query_block), jnp.bfloat16),
        ],
        compiler_params=params(),
        cost_estimate=SMALL,
        name="head_attention",
    )(*queries, *key_values, *beside))


def neck_kernel(ranks, paired, me_ref, tok_ref, wp_ref, wn_ref, gain_ref, *refs):
    heads = refs[:-2]
    out_ref, joined_ref = refs[-2:]
    for number in range(HEADS):
        span, shift = number // ranks, number % ranks
        head = lax.rem(me_ref[0] + shift, ranks) + span * ranks
        rows = pl.ds(pl.multiple_of(head * HDIM, 16), HDIM)
        joined_ref[rows, :] = heads[number][...]
        if number in paired:

            @pl.when(pl.program_id(0) == 1)
            def _(rows=rows, number=number):
                joined_ref[rows, :] = heads[HEADS + paired.index(number)][...]

    attended = joined_ref[...].T
    block_out = tok_ref[...].astype(jnp.float32) + jnp.dot(
        attended, wp_ref[...], preferred_element_type=jnp.float32
    )
    narrow = jnp.dot(
        block_out.astype(jnp.bfloat16), wn_ref[...], preferred_element_type=jnp.float32
    )
    out_ref[...] = layer_norm(narrow, gain_ref[...].reshape(1, -1), 1e-06).astype(jnp.bfloat16)


def neck(first, step, block, ranks, me, tokens, w_proj, w_neck1, gain, heads):
    model = tokens.shape[1]
    paired = [number for number, head in enumerate(heads) if len(head) == 4]
    parts = [(head[0], head[1], head[1] if len(head) == 4 else head[2]) for head in heads]
    parts += [(heads[number][2], heads[number][3], heads[number][3]) for number in paired]
    head_specs = [
        pl.BlockSpec((HDIM, block), lambda i, at=at, by=to - at: (0, at + i * by))
        for _, at, to in parts
    ]
    heads = [part for part, _, _ in parts]
    return pl.pallas_call(
        functools.partial(neck_kernel, ranks, paired),
        grid=(2,),
        in_specs=[
            pl.BlockSpec(memory_space=pltpu.SMEM),
            pl.BlockSpec((block, model), lambda i: (first + i * step, 0)),
            pl.BlockSpec(w_proj.shape, lambda i: (0, 0)),
            pl.BlockSpec(w_neck1.shape, lambda i: (0, 0)),
            pl.BlockSpec(gain.shape, lambda i: (0,)),
        ]
        + head_specs,
        out_specs=pl.BlockSpec((block, NECK), lambda i: (i, 0)),
        out_shape=jax.ShapeDtypeStruct((2 * block, NECK), jnp.bfloat16),
        scratch_shapes=[pltpu.VMEM((HEADS * HDIM, block), jnp.bfloat16)],
        compiler_params=params(),
        cost_estimate=SMALL,
        name="proj_and_narrow",
    )(me, tokens, w_proj, w_neck1, gain, *heads)


def embed_kernel(
    prev_ref,
    next_ref,
    edge_ref,
    mid_ref,
    w_ref,
    gain_ref,
    kv_ref,
    code_ref,
    query_ref,
    emb_ref,
    stats_ref,
    cells_ref,
):
    rows = emb_ref.shape[0]
    half = edge_ref.shape[0] // 2
    map_rows = jnp.concatenate(
        [prev_ref[...], edge_ref[:half, :], mid_ref[...], edge_ref[half:, :], next_ref[...]], axis=0
    )
    wide = map_rows.astype(jnp.float32)
    length = wide.shape[0]
    column = lax.rem(lax.broadcasted_iota(jnp.int32, (length, 1), 0), GRID)
    before = jnp.where(column == 0, 0.0, pltpu.roll(wide, 1, 0))
    after = jnp.where(column == GRID - 1, 0.0, pltpu.roll(wide, length - 1, 0))
    cells_ref[:, :NECK] = before.astype(jnp.bfloat16)
    cells_ref[:, NECK : 2 * NECK] = map_rows
    cells_ref[:, 2 * NECK :] = after.astype(jnp.bfloat16)
    total = None
    for row_off in range(3):
        share = jnp.dot(
            cells_ref[row_off * GRID : row_off * GRID + rows, :],
            w_ref[row_off * 3 * NECK : (row_off + 1) * 3 * NECK, :],
            preferred_element_type=jnp.float32,
        )
        total = share if total is None else total + share
    embedding = layer_norm(total, gain_ref[...].reshape(1, -1), 1e-06)
    high, low = split(embedding)
    emb_ref[...] = high

    from_high = jnp.dot(high, kv_ref[...], preferred_element_type=jnp.float32)
    from_low = jnp.dot(low, kv_ref[:, :ATTN_DIM], preferred_element_type=jnp.float32)
    dec_keys = from_high[:, :ATTN_DIM] + from_high[:, 2 * ATTN_DIM :] + from_low + code_ref[...]
    dec_values = from_high[:, ATTN_DIM : 2 * ATTN_DIM].astype(jnp.bfloat16)
    head_size = ATTN_DIM // DEC_HEADS
    key_high, key_low = split(dec_keys)
    query_high, query_low = split(query_ref[...])
    across = (((1,), (1,)), ((), ()))
    scores = (
        lax.dot_general(query_high, key_high, across, preferred_element_type=jnp.float32)
        + lax.dot_general(query_low, key_high, across, preferred_element_type=jnp.float32)
        + lax.dot_general(query_high, key_low, across, preferred_element_type=jnp.float32)
    )
    scores = scores * (1.0 / math.sqrt(head_size))
    maxima = jnp.max(scores, axis=1, keepdims=True)
    weights = jnp.exp(scores - maxima)
    totals = jnp.sum(weights, axis=1, keepdims=True)
    mixed = jnp.dot(weights.astype(jnp.bfloat16), dec_values, preferred_element_type=jnp.float32)
    number = stats_ref.shape[0] // 3
    lane_head = lax.broadcasted_iota(jnp.int32, (1, ATTN_DIM), 1) // head_size
    for at, stat in enumerate((mixed, maxima, totals)):
        picked = jnp.zeros((number, ATTN_DIM), jnp.float32)
        for head in range(DEC_HEADS):
            picked = jnp.where(
                lane_head == head, stat[head * number : (head + 1) * number, :], picked
            )
        stats_ref[at * number : (at + 1) * number, :] = picked


def embed(prev, following, edge, mid, w_neck2, gain, key_value, code_keys, spread_queries):
    rows = edge.shape[0] + mid.shape[0]
    number = spread_queries.shape[0] // DEC_HEADS
    length = rows + prev.shape[0] + following.shape[0]
    return pl.pallas_call(
        embed_kernel,
        out_shape=[
            jax.ShapeDtypeStruct((rows, NECK), jnp.bfloat16),
            jax.ShapeDtypeStruct((3 * number, ATTN_DIM), jnp.float32),
        ],
        scratch_shapes=[pltpu.VMEM((length, 3 * NECK), jnp.bfloat16)],
        compiler_params=params(),
        cost_estimate=SMALL,
        name="embedding_and_statistics",
    )(prev, following, edge, mid, w_neck2, gain, key_value, code_keys, spread_queries)


def upscale_kernel(emb_ref, weights_ref, gain_ref, out_ref):
    first_out = lax.dot_general(
        weights_ref[:NECK, :],
        emb_ref[...],
        (((0,), (1,)), ((), ())),
        preferred_element_type=jnp.float32,
    )
    for corner in range(4):
        part = layer_norm(
            first_out[corner * UP1 : (corner + 1) * UP1, :], gain_ref[...], 1e-06, axis=0
        )
        second = lax.dot_general(
            weights_ref[NECK:, : 4 * UP2],
            gelu(part).astype(jnp.bfloat16),
            (((0,), (0,)), ((), ())),
            preferred_element_type=jnp.float32,
        )
        out_ref[corner * 4 * UP2 : (corner + 1) * 4 * UP2, :] = gelu(second).astype(jnp.bfloat16)


def upscale(embedding, weights, up_gain):
    rows = embedding.shape[0]
    return pl.pallas_call(
        upscale_kernel,
        out_shape=jax.ShapeDtypeStruct((OFFSETS * UP2, rows), jnp.bfloat16),
        compiler_params=params(),
        cost_estimate=SMALL,
        name="upscaled_channels",
    )(embedding, weights, up_gain)


def masks_kernel(ranks, owners, *refs):
    stats = refs[:ranks]
    tok_ref, gains_ref, weights_ref, up_ref, out_ref = refs[ranks:]
    number = tok_ref.shape[0]
    maxima = stats[0][number : 2 * number, :]
    for part in stats[1:]:
        maxima = jnp.maximum(maxima, part[number : 2 * number, :])
    mixed, totals = 0.0, 0.0
    for part in stats:
        scale = jnp.exp(part[number : 2 * number, :] - maxima)
        mixed = mixed + part[:number, :] * scale
        totals = totals + part[2 * number :, :] * scale
    cross = mixed / totals
    top = weights_ref.shape[0] - ATTN_DIM
    wide = (top - 3 * NECK) // 2
    wh_at = 2 * wide
    first_out = layer_norm(
        tok_ref[...] + split_dot(cross, weights_ref[top:, :]), gains_ref[0:1, :], 1e-05
    )
    halves = jnp.concatenate(split(first_out))
    mixed = 0.0
    for block in range(0, wide, NECK):
        hidden = jnp.dot(
            halves, weights_ref[block : block + NECK, :], preferred_element_type=jnp.float32
        )
        hidden = jnp.maximum(hidden[:number] + hidden[number:], 0.0)
        mixed = mixed + split_dot(hidden, weights_ref[wide + block : wide + block + NECK, :])
    second = layer_norm(first_out + mixed, gains_ref[1:2, :], 1e-05)
    hyper_vec = jnp.maximum(split_dot(second, weights_ref[wh_at : wh_at + NECK, :]), 0.0)
    wh_at += NECK
    hyper_vec = jnp.maximum(split_dot(hyper_vec, weights_ref[wh_at : wh_at + NECK, :]), 0.0)
    wh_at += NECK
    hyper_vec = split_dot(hyper_vec, weights_ref[wh_at : wh_at + NECK, :UP2])
    hyper_vec = hyper_vec.astype(jnp.bfloat16)

    depth = OFFSETS * UP2
    span = OFFSETS * CAP
    channel = lax.broadcasted_iota(jnp.int32, (UP2, depth), 0)
    lane = lax.broadcasted_iota(jnp.int32, (UP2, depth), 1)
    repeat = jnp.where(lax.rem(lane, UP2) == channel, 1.0, 0.0).astype(jnp.bfloat16)
    tiled = jnp.dot(hyper_vec, repeat, preferred_element_type=jnp.float32).astype(jnp.bfloat16)
    row = lax.broadcasted_iota(jnp.int32, (owners * span, number), 0)
    slot = lax.broadcasted_iota(jnp.int32, (owners * span, number), 1)
    chosen = (row // span) * CAP + lax.rem(row, CAP)
    choose = jnp.where(chosen == slot, 1.0, 0.0).astype(jnp.bfloat16)
    spread = jnp.dot(choose, tiled, preferred_element_type=jnp.float32)
    row = lax.broadcasted_iota(jnp.int32, spread.shape, 0)
    lane = lax.broadcasted_iota(jnp.int32, spread.shape, 1)
    same = lax.rem(row, span) // CAP == lane // UP2
    spread = jnp.where(same, spread, 0.0).astype(jnp.bfloat16)
    logits = jnp.dot(spread, up_ref[...], preferred_element_type=jnp.float32).astype(jnp.bfloat16)
    for owner in range(owners):
        out_ref[owner] = logits[owner * span : (owner + 1) * span, :]


def mask_logits(stats, query_tok, owners, gains, weights, upscaled):
    cells = upscaled.shape[1]
    return pl.pallas_call(
        functools.partial(masks_kernel, len(stats), owners),
        out_shape=jax.ShapeDtypeStruct((owners, OFFSETS * CAP, cells), jnp.bfloat16),
        compiler_params=params(),
        cost_estimate=SMALL,
        name="token_side_and_masks",
    )(*stats, query_tok, gains, weights, upscaled)


def place_kernel(slots, recv_ref, choose_ref, order_ref, out_ref, tiles_ref):
    cells = recv_ref.shape[1]
    pairs = cells // LANES
    rows = jnp.dot(choose_ref[...], recv_ref[...], preferred_element_type=jnp.float32)
    rows = rows.astype(jnp.bfloat16)
    for top in range(2):
        for low in range(2):
            for pair in range(pairs):
                at = ((top * 2 + low) * pairs + pair) * slots
                for left in range(2):
                    for right in range(2):
                        offset = ((top * 2 + left) * 2 + low) * 2 + right
                        corner = left * 2 + right
                        tiles_ref[at : at + slots, corner * LANES : (corner + 1) * LANES] = rows[
                            offset * slots : (offset + 1) * slots,
                            pair * LANES : (pair + 1) * LANES,
                        ]
    ordered = jnp.dot(tiles_ref[...], order_ref[...], preferred_element_type=jnp.float32)
    width = 4 * GRID
    for top in range(2):
        for low in range(2):
            for pair in range(pairs):
                at = ((top * 2 + low) * pairs + pair) * slots
                for odd in range(2):
                    line = (2 * pair + odd) * 4 + top * 2 + low
                    out_ref[:, line * width : (line + 1) * width] = ordered[
                        at : at + slots, odd * width : (odd + 1) * width
                    ]


def place_rows(received, choose, order, slots):
    cells = received.shape[1]
    return pl.pallas_call(
        functools.partial(place_kernel, slots),
        out_shape=jax.ShapeDtypeStruct((slots, OFFSETS * cells), jnp.float32),
        scratch_shapes=[pltpu.VMEM((4 * (cells // LANES) * slots, 4 * LANES), jnp.bfloat16)],
        compiler_params=params(),
        cost_estimate=SMALL,
        name="rows_in_pixel_order",
    )(received, choose, order)


def pixel_order():
    source = np.arange(4 * LANES)
    corner, odd, column = source // LANES, source // GRID % 2, source % GRID
    target = odd * 4 * GRID + column * 4 + corner
    matrix = np.zeros((4 * LANES, 4 * LANES), np.float32)
    matrix[source, target] = 1.0
    return jnp.asarray(matrix, jnp.bfloat16)


def after(value, done):
    return lax.optimization_barrier((value, done))[0]


def shifted(block, shift, ranks):
    return lax.ppermute(block, "tok", [(i, (i + shift) % ranks) for i in range(ranks)])


def exchanged(blocks, back=False):
    ranks = len(blocks)
    return [blocks[0]] + [
        shifted(blocks[shift], ranks - shift if back else shift, ranks)
        for shift in range(1, ranks)
    ]


def gathered(block, axis):
    count = lax.axis_size(axis)
    if count & (count - 1):
        return lax.all_gather(block, axis, axis=0, tiled=True)
    place = lax.axis_index(axis)
    reach = 1
    while reach < count:
        other = lax.ppermute(block, axis, [(i, i ^ reach) for i in range(count)])
        low = (place & reach) == 0
        block = jnp.concatenate([jnp.where(low, block, other), jnp.where(low, other, block)])
        reach *= 2
    return block


def body(
    tokens,
    ln_gain,
    w_qkv,
    w_proj,
    w_neck1,
    neck_gain1,
    w_neck2,
    neck_gain2,
    pe_matrix,
    query_bias,
    dec_qkv,
    dec_out,
    dec_gains,
    w_mlp1,
    w_mlp2,
    w_hyper,
    w_hyper_out,
    w_up1,
    up_gain,
    w_up2,
    req_image,
    points,
):
    picture = tokens[0]
    tok_rows = picture.shape[0]
    grid_rows = tok_rows // GRID
    ranks = lax.axis_size("tok")
    owners = lax.axis_size("img")
    rank = lax.axis_index("tok")
    me = rank.astype(jnp.int32).reshape(1)
    edge = tok_rows // 4

    first_out = project(0, ranks, ((0, 1, 2),), me, picture, ln_gain, w_qkv)
    first_in = exchanged(first_out)
    second_out = project(
        1, ranks, ((0,), (0,), (1, 2)), me, after(picture, first_out[0]), ln_gain, w_qkv
    )
    edge_out, mid_out, kv_out = (second_out[at * ranks : (at + 1) * ranks] for at in range(3))

    targets, spots, pe_late = after((req_image[:, 0], points, pe_matrix), first_out[0])
    slots = targets.shape[0]
    asked = jnp.concatenate([targets[:, None], spots], axis=1)
    everyone = gathered(asked[None], "img")
    here = (everyone[:, :, 0] == lax.axis_index("img")).astype(jnp.int32)
    turn = jnp.cumsum(here, axis=1) - here
    filling = here[:, :, None] * (turn[:, :, None] == jnp.arange(CAP)[None, None, :])
    arrived = jnp.sum(filling[:, :, :, None] * everyone[:, :, None, 1:], axis=1)
    matches = (targets[:, None] == jnp.arange(owners, dtype=jnp.int32)[None, :]).astype(jnp.int32)
    order_no = jnp.sum((jnp.cumsum(matches, axis=0) - matches) * matches, axis=1)
    places = targets * CAP + order_no
    placing = places[:, None] == jnp.arange(owners * CAP, dtype=jnp.int32)[None, :]
    number = owners * CAP
    flattened = arrived.reshape(number, 2).astype(jnp.float32)
    query_tok = query_bias + fourier((flattened + 0.5) / IMG_SIDE * 2.0 - 1.0, pe_late)
    query_matrix = jnp.dot(query_tok, dec_qkv[0], precision=highest_precision)
    head_size = ATTN_DIM // DEC_HEADS
    head_mask = (
        jnp.arange(DEC_HEADS)[:, None] == jnp.arange(ATTN_DIM)[None, :] // head_size
    ).astype(jnp.float32)
    spread_queries = (head_mask[:, None, :] * query_matrix[None, :, :]).reshape(
        DEC_HEADS * number, ATTN_DIM
    )
    offset_eye = jnp.eye(OFFSETS, dtype=jnp.bfloat16)
    choose = (
        offset_eye[:, None, None, :, None]
        * placing.astype(jnp.bfloat16).reshape(1, slots, owners, 1, CAP)
    ).reshape(OFFSETS * slots, owners * OFFSETS * CAP)
    order = pixel_order()

    kv_in = exchanged(after(kv_out, first_in[1:]))
    sines, decoder = after(
        (
            grid_sines(rank * grid_rows, grid_rows, pe_late),
            (dec_qkv, dec_out, w_mlp1, w_mlp2, w_hyper, w_hyper_out, w_up1, w_up2),
        ),
        first_out[0],
    )
    prepared = prepare(sines, *decoder)
    up_column = after(up_gain, first_out[0]).reshape(-1, 1)
    first_in, prepared, spread_queries, query_tok, up_column = lax.optimization_barrier(
        (first_in, prepared, spread_queries, query_tok, up_column)
    )
    token_weights, up_weights, key_value, code_keys = prepared
    first_mixed = attention(first_in, first_in, tok_rows)
    edge_in = exchanged(after(edge_out, first_mixed))
    own_edge, own_mid = attention(
        after([edge_out[0], mid_out[0]], first_mixed), kv_in, 2 * edge
    )
    quarter = after([mixed[:, :edge] for mixed in first_mixed], kv_in[1:])
    mid_out = [mid_out[0]] + [
        jnp.concatenate([mid_out[shift], quarter[ranks - shift]], axis=1)
        for shift in range(1, ranks)
    ]
    mid_in = exchanged(after(mid_out, (edge_in[1:], own_edge)))
    edge_mixed = attention(
        after(edge_in[1:], own_edge),
        kv_in,
        2 * edge,
        beside=first_mixed[1:],
        spans=((tok_rows - edge, tok_rows),),
    )
    edge_heads = exchanged(after([own_edge] + edge_mixed, mid_in[1:]), back=True)[1:]
    mid_mixed = attention(
        after(mid_in[1:], edge_mixed),
        kv_in,
        2 * edge,
        beside=first_mixed[1:],
        spans=((edge, tok_rows - edge),),
    )
    mid_heads = exchanged([own_mid] + mid_mixed, back=True)[1:]
    neck_args = (edge, ranks, me, picture, w_proj, w_neck1, neck_gain1)
    edge_narrow = neck(
        0,
        3,
        *neck_args,
        [(first_mixed[0], 0, 3)]
        + [(early, 2, late, 0) for early, late in zip(mid_in[:0:-1], edge_heads)]
        + [(own_edge, 0, 1)]
        + [(part, 1, 2) for part in edge_heads],
    )
    ends = ranks - 1
    prev = lax.ppermute(edge_narrow[-GRID:], "tok", [(i, i + 1) for i in range(ends)])
    following = lax.ppermute(edge_narrow[:GRID], "tok", [(i + 1, i) for i in range(ends)])
    mid_narrow = neck(
        1,
        1,
        *neck_args,
        [(first_mixed[0], 1, 2)]
        + [(part, 0, 1) for part in mid_heads]
        + [(own_mid, 0, 1)]
        + [(part, 2, 3) for part in mid_heads],
    )

    embedding, stats = embed(
        prev,
        following,
        edge_narrow,
        mid_narrow,
        w_neck2,
        neck_gain2,
        key_value,
        code_keys,
        spread_queries,
    )
    all_stats = exchanged([stats] * ranks)
    upscaled = upscale(embedding, up_weights, up_column)
    outgoing = mask_logits(
        all_stats,
        query_tok,
        owners,
        dec_gains,
        token_weights,
        upscaled,
    )
    answer = lax.all_to_all(outgoing, "img", split_axis=0, concat_axis=0, tiled=True)
    return place_rows(answer.reshape(number * OFFSETS, tok_rows), choose, order, slots)


def solution(mesh):
    placed = (
        (P("img", "tok", None),) + (P(),) * 19 + (P("img", None),) * 2
    )
    return jax.shard_map(
        body, mesh=mesh, in_specs=placed, out_specs=P("img", "tok"), check_vma=False
    )
```
